256 devices in a mesh: space: 16 (over z, x_lo), tracer: 16 (over x_hi, y, core).
Axes of the slice: x: 4 (x_hi: 2, x_lo: 2; x = x_hi * 2 + x_lo), y: 4, z: 8, core: 2. Of those that a mesh axis runs over, the one named last changes fastest.
Arguments:
- tracer_mass: float32 [288, 3, 32, 2048], P('tracer', None, None, 'space'), may hold values from -6 to 6
- thickness: float32 [16, 3, 32, 2048], P('tracer', None, None, 'space'), may hold values from 0.6 to 1.8
- flux_east: float32 [16, 3, 32, 2048], P('tracer', None, None, 'space'), may hold values from -0.08 to 0.08
- flux_north: float32 [16, 3, 32, 2048], P('tracer', None, None, 'space'), may hold values from -0.08 to 0.08
- courant_east: float32 [16, 3, 32, 2048], P('tracer', None, None, 'space'), may hold values from -0.95 to 0.95
- courant_north: float32 [16, 3, 32, 2048], P('tracer', None, None, 'space'), may hold values from -0.9 to 0.9
- whole_east: int32 [16, 3, 32, 2048], P('tracer', None, None, 'space'), may hold values from 0 to 2
- dynamics_owner: int32 [16], P('space'), may hold values from 0 to 15
Outputs:
- mixing_ratio: float32 [288, 3, 32, 2048], P('tracer', None, None, 'space')
The draws below stay inside these ranges and needn't reach their ends.
Inputs may be any that keep to these rules, and one draw needn't show every extreme that they name: `whole_east`: whole cells counts, 0 to 2.
All inputs are finite; a program needn't handle non-finite values.
Results may differ from the reference program's by a relative error of at most 0.0003.
Values sent between devices are 32-bit elements; how exact they have to be, the bound alone decides.
No kernel may reach another device: no remote copies, remote signals or barrier semaphores. Data moves between devices by JAX's collectives and lax.ppermute only.
A program may use at most 64 MiB of HBM per device.

```python
import jax
import jax.numpy as jnp
from jax import lax

TRACERS = 288
L = 3
NY = 32
CX = 128
NS = 2
NX = 2048
N_SPACE = 16
N_TRACER = 16


def plant(array, key, least, high):
    place = [jax.random.randint(jax.random.fold_in(key, axis), (), 0, length) for axis, length in enumerate(array.shape)]
    longest = array.shape.index(max(array.shape))
    next_to = place[:longest] + [(place[longest] + 1) % array.shape[longest]] + place[longest + 1:]
    return array.at[tuple(place)].set(least).at[tuple(next_to)].set(high)


def shard_levels(rng, extent, shards, least, top_value):
    loudness = 1.0
    for dim, blocks in shards:
        draws = jax.random.uniform(jax.random.fold_in(jax.random.fold_in(rng, 6), dim), (blocks,), jnp.float32, least / len(shards), top_value / len(shards))
        loudness = loudness * jnp.repeat(jnp.exp(draws), extent[dim] // blocks).reshape((-1,) + (1,) * (len(extent) - 1 - dim))
    return loudness


def gaussian(own_key, dims, deviation, most, cuts=(), held_as=jnp.bfloat16):
    entries = deviation * jax.random.normal(own_key, dims, jnp.float32)
    if cuts:
        entries = entries * shard_levels(own_key, dims, cuts, -0.22, 0.18)
    return jnp.clip(entries, -most, most).astype(held_as)


def setup_inputs(seed: int = 0) -> dict:
    seeds = jax.random.split(jax.random.key(seed), 9)
    tracer_mass = gaussian(seeds[0], (TRACERS, L, NY, NX), 1.0, 6.0, ((0, 16), (3, 16)), jnp.float32)
    thickness = jnp.clip(0.6 + 1.1999999 * jax.random.uniform(seeds[1], (N_TRACER, L, NY, NX), jnp.float32) ** shard_levels(seeds[1], (N_TRACER, L, NY, NX), ((0, 16), (3, 16)), -0.2, 0.2), 0.6, 1.8)
    flux_east = jnp.clip(jax.random.uniform(seeds[2], (N_TRACER, L, NY, NX), jnp.float32, -0.08, 0.08) * shard_levels(seeds[2], (N_TRACER, L, NY, NX), ((0, 16), (3, 16)), -0.4, 0.0), -0.08, 0.08)
    flux_north = jnp.clip(jax.random.uniform(seeds[3], (N_TRACER, L, NY, NX), jnp.float32, -0.08, 0.08) * shard_levels(seeds[3], (N_TRACER, L, NY, NX), ((0, 16), (3, 16)), -0.4, 0.0), -0.08, 0.08)
    courant_east = jnp.clip(jax.random.uniform(seeds[4], (N_TRACER, L, NY, NX), jnp.float32, -0.95, 0.95) * shard_levels(seeds[4], (N_TRACER, L, NY, NX), ((0, 16), (3, 16)), -0.4, 0.0), -0.95, 0.95)
    courant_north = jnp.clip(jax.random.uniform(seeds[5], (N_TRACER, L, NY, NX), jnp.float32, -0.9, 0.9) * shard_levels(seeds[5], (N_TRACER, L, NY, NX), ((0, 16), (3, 16)), -0.4, 0.0), -0.9, 0.9)
    whole_east = plant(jax.random.randint(seeds[6], (N_TRACER, L, NY, NX), 0, NS + 1), jax.random.fold_in(seeds[6], 1), 0, NS).astype(jnp.int32)
    dynamics_owner = plant(jax.random.randint(seeds[7], (N_SPACE,), 0, N_TRACER), jax.random.fold_in(seeds[7], 1), 0, N_TRACER - 1).astype(jnp.int32)
    return {"tracer_mass": tracer_mass, "thickness": thickness, "flux_east": flux_east, "flux_north": flux_north, "courant_east": courant_east, "courant_north": courant_north, "whole_east": whole_east, "dynamics_owner": dynamics_owner}


def take_slice(values_in, start_at, stop_at, along):
    return lax.slice_in_dim(values_in, start_at, stop_at, axis=along)


def parabola_parts(extended, along):
    length = extended.shape[along]
    edge_values = (7.0 * (take_slice(extended, 1, length - 2, along) + take_slice(extended, 2, length - 1, along)) - (take_slice(extended, 0, length - 3, along) + take_slice(extended, 3, length, along))) / 12.0
    left_edge = take_slice(edge_values, 0, length - 4, along)
    right_edge = take_slice(edge_values, 1, length - 3, along)
    cell_mean = take_slice(extended, 2, length - 2, along)
    curvature = 6.0 * cell_mean - 3.0 * (left_edge + right_edge)
    return left_edge, right_edge, right_edge - left_edge, curvature


def face_flux(extended, parabola, courant, whole_cells, most_cells, margin, face_count, along):
    left_edge, right_edge, edge_slope, curvature = parabola
    fraction = jnp.abs(courant)
    forward = courant >= 0.0
    shape_term = 1.0 - (2.0 / 3.0) * fraction
    whole_forward = 0.0
    whole_backward = 0.0
    flux_total = None
    for shift_count in range(most_cells + 1):
        if shift_count > 0:
            whole_forward = whole_forward + take_slice(extended, margin - shift_count, margin - shift_count + face_count, along)
            whole_backward = whole_backward + take_slice(extended, margin + shift_count - 1, margin + shift_count - 1 + face_count, along)
        upwind_left = margin - shift_count - 3
        upwind_right = margin + shift_count - 2
        from_left = take_slice(right_edge, upwind_left, upwind_left + face_count, along) - 0.5 * fraction * (take_slice(edge_slope, upwind_left, upwind_left + face_count, along) - shape_term * take_slice(curvature, upwind_left, upwind_left + face_count, along))
        from_right = take_slice(left_edge, upwind_right, upwind_right + face_count, along) + 0.5 * fraction * (take_slice(edge_slope, upwind_right, upwind_right + face_count, along) + shape_term * take_slice(curvature, upwind_right, upwind_right + face_count, along))
        candidate = jnp.where(forward, whole_forward + fraction * from_left, -(whole_backward + fraction * from_right))
        if shift_count == 0:
            flux_total = candidate
        else:
            flux_total = jnp.where(whole_cells == shift_count, candidate, flux_total)
    return flux_total


def row_flux(quantity, courant):
    row_count = quantity.shape[2]
    padded = jnp.pad(quantity, ((0, 0), (0, 0), (2, 2), (0, 0)))
    parabola = parabola_parts(padded, 2)
    inner_faces = face_flux(padded, parabola, take_slice(courant, 1, row_count, 1), None, 0, 3, row_count - 1, 2)
    zero_row = jnp.zeros_like(take_slice(inner_faces, 0, 1, 2))
    return jnp.concatenate([zero_row, inner_faces, zero_row], axis=2)


def row_update(quantity, face_fluxes, factor):
    row_count = quantity.shape[2]
    return quantity + factor * (take_slice(face_fluxes, 0, row_count, 2) - take_slice(face_fluxes, 1, row_count + 1, 2))


def column_flux(extended, courant_faces, whole_faces):
    parabola = parabola_parts(extended, 3)
    return face_flux(extended, parabola, courant_faces, whole_faces, NS, NS + 3, courant_faces.shape[3], 3)


def column_update(quantity, face_fluxes, factor):
    column_count = quantity.shape[3]
    return quantity + factor * (take_slice(face_fluxes, 0, column_count, 3) - take_slice(face_fluxes, 1, column_count + 1, 3))


def pick_owned(field_all, dynamics_owner):
    columns = field_all.shape[3]
    column_block = jnp.arange(columns, dtype=jnp.int32) // CX
    chosen = dynamics_owner[column_block]
    selected = jnp.arange(N_TRACER, dtype=jnp.int32)[:, None] == chosen[None, :]
    summed = jnp.sum(jnp.where(selected[:, None, None, :], field_all, jnp.zeros_like(field_all)), axis=0)
    return summed.astype(field_all.dtype)


def widen_east(quantity, margin):
    total_columns = quantity.shape[3]
    return jnp.concatenate([take_slice(quantity, total_columns - margin, total_columns, 3), quantity, take_slice(quantity, 0, margin, 3)], axis=3)


def reference(tracer_mass, thickness, flux_east, flux_north, courant_east, courant_north, whole_east, dynamics_owner):
    margin = NS + 3
    thick_here = pick_owned(thickness, dynamics_owner)
    east_mass = pick_owned(flux_east, dynamics_owner)
    north_mass = pick_owned(flux_north, dynamics_owner)
    east_frac = pick_owned(courant_east, dynamics_owner)
    north_frac = pick_owned(courant_north, dynamics_owner)
    whole_here = pick_owned(whole_east, dynamics_owner)
    east_faces = jnp.concatenate([east_frac, east_frac[:, :, :1]], axis=2)
    whole_faces = jnp.concatenate([whole_here, whole_here[:, :, :1]], axis=2)
    mass_faces = jnp.concatenate([east_mass, east_mass[:, :, :1]], axis=2)
    inner_north = row_update(tracer_mass, row_flux(tracer_mass, north_frac), 0.5)
    east_first = column_flux(widen_east(tracer_mass, margin), east_faces[None], whole_faces[None])
    inner_east = column_update(tracer_mass, east_first, 0.5)
    east_final = column_flux(widen_east(inner_north, margin), east_faces[None], whole_faces[None])
    north_final = row_flux(inner_east, north_frac)
    new_mass = row_update(column_update(tracer_mass, east_final, 1.0), north_final, 1.0)
    row_count = north_mass.shape[1]
    zero_row = jnp.zeros_like(north_mass[:, :1, :])
    north_faces = jnp.concatenate([zero_row, north_mass[:, 1:row_count, :], zero_row], axis=1)
    new_thickness = thick_here + (mass_faces[:, :, :-1] - mass_faces[:, :, 1:]) + (north_faces[:, :-1, :] - north_faces[:, 1:, :])
    return new_mass / new_thickness[None]
```

```python
import functools

import jax
import jax.numpy as jnp
from jax import lax
from jax.experimental import pallas as pl
from jax.experimental.pallas import tpu as pltpu
from jax.sharding import PartitionSpec as P

NS = 2
EDGE = NS + 3
SEG = 2 * EDGE
PACK = 9
GROUP = 3
MET_SEG = 16


def lane_index(shape):
    return lax.broadcasted_iota(jnp.int32, shape, len(shape) - 1)


def row_index(shape):
    return lax.broadcasted_iota(jnp.int32, shape, len(shape) - 2)


def lanes(x, shift):
    return pltpu.roll(x, shift % x.shape[-1], x.ndim - 1)


def rows(x, shift):
    return pltpu.roll(x, shift % x.shape[-2], x.ndim - 2)


def face_weights(courant):
    fraction = jnp.abs(courant)
    ramp = 1.5 * fraction * (1.0 - 2.0 / 3.0 * fraction)
    near = 0.5 * courant * (1.0 - 0.5 * fraction - ramp)
    far = 0.5 * courant * (0.5 * fraction - ramp)
    mean = courant * ramp
    far_outer = far * (1.0 / 12.0)
    near_outer = near * (1.0 / 12.0)
    return (
        -near_outer,
        7.0 * near_outer - far_outer,
        7.0 * (near_outer + far_outer) + mean,
        7.0 * far_outer - near_outer,
        -far_outer,
    )


def north_taps(courant):
    down1, up0, up1, up2, up3 = (w for w in face_weights(courant))
    forward = courant >= 0.0
    zero = jnp.zeros_like(courant)
    f = {1: down1, 0: up0, -1: up1, -2: up2, -3: up3}
    b = {-2: down1, -1: up0, 0: up1, 1: up2, 2: up3}
    return {m: jnp.where(forward, f.get(m, zero), b.get(m, zero)) for m in range(-3, 3)}


def east_taps(courant, whole):
    weights = face_weights(courant)
    forward = courant >= 0.0
    zero = jnp.zeros_like(courant)
    one = whole == 1.0
    two = whole == 2.0
    some = whole > 0.5
    taps = {}
    for m in range(-EDGE, EDGE):
        ahead = []
        behind = []
        for n in range(NS + 1):
            place = 1 - n - m
            ahead.append(weights[place] if 0 <= place < 5 else zero)
            place = m + 2 - n
            behind.append(weights[place] if 0 <= place < 5 else zero)
        f = jnp.where(two, ahead[2], jnp.where(one, ahead[1], ahead[0]))
        b = jnp.where(two, behind[2], jnp.where(one, behind[1], behind[0]))
        if m == -1:
            f = f + jnp.where(some, 0.5, 0.0)
        if m == -2:
            f = f + jnp.where(two, 0.5, 0.0)
        if m == 0:
            b = b - jnp.where(some, 0.5, 0.0)
        if m == 1:
            b = b - jnp.where(two, 0.5, 0.0)
        taps[m] = jnp.where(forward, f, b)
    return taps


def difference_taps(here, ahead, reach):
    out = {}
    for m in range(-reach, reach + 1):
        if m in here and m - 1 in ahead:
            out[m] = here[m] - ahead[m - 1]
        elif m in here:
            out[m] = here[m]
        else:
            out[m] = -ahead[m - 1]
    return out


def north_coefficients(courant):
    count = courant.shape[0]
    row = row_index(courant.shape)
    here = jnp.where(row == 0, 0.0, courant)
    ahead = rows(here, -1)
    taps = difference_taps(north_taps(here), north_taps(ahead), 3)
    return [
        jnp.where((row + m >= 0) & (row + m < count), taps[m], 0.0) for m in range(-3, 4)
    ]


def repeated(x):
    one = jnp.where(lane_index(x.shape) < SEG, x, 0.0)
    two = one + lanes(one, SEG)
    four = two + lanes(two, 2 * SEG)
    eight = four + lanes(four, 4 * SEG)
    return eight + lanes(one, 8 * SEG)


def prepare_kernel(ids, thick, fe, fn, ce, cn, ne, mass, parts, cells):
    owned = ids[0] == ids[1]
    core = ids[1] % 2
    levels, count, width = thick.shape[1:]
    lane = lane_index((count, width))
    row = row_index((count, width))
    edge_rows = jnp.zeros((count, width), jnp.float32)
    for l in range(levels):
        east_mass = fe[0, l]
        north_mass = jnp.where(row == 0, 0.0, fn[0, l])
        thickness = (
            thick[0, l]
            + (east_mass - jnp.where(lane == width - 1, 0.0, lanes(east_mass, -1)))
            + (north_mass - rows(north_mass, -1))
        )
        whole = ne[0, l].astype(jnp.float32)
        first = (thickness, ce[0, l])
        second = (cn[0, l], whole)
        for half, pair in enumerate((first, second)):
            for k, value in enumerate(pair):
                start = (k * levels + l) * count
                parts[(half + core) % 2, start : start + count, :] = jnp.where(owned, value, 0.0)
        edges = jnp.where(lane < SEG, lanes(cn[0, l], EDGE), 0.0)
        for k, value in enumerate((ce[0, l], whole, east_mass)):
            edges = jnp.where(lane == SEG + k, lanes(value, SEG + k), edges)
        edge_rows = edge_rows + lanes(jnp.where(lane < MET_SEG, edges, 0.0), MET_SEG * l)
    edge_rows = jnp.where(owned, edge_rows, 0.0)
    base = 2 * levels * count
    parts[0, base : base + count, :] = edge_rows
    parts[1, base : base + count, :] = edge_rows
    for half in range(2):
        for l in range(levels):
            packed = jnp.zeros((count, width), jnp.float32)
            for k in range(PACK):
                value = lanes(mass[half * PACK + k, l], EDGE + SEG * k)
                inside = (lane >= SEG * k) & (lane < SEG * (k + 1))
                packed = jnp.where(inside, value, packed)
            cells[half, l] = packed


def prepare(ids, thick, fe, fn, ce, cn, ne, mass):
    tracers, levels, count, width = mass.shape
    vmem = pl.BlockSpec(memory_space=pltpu.VMEM)
    return pl.pallas_call(
        prepare_kernel,
        out_shape=(
            jax.ShapeDtypeStruct((2, 2 * levels * count + count, width), jnp.float32),
            jax.ShapeDtypeStruct((2, levels, count, width), jnp.float32),
        ),
        in_specs=[pl.BlockSpec(memory_space=pltpu.SMEM)] + [vmem] * 7,
        out_specs=(vmem, vmem),
        name="prepare",
    )(ids, thick, fe, fn, ce, cn, ne, mass)


PAD = 8


def transport_kernel(
    ids, mine, other, met_west, met_east, cells_west, cells_east, mass, out,
    east_c, north_c, inverse, packed_first, packed_final, padded, middle,
):
    levels, count, width = mass.shape[1:]
    lane = lane_index((count, width))
    row = row_index((count, width))
    low = ids[1] % 2 == 0
    in_segment = lane % SEG
    packed_lane = lane < SEG * PACK
    zero_rows = jnp.zeros((PAD, width), jnp.float32)
    for buffer in (padded, middle):
        for g in range(2 * GROUP):
            if g < buffer.shape[0]:
                buffer[g, :PAD, :] = zero_rows
                buffer[g, PAD + count :, :] = zero_rows
    for l in range(levels):
        fields = []
        for half in range(2):
            for k in range(2):
                start = (k * levels + l) * count
                a = mine[start : start + count, :]
                b = other[start : start + count, :]
                fields.append(jnp.where(low, a, b) if half == 0 else jnp.where(low, b, a))
        thickness, east, north, whole = fields
        from_west = lanes(met_west[:, :], -MET_SEG * l)
        from_east = lanes(met_east[:, :], -MET_SEG * l)

        def next_face(value, k):
            return jnp.where(
                lane == width - 1, lanes(from_east, width - 1 - SEG - k), lanes(value, -1)
            )

        next_east = next_face(east, 0)
        next_whole = next_face(whole, 1)
        edge_mass = jnp.where(lane == width - 1, lanes(from_east, width - 1 - SEG - 2), 0.0)
        inverse[l] = 2.0 / (thickness - edge_mass)
        taps = difference_taps(east_taps(east, whole), east_taps(next_east, next_whole), EDGE)
        for m in range(-EDGE, EDGE + 1):
            value = taps[m]
            if m < 0:
                value = jnp.where(lane >= -m, value, 0.0)
            if m > 0:
                value = jnp.where(lane < width - m, value, 0.0)
            east_c[m + EDGE, l] = value
        for m, value in enumerate(north_coefficients(north)):
            north_c[m, l] = value

        packed_north = repeated(jnp.where(lane < EDGE, from_west, from_east))
        packed_east = [
            repeated(lanes(v, EDGE)) for v in (east, whole, next_east, next_whole)
        ]
        taps = difference_taps(
            east_taps(packed_east[0], packed_east[1]),
            east_taps(packed_east[2], packed_east[3]),
            EDGE,
        )
        outer = {}
        for m in range(-EDGE, EDGE + 1):
            if m != 0:
                crosses = ((in_segment < EDGE) != (in_segment + m < EDGE)) & packed_lane
                outer[m] = jnp.where(crosses, taps[m], 0.0)
        packed_taps = north_coefficients(packed_north)
        for half in range(2):
            cells = jnp.where(in_segment < EDGE, cells_west[half, l], cells_east[half, l])
            inner = cells
            for m in range(-3, 4):
                inner = inner + packed_taps[m + 3] * rows(cells, -m)
            first = jnp.zeros_like(cells)
            final = jnp.zeros_like(cells)
            for m in outer:
                first = first + outer[m] * lanes(cells, -m)
                final = final + outer[m] * lanes(inner, -m)
            packed_first[half, l] = first
            packed_final[half, l] = final

    at_edge = (lane < EDGE) | (lane >= width - EDGE)

    def group(step, carry):
        l = step % levels
        tg = step // levels
        t0 = tg * GROUP
        half = t0 // PACK
        zero = jnp.zeros((GROUP, count, width), jnp.float32)
        value = mass[pl.ds(t0, GROUP), pl.ds(l, 1)].reshape(GROUP, count, width)
        for j in range(GROUP):
            padded[j, PAD : PAD + count, :] = value[j]

        def edges(ref):
            parts = []
            for j in range(GROUP):
                k = t0 + j - half * PACK
                moved = pltpu.roll(ref[half, l], width - EDGE - SEG * k, 1)
                parts.append(jnp.where(at_edge, moved, 0.0))
            return jnp.stack(parts)

        def east_sum(start, x):
            flat = x.reshape(GROUP * count, width)
            total = start
            for m in range(-EDGE, EDGE + 1):
                moved = x if m == 0 else lanes(flat, -m).reshape(GROUP, count, width)
                total = total + east_c[m + EDGE, l][None] * moved
            return total

        def north_sum(start, ref):
            total = start
            for m in range(-3, 4):
                total = total + north_c[m + 3, l][None] * ref[:, PAD + m : PAD + m + count, :]
            return total

        inner_east = east_sum(value + edges(packed_first), value)
        middle[:, PAD : PAD + count, :] = inner_east
        inner_north = north_sum(value, padded)
        total = east_sum(0.5 * value + edges(packed_final), inner_north)
        total = north_sum(total, middle)
        result = total * inverse[l][None]
        out[pl.ds(t0, GROUP), pl.ds(l, 1)] = result.reshape(GROUP, 1, count, width)
        return carry

    lax.fori_loop(0, levels * (mass.shape[0] // GROUP), group, 0)


def transport(ids, mine, other, met_west, met_east, cells_west, cells_east, mass):
    tracers, levels, count, width = mass.shape
    vmem = pl.BlockSpec(memory_space=pltpu.VMEM)
    return pl.pallas_call(
        transport_kernel,
        out_shape=jax.ShapeDtypeStruct(mass.shape, jnp.float32),
        in_specs=[pl.BlockSpec(memory_space=pltpu.SMEM)] + [vmem] * 7,
        out_specs=vmem,
        scratch_shapes=[
            pltpu.VMEM((2 * EDGE + 1, levels, count, width), jnp.float32),
            pltpu.VMEM((7, levels, count, width), jnp.float32),
            pltpu.VMEM((levels, count, width), jnp.float32),
            pltpu.VMEM((2, levels, count, width), jnp.float32),
            pltpu.VMEM((2, levels, count, width), jnp.float32),
            pltpu.VMEM((GROUP, count + 2 * PAD, width), jnp.float32),
            pltpu.VMEM((GROUP, count + 2 * PAD, width), jnp.float32),
        ],
        compiler_params=pltpu.CompilerParams(vmem_limit_bytes=32 * 1024 * 1024),
        name="transport",
    )(ids, mine, other, met_west, met_east, cells_west, cells_east, mass)


def ring(x, by):
    size = lax.axis_size("space")
    return lax.ppermute(x, "space", [(i, (i + by) % size) for i in range(size)])


def exchange(x, flip):
    size = lax.axis_size("tracer")
    return lax.ppermute(x, "tracer", [(i, i ^ flip) for i in range(size)])


def shards(thickness_args, mass, dynamics_owner):
    thick, fe, fn, ce, cn, ne = thickness_args
    me = lax.axis_index("tracer")
    ids = jnp.stack([dynamics_owner[0], me]).astype(jnp.int32)
    parts, cells = prepare(ids, thick, fe, fn, ce, cn, ne, mass)
    main = 2 * mass.shape[1] * mass.shape[2]
    total = parts[0] + exchange(parts[1], 1)
    for flip in (2, 6, 8):
        total = total + exchange(total, flip)
    cells_west = ring(cells, 1)
    cells_east = ring(cells, -1)
    mine = total[:main]
    edges = total[main:]
    met_west = ring(edges, 1)
    met_east = ring(edges, -1)
    other = exchange(mine, 1)
    return transport(ids, mine, other, met_west, met_east, cells_west, cells_east, mass)


def solution(mesh):
    spec = P("tracer", None, None, "space")

    def run(mass, thick, fe, fn, ce, cn, ne, owner):
        return shards((thick, fe, fn, ce, cn, ne), mass, owner)

    return jax.shard_map(
        run, mesh=mesh, in_specs=(spec,) * 7 + (P("space"),), out_specs=spec, check_vma=False
    )
```

```python
import jax
import jax.numpy as jnp
from jax import lax
from jax.experimental import pallas as pl
from jax.experimental.pallas import tpu as pltpu
from jax.sharding import PartitionSpec as P

NS = 2
EDGE = NS + 3
SEG = 2 * EDGE
PACK = 9
STEP = 4
GROUP = 3
PAD = 8
BLOCK = 8
MET_SEG = 16


def lane_index(shape):
    return lax.broadcasted_iota(jnp.int32, shape, len(shape) - 1)


def row_index(shape):
    return lax.broadcasted_iota(jnp.int32, shape, len(shape) - 2)


def lanes(x, shift):
    return pltpu.roll(x, shift % x.shape[-1], x.ndim - 1)


def rows(x, shift):
    return pltpu.roll(x, shift % x.shape[-2], x.ndim - 2)


def face_weights(courant):
    fraction = jnp.abs(courant)
    ramp = 1.5 * fraction * (1.0 - 2.0 / 3.0 * fraction)
    near = 0.5 * courant * (1.0 - 0.5 * fraction - ramp)
    far = 0.5 * courant * (0.5 * fraction - ramp)
    mean = courant * ramp
    far_outer = far * (1.0 / 12.0)
    near_outer = near * (1.0 / 12.0)
    return (
        -near_outer,
        7.0 * near_outer - far_outer,
        7.0 * (near_outer + far_outer) + mean,
        7.0 * far_outer - near_outer,
        -far_outer,
    )


def north_taps(courant):
    down1, up0, up1, up2, up3 = (w for w in face_weights(courant))
    forward = courant >= 0.0
    zero = jnp.zeros_like(courant)
    f = {1: down1, 0: up0, -1: up1, -2: up2, -3: up3}
    b = {-2: down1, -1: up0, 0: up1, 1: up2, 2: up3}
    return {m: jnp.where(forward, f.get(m, zero), b.get(m, zero)) for m in range(-3, 3)}


def east_taps(courant, whole):
    weights = face_weights(courant)
    forward = courant >= 0.0
    zero = jnp.zeros_like(courant)
    one = whole == 1.0
    two = whole == 2.0
    some = whole > 0.5
    taps = {}
    for m in range(-EDGE, EDGE):
        ahead = []
        behind = []
        for n in range(NS + 1):
            place = 1 - n - m
            ahead.append(weights[place] if 0 <= place < 5 else zero)
            place = m + 2 - n
            behind.append(weights[place] if 0 <= place < 5 else zero)
        f = jnp.where(two, ahead[2], jnp.where(one, ahead[1], ahead[0]))
        b = jnp.where(two, behind[2], jnp.where(one, behind[1], behind[0]))
        if m == -1:
            f = f + jnp.where(some, 0.5, 0.0)
        if m == -2:
            f = f + jnp.where(two, 0.5, 0.0)
        if m == 0:
            b = b - jnp.where(some, 0.5, 0.0)
        if m == 1:
            b = b - jnp.where(two, 0.5, 0.0)
        taps[m] = jnp.where(forward, f, b)
    return taps


def difference_taps(here, ahead, reach):
    out = {}
    for m in range(-reach, reach + 1):
        if m in here and m - 1 in ahead:
            out[m] = here[m] - ahead[m - 1]
        elif m in here:
            out[m] = here[m]
        else:
            out[m] = -ahead[m - 1]
    return out


def north_coefficients(courant):
    count = courant.shape[0]
    row = row_index(courant.shape)
    here = north_taps(jnp.where(row == 0, 0.0, courant))
    taps = difference_taps(here, {m: rows(here[m], -1) for m in here}, 3)
    return [
        jnp.where((row + m >= 0) & (row + m < count), taps[m], 0.0) for m in range(-3, 4)
    ]


def pick(x, index):
    return jnp.take_along_axis(x, index, axis=1, mode="promise_in_bounds")


def position():
    return lax.axis_index("tracer")


def prepare_kernel(owner, thick, fe, fn, ce, cn, ne, keep, send):
    me = position()
    owned = owner[0] == me
    core = me % 2
    levels, count, width = thick.shape[1:]
    lane = lane_index((count, width))
    row = row_index((count, width))
    edge_rows = jnp.zeros((count, width), jnp.float32)
    for l in range(levels):
        east_mass = fe[0, l]
        north_mass = jnp.where(row == 0, 0.0, fn[0, l])
        thickness = (
            thick[0, l]
            + (east_mass - jnp.where(lane == width - 1, 0.0, lanes(east_mass, -1)))
            + (north_mass - rows(north_mass, -1))
        )
        whole = ne[0, l].astype(jnp.float32)
        first = (thickness, ce[0, l])
        second = (cn[0, l], whole)
        for k in range(2):
            start = (k * levels + l) * count
            a = jnp.where(owned, first[k], 0.0)
            b = jnp.where(owned, second[k], 0.0)
            keep[start : start + count, :] = jnp.where(core == 0, a, b)
            send[start : start + count, :] = jnp.where(core == 0, b, a)
        edges = jnp.where(lane < SEG, lanes(cn[0, l], EDGE), 0.0)
        for k, value in enumerate((ce[0, l], whole, east_mass)):
            edges = jnp.where(lane == SEG + k, lanes(value, SEG + k), edges)
        edge_rows = edge_rows + lanes(jnp.where(lane < MET_SEG, edges, 0.0), MET_SEG * l)
    edge_rows = jnp.where(owned, edge_rows, 0.0)
    base = 2 * levels * count
    keep[base : base + count, :] = edge_rows
    send[base : base + count, :] = edge_rows


def prepare(owner, thick, fe, fn, ce, cn, ne):
    levels, count, width = thick.shape[1:]
    vmem = pl.BlockSpec(memory_space=pltpu.VMEM)
    half = pltpu.VMEM(((2 * levels + 1) * count, width), jnp.float32)
    return pl.pallas_call(
        prepare_kernel,
        out_shape=(half, half),
        in_specs=[pl.BlockSpec(memory_space=pltpu.SMEM)] + [vmem] * 6,
        out_specs=(vmem, vmem),
        name="prepare",
    )(owner, thick, fe, fn, ce, cn, ne)


def pack_kernel(mass, last, first):
    tracers, levels, count, width = mass.shape
    lane = lane_index((count, width))
    for l in range(levels):
        a = jnp.zeros((count, width), jnp.float32)
        b = a
        for t in range(tracers):
            value = mass[t, l]
            inside = (lane >= EDGE * t) & (lane < EDGE * (t + 1))
            a = jnp.where(inside, lanes(value, EDGE * (t + 1)), a)
            b = jnp.where(inside, lanes(value, EDGE * t), b)
        last[l * count : (l + 1) * count, :] = a
        first[l * count : (l + 1) * count, :] = b


def pack(mass):
    tracers, levels, count, width = mass.shape
    vmem = pl.BlockSpec(memory_space=pltpu.VMEM)
    packed = pltpu.VMEM((levels * count, width), jnp.float32)
    return pl.pallas_call(
        pack_kernel,
        out_shape=(packed, packed),
        in_specs=[vmem],
        out_specs=(vmem, vmem),
        cost_estimate=pl.CostEstimate(flops=2000000, bytes_accessed=1000000, transcendentals=0),
        name="pack",
    )(mass)


def transport_kernel(
    owner, mine, other, west, east, mass, out,
    east_c, north_c, inverse, packed_first, packed_final, padded, middle, stage, sems,
):
    tracers, levels, count, width = mass.shape
    shape = (count, width)
    lane = lane_index(shape)
    low = position() % 2 == 0
    segment = sum(((lane >= SEG * k).astype(jnp.int32) for k in range(1, PACK)), jnp.zeros(shape, jnp.int32))
    in_segment = lane - SEG * segment
    packed_lane = lane < SEG * PACK
    from_west_lane = in_segment < EDGE
    zero_rows = jnp.zeros((PAD, width), jnp.float32)
    for buffer in (padded, middle):
        for g in range(GROUP):
            buffer[g, :PAD, :] = zero_rows
            buffer[g, PAD + count :, :] = zero_rows

    base = levels * count
    met_east = east[base : base + count, :]
    met_lane = sum((jnp.where(lane >= MET_SEG * l, MET_SEG, 0) for l in range(1, levels)), jnp.zeros(shape, jnp.int32))
    met = jnp.where(lane - met_lane < EDGE, west[base : base + count, :], met_east)
    beyond = east_taps(met_east, lanes(met_east, -1))
    edge_index = jnp.where(packed_lane, in_segment + (width - EDGE), 0)
    edge_index = jnp.where(edge_index >= width, edge_index - width, edge_index)

    for l in range(levels):
        fields = []
        for half in range(2):
            for k in range(2):
                start = (k * levels + l) * count
                a = mine[start : start + count, :]
                b = other[start : start + count, :]
                fields.append(jnp.where(low, a, b) if half == 0 else jnp.where(low, b, a))
        thickness, east_courant, north_courant, whole = fields
        last = width - 1 - MET_SEG * l - SEG
        edge_mass = jnp.where(lane == width - 1, lanes(met_east, last - 2), 0.0)
        inverse[l] = 2.0 / (thickness - edge_mass)
        here = east_taps(east_courant, whole)
        ahead = {
            m: jnp.where(lane == width - 1, lanes(beyond[m], last), lanes(here[m], -1)) for m in here
        }
        taps = difference_taps(here, ahead, EDGE)
        outer = {}
        for m in range(-EDGE, EDGE + 1):
            value = taps[m]
            if m != 0:
                crosses = (from_west_lane != (in_segment + m < EDGE)) & packed_lane
                outer[m] = jnp.where(crosses, pick(value, edge_index), 0.0)
            if m < 0:
                value = jnp.where(lane >= -m, value, 0.0)
            if m > 0:
                value = jnp.where(lane < width - m, value, 0.0)
            shift = east_group(m)
            east_c[m + EDGE, l] = lanes(value, shift) if shift else value
        for m, value in enumerate(north_coefficients(north_courant)):
            north_c[m, l] = value

        packed_taps = north_coefficients(pick(met, jnp.where(packed_lane, in_segment + MET_SEG * l, 0)))
        for half in range(2):
            west_index = jnp.where(
                packed_lane, in_segment + EDGE * (segment + PACK * half), 0
            )
            east_index = west_index - EDGE
            cells = jnp.where(
                from_west_lane,
                pick(west[l * count : (l + 1) * count, :], jnp.where(from_west_lane, west_index, 0)),
                pick(east[l * count : (l + 1) * count, :], jnp.where(from_west_lane, 0, jnp.maximum(east_index, 0))),
            )
            inner = cells
            for m in range(-3, 4):
                inner = inner + packed_taps[m + 3] * rows(cells, -m)
            first = jnp.zeros_like(cells)
            final = jnp.zeros_like(cells)
            for m in outer:
                first = first + outer[m] * lanes(cells, -m)
                final = final + outer[m] * lanes(inner, -m)
            packed_first[half, l] = first
            packed_final[half, l] = final

    block_lane = lane_index((BLOCK, width))
    at_edge = (block_lane < EDGE) | (block_lane >= width - EDGE)

    def east_sum(start, taps, x):
        near = {-1: lanes(x, 1), 0: x, 1: lanes(x, -1), 2: lanes(x, -2)}
        parts = {}
        for m in range(-EDGE, EDGE + 1):
            shift = east_group(m)
            term = taps[m + EDGE] * near[m - shift]
            parts[shift] = parts[shift] + term if shift in parts else term
        return start + parts[0] + (lanes(parts[-STEP], STEP) + lanes(parts[STEP], -STEP))

    def group(step, carry):
        l = step % levels
        t0 = (step // levels) * GROUP
        half = t0 // PACK
        first_place = t0 - half * PACK

        def block(b):
            return slice(b * BLOCK, (b + 1) * BLOCK)

        def edges(ref, j, b):
            moved = pltpu.roll(ref[half, l, block(b), :], width - EDGE - SEG * (j + first_place), 1)
            return jnp.where(at_edge, moved, 0.0)

        for b in range(count // BLOCK):
            taps = [east_c[m, l, block(b), :] for m in range(2 * EDGE + 1)]
            for j in range(GROUP):
                x = mass[t0 + j, l, block(b), :]
                place = slice(PAD + b * BLOCK, PAD + (b + 1) * BLOCK)
                padded[j, place, :] = x
                middle[j, place, :] = east_sum(x + edges(packed_first, j, b), taps, x)
        for b in range(count // BLOCK):
            taps = [east_c[m, l, block(b), :] for m in range(2 * EDGE + 1)]
            north = [north_c[m, l, block(b), :] for m in range(7)]
            scale = inverse[l, block(b), :]
            for j in range(GROUP):
                x = mass[t0 + j, l, block(b), :]
                inner = x
                total = 0.5 * x + edges(packed_final, j, b)
                for m in range(-3, 4):
                    start = PAD + b * BLOCK + m
                    inner = inner + north[m + 3] * padded[j, start : start + BLOCK, :]
                    total = total + north[m + 3] * middle[j, start : start + BLOCK, :]
                stage[t0 + j, l, block(b), :] = east_sum(total, taps, inner) * scale
        copy(step).start()
        return carry

    def copy(step):
        l = step % levels
        place = pl.ds((step // levels) * GROUP, GROUP)
        return pltpu.make_async_copy(stage.at[place, l], out.at[place, l], sems.at[step])

    steps = levels * (tracers // GROUP)
    lax.fori_loop(0, steps, group, 0)
    for step in range(steps):
        copy(step).wait()


def east_group(m):
    return -STEP if m < -1 else (STEP if m > 2 else 0)


def transport(owner, mine, other, west, east, mass):
    tracers, levels, count, width = mass.shape
    vmem = pl.BlockSpec(memory_space=pltpu.VMEM)
    return pl.pallas_call(
        transport_kernel,
        out_shape=jax.ShapeDtypeStruct(mass.shape, jnp.float32),
        in_specs=[pl.BlockSpec(memory_space=pltpu.SMEM)] + [vmem] * 5,
        out_specs=pl.BlockSpec(memory_space=pl.ANY),
        scratch_shapes=[
            pltpu.VMEM((2 * EDGE + 1, levels, count, width), jnp.float32),
            pltpu.VMEM((7, levels, count, width), jnp.float32),
            pltpu.VMEM((levels, count, width), jnp.float32),
            pltpu.VMEM((2, levels, count, width), jnp.float32),
            pltpu.VMEM((2, levels, count, width), jnp.float32),
            pltpu.VMEM((GROUP, count + 2 * PAD, width), jnp.float32),
            pltpu.VMEM((GROUP, count + 2 * PAD, width), jnp.float32),
            pltpu.VMEM(mass.shape, jnp.float32),
            pltpu.SemaphoreType.DMA((levels * (tracers // GROUP),)),
        ],
        compiler_params=pltpu.CompilerParams(vmem_limit_bytes=24 * 1024 * 1024),
        name="transport",
    )(owner, mine, other, west, east, mass)


def ring(x, by):
    size = lax.axis_size("space")
    return lax.ppermute(x, "space", [(i, (i + by) % size) for i in range(size)])


def exchange(x, flip):
    size = lax.axis_size("tracer")
    return lax.ppermute(x, "tracer", [(i, i ^ flip) for i in range(size)])


def shards(mass, thick, fe, fn, ce, cn, ne, owner):
    keep, send = prepare(owner, thick, fe, fn, ce, cn, ne)
    last, first = pack(mass)
    total = keep + exchange(send, 1)
    for flip in (2, 6, 8):
        total = total + exchange(total, flip)
    main = 2 * mass.shape[1] * mass.shape[2]
    mine = total[:main]
    edges = total[main:]
    other = exchange(mine, 1)
    west = ring(jnp.concatenate([last, edges]), 1)
    east = ring(jnp.concatenate([first, edges]), -1)
    return transport(owner, mine, other, west, east, mass)


def solution(mesh):
    spec = P("tracer", None, None, "space")
    return jax.shard_map(
        shards, mesh=mesh, in_specs=(spec,) * 7 + (P("space"),), out_specs=spec, check_vma=False
    )
```

```python
import jax
import jax.numpy as jnp
from jax import lax
from jax.experimental import pallas as pl
from jax.experimental.pallas import tpu as pltpu
from jax.sharding import PartitionSpec as P

NS = 2
EDGE = NS + 3
SEG = 2 * EDGE
PACK = 9
STEP = 4
GROUP = 3
PAD = 8
BLOCK = 8
NEAR = (-1, 1, 2)
MET_SEG = 16


def lane_index(shape):
    return lax.broadcasted_iota(jnp.int32, shape, len(shape) - 1)


def row_index(shape):
    return lax.broadcasted_iota(jnp.int32, shape, len(shape) - 2)


def lanes(x, shift):
    return pltpu.roll(x, shift % x.shape[-1], x.ndim - 1)


def rows(x, shift):
    return pltpu.roll(x, shift % x.shape[-2], x.ndim - 2)


def face_weights(courant):
    fraction = jnp.abs(courant)
    ramp = 1.5 * fraction * (1.0 - 2.0 / 3.0 * fraction)
    near = 0.5 * courant * (1.0 - 0.5 * fraction - ramp)
    far = 0.5 * courant * (0.5 * fraction - ramp)
    mean = courant * ramp
    far_outer = far * (1.0 / 12.0)
    near_outer = near * (1.0 / 12.0)
    return (
        -near_outer,
        7.0 * near_outer - far_outer,
        7.0 * (near_outer + far_outer) + mean,
        7.0 * far_outer - near_outer,
        -far_outer,
    )


def north_taps(courant):
    down1, up0, up1, up2, up3 = (w for w in face_weights(courant))
    forward = courant >= 0.0
    zero = jnp.zeros_like(courant)
    f = {1: down1, 0: up0, -1: up1, -2: up2, -3: up3}
    b = {-2: down1, -1: up0, 0: up1, 1: up2, 2: up3}
    return {m: jnp.where(forward, f.get(m, zero), b.get(m, zero)) for m in range(-3, 3)}


def east_taps(courant, whole):
    weights = face_weights(courant)
    forward = courant >= 0.0
    zero = jnp.zeros_like(courant)
    one = whole == 1.0
    two = whole == 2.0
    some = whole > 0.5
    taps = {}
    for m in range(-EDGE, EDGE):
        ahead = []
        behind = []
        for n in range(NS + 1):
            place = 1 - n - m
            ahead.append(weights[place] if 0 <= place < 5 else zero)
            place = m + 2 - n
            behind.append(weights[place] if 0 <= place < 5 else zero)
        f = jnp.where(two, ahead[2], jnp.where(one, ahead[1], ahead[0]))
        b = jnp.where(two, behind[2], jnp.where(one, behind[1], behind[0]))
        if m == -1:
            f = f + jnp.where(some, 0.5, 0.0)
        if m == -2:
            f = f + jnp.where(two, 0.5, 0.0)
        if m == 0:
            b = b - jnp.where(some, 0.5, 0.0)
        if m == 1:
            b = b - jnp.where(two, 0.5, 0.0)
        taps[m] = jnp.where(forward, f, b)
    return taps


def difference_taps(here, ahead, reach):
    out = {}
    for m in range(-reach, reach + 1):
        if m in here and m - 1 in ahead:
            out[m] = here[m] - ahead[m - 1]
        elif m in here:
            out[m] = here[m]
        else:
            out[m] = -ahead[m - 1]
    return out


def north_coefficients(courant):
    count = courant.shape[0]
    row = row_index(courant.shape)
    here = north_taps(jnp.where(row == 0, 0.0, courant))
    taps = difference_taps(here, {m: rows(here[m], -1) for m in here}, 3)
    return [
        jnp.where((row + m >= 0) & (row + m < count), taps[m], 0.0) for m in range(-3, 4)
    ]


def pick(x, index):
    return jnp.take_along_axis(x, index, axis=1, mode="promise_in_bounds")


def position():
    return lax.axis_index("tracer")


def prepare_kernel(*refs):
    sources, (keep, send, owner, *fields, sems) = refs[:7], refs[7:]
    copies = [
        pltpu.make_async_copy(source, place, sems.at[k])
        for k, (source, place) in enumerate(zip(sources, (owner, *fields)))
    ]
    for copy in copies:
        copy.start()
    for copy in copies:
        copy.wait()
    thick, fe, fn, ce, cn, ne = fields
    me = position()
    owned = owner[0] == me
    core = me % 2
    levels, count, width = thick.shape[1:]
    lane = lane_index((count, width))
    row = row_index((count, width))
    edge_rows = jnp.zeros((count, width), jnp.float32)
    for l in range(levels):
        east_mass = fe[0, l]
        north_mass = jnp.where(row == 0, 0.0, fn[0, l])
        thickness = (
            thick[0, l]
            + (east_mass - jnp.where(lane == width - 1, 0.0, lanes(east_mass, -1)))
            + (north_mass - rows(north_mass, -1))
        )
        whole = ne[0, l].astype(jnp.float32)
        first = (thickness, ce[0, l])
        second = (cn[0, l], whole)
        for k in range(2):
            start = (k * levels + l) * count
            a = jnp.where(owned, first[k], 0.0)
            b = jnp.where(owned, second[k], 0.0)
            keep[start : start + count, :] = jnp.where(core == 0, a, b)
            send[start : start + count, :] = jnp.where(core == 0, b, a)
        edges = jnp.where(lane < SEG, lanes(cn[0, l], EDGE), 0.0)
        for k, value in enumerate((ce[0, l], whole, east_mass)):
            edges = jnp.where(lane == SEG + k, lanes(value, SEG + k), edges)
        edge_rows = edge_rows + lanes(jnp.where(lane < MET_SEG, edges, 0.0), MET_SEG * l)
    edge_rows = jnp.where(owned, edge_rows, 0.0)
    base = 2 * levels * count
    keep[base : base + count, :] = edge_rows
    send[base : base + count, :] = edge_rows


def prepare(owner, thick, fe, fn, ce, cn, ne):
    levels, count, width = thick.shape[1:]
    vmem = pl.BlockSpec(memory_space=pltpu.VMEM)
    half = pltpu.VMEM(((2 * levels + 1) * count, width), jnp.float32)
    return pl.pallas_call(
        prepare_kernel,
        out_shape=(half, half),
        in_specs=[pl.BlockSpec(memory_space=pl.ANY)] * 7,
        out_specs=(vmem, vmem),
        scratch_shapes=[pltpu.SMEM((1,), jnp.int32)]
        + [pltpu.VMEM(thick.shape, jnp.float32)] * 5
        + [pltpu.VMEM(ne.shape, jnp.int32), pltpu.SemaphoreType.DMA((7,))],
        name="prepare",
    )(owner, thick, fe, fn, ce, cn, ne)


def pack_kernel(mass, last, first, padded, moved):
    tracers, levels, count, width = mass.shape
    lane = lane_index((count, width))
    zero_rows = jnp.zeros((PAD, width), jnp.float32)

    def level(l, carry):
        a = jnp.zeros((count, width), jnp.float32)
        b = a
        for t in range(tracers):
            value = mass[t, l]
            inside = (lane >= EDGE * t) & (lane < EDGE * (t + 1))
            a = jnp.where(inside, lanes(value, EDGE * (t + 1)), a)
            b = jnp.where(inside, lanes(value, EDGE * t), b)
            padded[t, l, :PAD, :] = zero_rows
            padded[t, l, PAD : PAD + count, :] = value
            padded[t, l, PAD + count :, :] = zero_rows
            for k, shift in enumerate(NEAR):
                moved[k, t, l] = lanes(value, -shift)
        last[l] = a
        first[l] = b
        return carry

    lax.fori_loop(0, levels, level, 0)


def pack(mass):
    tracers, levels, count, width = mass.shape
    vmem = pl.BlockSpec(memory_space=pltpu.VMEM)
    packed = pltpu.VMEM((levels, count, width), jnp.float32)
    last, first, padded, moved = pl.pallas_call(
        pack_kernel,
        out_shape=(
            packed,
            packed,
            pltpu.VMEM((tracers, levels, count + 2 * PAD, width), jnp.float32),
            pltpu.VMEM((len(NEAR),) + mass.shape, jnp.float32),
        ),
        in_specs=[vmem],
        out_specs=(vmem,) * 4,
        compiler_params=pltpu.CompilerParams(vmem_limit_bytes=24 * 1024 * 1024),
        cost_estimate=pl.CostEstimate(flops=2000000, bytes_accessed=1000000, transcendentals=0),
        name="pack",
    )(mass)
    rows_flat = (levels * count, width)
    return last.reshape(rows_flat), first.reshape(rows_flat), padded, moved


def transport_kernel(
    mine, other, west, east, padded, shifted, out,
    east_c, north_c, inverse, corrections, inners, middle, partial, stage, sems,
):
    tracers, levels, count, width = out.shape
    shape = (count, width)
    lane = lane_index(shape)
    low = position() % 2 == 0
    segment = sum(((lane >= SEG * k).astype(jnp.int32) for k in range(1, PACK)), jnp.zeros(shape, jnp.int32))
    in_segment = lane - SEG * segment
    packed_lane = lane < SEG * PACK
    at_edge = (lane < EDGE) | (lane >= width - EDGE)
    from_west_lane = in_segment < EDGE
    zero_rows = jnp.zeros((PAD, width), jnp.float32)
    for slot in range(2):
        for j in range(GROUP):
            middle[slot, j, :PAD, :] = zero_rows
            middle[slot, j, PAD + count :, :] = zero_rows

    base = levels * count
    met_east = east[base : base + count, :]
    met_lane = sum((jnp.where(lane >= MET_SEG * l, MET_SEG, 0) for l in range(1, levels)), jnp.zeros(shape, jnp.int32))
    met = jnp.where(lane - met_lane < EDGE, west[base : base + count, :], met_east)
    beyond = east_taps(met_east, lanes(met_east, -1))
    edge_index = jnp.where(packed_lane, in_segment + (width - EDGE), 0)
    edge_index = jnp.where(edge_index >= width, edge_index - width, edge_index)
    moved_index = {0: edge_index, -STEP: lanes(edge_index, -STEP), STEP: lanes(edge_index, STEP)}
    held = jnp.where(packed_lane, in_segment, -2 * SEG)
    moved_segment = {0: held, -STEP: lanes(held, -STEP), STEP: lanes(held, STEP)}

    def outer_sum(outer, cells):
        near = {shift: lanes(cells, -shift) for shift in NEAR}
        near[0] = cells
        parts = {}
        for m in outer:
            shift = east_group(m)
            term = outer[m] * near[m - shift]
            parts[shift] = parts[shift] + term if shift in parts else term
        return parts[0] + (lanes(parts[-STEP], STEP) + lanes(parts[STEP], -STEP))

    def level(l, carry):
        level_rows = pl.ds(pl.multiple_of(l * count, count), count)
        fields = []
        for half in range(2):
            for k in range(2):
                place = pl.ds(pl.multiple_of((k * levels + l) * count, count), count)
                a = mine[place, :]
                b = other[place, :]
                fields.append(jnp.where(low, a, b) if half == 0 else jnp.where(low, b, a))
        thickness, east_courant, north_courant, whole = fields
        last = width - 1 - MET_SEG * l - SEG
        edge_mass = jnp.where(lane == width - 1, pltpu.roll(met_east, last - 2, 1), 0.0)
        inverse[l] = 2.0 / (thickness - edge_mass)
        here = east_taps(east_courant, whole)
        ahead = {
            m: jnp.where(lane == width - 1, pltpu.roll(beyond[m], last, 1), lanes(here[m], -1)) for m in here
        }
        taps = difference_taps(here, ahead, EDGE)
        outer = {}
        for m in range(-EDGE, EDGE + 1):
            value = taps[m]
            if m != 0:
                q = moved_segment[east_group(m)]
                crosses = ((q < EDGE) != (q + m < EDGE)) & (q >= 0)
                outer[m] = jnp.where(crosses, pick(value, moved_index[east_group(m)]), 0.0)
            if m < 0:
                value = jnp.where(lane >= -m, value, 0.0)
            if m > 0:
                value = jnp.where(lane < width - m, value, 0.0)
            shift = east_group(m)
            east_c[m + EDGE, l] = lanes(value, shift) if shift else value
        for m, value in enumerate(north_coefficients(north_courant)):
            north_c[m, l] = value

        edge_taps = north_coefficients(pick(north_courant, edge_index))
        packed_taps = north_coefficients(pick(met, jnp.where(packed_lane, in_segment + MET_SEG * l, 0)))
        for half in range(2):
            west_index = jnp.where(
                packed_lane, in_segment + EDGE * (segment + PACK * half), 0
            )
            east_index = west_index - EDGE
            cells = jnp.where(
                from_west_lane,
                pick(west[level_rows, :], jnp.where(from_west_lane, west_index, 0)),
                pick(east[level_rows, :], jnp.where(from_west_lane, 0, jnp.maximum(east_index, 0))),
            )
            inner = cells
            for m in range(-3, 4):
                inner = inner + packed_taps[m + 3] * rows(cells, -m)
            first = outer_sum(outer, cells)
            total = outer_sum(outer, inner)
            for m in range(-3, 4):
                total = total + edge_taps[m + 3] * rows(first, -m)
            for k in range(PACK):
                moved = lanes(total, width - EDGE - SEG * k)
                corrections[half * PACK + k, l] = jnp.where(at_edge, moved, 0.0)
        return carry

    lax.fori_loop(0, levels, level, 0)

    def east_parts(taps, near):
        parts = {}
        for m in range(-EDGE, EDGE + 1):
            shift = east_group(m)
            term = taps[m + EDGE] * near[m - shift]
            parts[shift] = parts[shift] + term if shift in parts else term
        return parts

    steps = levels * (tracers // GROUP)

    def block(b):
        return slice(b * BLOCK, (b + 1) * BLOCK)

    def padded_block(b, m=0):
        return slice(PAD + b * BLOCK + m, PAD + (b + 1) * BLOCK + m)

    def place(step):
        step = jnp.clip(step, 0, steps - 1)
        return step % levels, (step // levels) * GROUP

    def copy(step):
        l, t0 = place(step)
        where = pl.ds(t0, GROUP)
        return pltpu.make_async_copy(stage.at[where, l], out.at[where, l], sems.at[step])

    def front(step):
        l, t0 = place(step)
        slot = (step + 2) % 2
        for b in range(count // BLOCK):
            taps = [east_c[m, l, block(b), :] for m in range(2 * EDGE + 1)]
            north = [north_c[m, l, block(b), :] for m in range(7)]
            for j in range(GROUP):
                x = padded[t0 + j, l, padded_block(b), :]
                inner = x + north[3] * x
                for m in (-3, -2, -1, 1, 2, 3):
                    inner = inner + north[m + 3] * padded[t0 + j, l, padded_block(b, m), :]
                inners[slot, j, block(b), :] = inner
                near = {0: x}
                for k, shift in enumerate(NEAR):
                    near[shift] = shifted[k, t0 + j, l, block(b), :]
                parts = east_parts(taps, near)
                middle[slot, j, padded_block(b), :] = (x + parts[0]) + (
                    lanes(parts[-STEP], STEP) + lanes(parts[STEP], -STEP)
                )

    def back(step):
        l, t0 = place(step)
        slot = (step + 2) % 2
        for b in range(count // BLOCK):
            taps = [east_c[m, l, block(b), :] for m in range(2 * EDGE + 1)]
            north = [north_c[m, l, block(b), :] for m in range(7)]
            for j in range(GROUP):
                inner = inners[slot, j, block(b), :]
                near = {0: inner}
                for shift in NEAR:
                    near[shift] = lanes(inner, -shift)
                parts = east_parts(taps, near)
                total = 0.5 * padded[t0 + j, l, padded_block(b), :] + parts[0]
                for m in range(-3, 4):
                    total = total + north[m + 3] * middle[slot, j, padded_block(b, m), :]
                partial[slot, 0, j, block(b), :] = total
                partial[slot, 1, j, block(b), :] = parts[-STEP]
                partial[slot, 2, j, block(b), :] = parts[STEP]

    def finish(step):
        l, t0 = place(step)
        slot = (step + 2) % 2
        for b in range(count // BLOCK):
            scale = inverse[l, block(b), :]
            for j in range(GROUP):
                total = partial[slot, 0, j, block(b), :] + (
                    lanes(partial[slot, 1, j, block(b), :], STEP)
                    + lanes(partial[slot, 2, j, block(b), :], -STEP)
                )
                stage[t0 + j, l, block(b), :] = (total + corrections[t0 + j, l, block(b), :]) * scale

    def step_of_three(step, carry):
        finish(step - 1)
        back(step)
        front(step + 1)

        @pl.when(step >= 1)
        def _():
            copy(step - 1).start()

        return carry

    lax.fori_loop(-1, steps + 1, step_of_three, 0)
    for step in range(steps):
        copy(step).wait()


def east_group(m):
    return -STEP if m < -1 else (STEP if m > 2 else 0)


def transport(mine, other, west, east, padded, shifted):
    tracers, levels, count, width = shifted.shape[1:]
    vmem = pl.BlockSpec(memory_space=pltpu.VMEM)
    return pl.pallas_call(
        transport_kernel,
        out_shape=jax.ShapeDtypeStruct(shifted.shape[1:], jnp.float32),
        in_specs=[vmem] * 6,
        out_specs=pl.BlockSpec(memory_space=pl.ANY),
        scratch_shapes=[
            pltpu.VMEM((2 * EDGE + 1, levels, count, width), jnp.float32),
            pltpu.VMEM((7, levels, count, width), jnp.float32),
            pltpu.VMEM((levels, count, width), jnp.float32),
            pltpu.VMEM((tracers, levels, count, width), jnp.float32),
            pltpu.VMEM((2, GROUP, count, width), jnp.float32),
            pltpu.VMEM((2, GROUP, count + 2 * PAD, width), jnp.float32),
            pltpu.VMEM((2, 3, GROUP, count, width), jnp.float32),
            pltpu.VMEM((tracers, levels, count, width), jnp.float32),
            pltpu.SemaphoreType.DMA((levels * (tracers // GROUP),)),
        ],
        compiler_params=pltpu.CompilerParams(vmem_limit_bytes=24 * 1024 * 1024),
        name="transport",
    )(mine, other, west, east, padded, shifted)


def ring(x, by):
    size = lax.axis_size("space")
    return lax.ppermute(x, "space", [(i, (i + by) % size) for i in range(size)])


def exchange(x, flip):
    size = lax.axis_size("tracer")
    return lax.ppermute(x, "tracer", [(i, i ^ flip) for i in range(size)])


def turn(x, by):
    size = lax.axis_size("tracer")
    return lax.ppermute(x, "tracer", [(i, i // 8 * 8 + (i + 2 * by) % 8) for i in range(size)])


def shards(mass, thick, fe, fn, ce, cn, ne, owner):
    keep, send = prepare(owner, thick, fe, fn, ce, cn, ne)
    last, first, padded, shifted = pack(mass)
    total = keep + exchange(send, 1)
    total = total + (turn(total, 1) + turn(total, -1) + turn(total, 2))
    total = total + exchange(total, 8)
    main = 2 * mass.shape[1] * mass.shape[2]
    mine = total[:main]
    edges = total[main:]
    other = exchange(mine, 1)
    west = ring(jnp.concatenate([last, edges]), 1)
    east = ring(jnp.concatenate([first, edges]), -1)
    return transport(mine, other, west, east, padded, shifted)


def solution(mesh):
    spec = P("tracer", None, None, "space")
    return jax.shard_map(
        shards, mesh=mesh, in_specs=(spec,) * 7 + (P("space"),), out_specs=spec, check_vma=False
    )
```

```python
import jax
import jax.numpy as jnp
from jax import lax
from jax.experimental import pallas as pl
from jax.experimental.pallas import tpu as pltpu
from jax.sharding import PartitionSpec as P

NS = 2
EDGE = NS + 3
SEG = 2 * EDGE
PACK = 9
STEP = 4
GROUP = 3
PAD = 8
BLOCK = 8
NEAR = (-1, 1, 2)
MET_SEG = 16


def lane_index(shape):
    return lax.broadcasted_iota(jnp.int32, shape, len(shape) - 1)


def row_index(shape):
    return lax.broadcasted_iota(jnp.int32, shape, len(shape) - 2)


def lanes(x, shift):
    return pltpu.roll(x, shift % x.shape[-1], x.ndim - 1)


def rows(x, shift):
    return pltpu.roll(x, shift % x.shape[-2], x.ndim - 2)


def face_weights(courant):
    fraction = jnp.abs(courant)
    ramp = 1.5 * fraction * (1.0 - 2.0 / 3.0 * fraction)
    near = 0.5 * courant * (1.0 - 0.5 * fraction - ramp)
    far = 0.5 * courant * (0.5 * fraction - ramp)
    mean = courant * ramp
    far_outer = far * (1.0 / 12.0)
    near_outer = near * (1.0 / 12.0)
    return (
        -near_outer,
        7.0 * near_outer - far_outer,
        7.0 * (near_outer + far_outer) + mean,
        7.0 * far_outer - near_outer,
        -far_outer,
    )


def north_taps(courant):
    down1, up0, up1, up2, up3 = (w for w in face_weights(courant))
    forward = courant >= 0.0
    zero = jnp.zeros_like(courant)
    f = {1: down1, 0: up0, -1: up1, -2: up2, -3: up3}
    b = {-2: down1, -1: up0, 0: up1, 1: up2, 2: up3}
    return {m: jnp.where(forward, f.get(m, zero), b.get(m, zero)) for m in range(-3, 3)}


def east_taps(courant, whole):
    weights = face_weights(courant)
    forward = courant >= 0.0
    zero = jnp.zeros_like(courant)
    one = whole == 1.0
    two = whole == 2.0
    some = whole > 0.5
    taps = {}
    for m in range(-EDGE, EDGE):
        ahead = []
        behind = []
        for n in range(NS + 1):
            place = 1 - n - m
            ahead.append(weights[place] if 0 <= place < 5 else zero)
            place = m + 2 - n
            behind.append(weights[place] if 0 <= place < 5 else zero)
        f = jnp.where(two, ahead[2], jnp.where(one, ahead[1], ahead[0]))
        b = jnp.where(two, behind[2], jnp.where(one, behind[1], behind[0]))
        if m == -1:
            f = f + jnp.where(some, 0.5, 0.0)
        if m == -2:
            f = f + jnp.where(two, 0.5, 0.0)
        if m == 0:
            b = b - jnp.where(some, 0.5, 0.0)
        if m == 1:
            b = b - jnp.where(two, 0.5, 0.0)
        taps[m] = jnp.where(forward, f, b)
    return taps


def difference_taps(here, ahead, reach):
    out = {}
    for m in range(-reach, reach + 1):
        if m in here and m - 1 in ahead:
            out[m] = here[m] - ahead[m - 1]
        elif m in here:
            out[m] = here[m]
        else:
            out[m] = -ahead[m - 1]
    return out


def north_coefficients(courant):
    count = courant.shape[0]
    row = row_index(courant.shape)
    here = north_taps(jnp.where(row == 0, 0.0, courant))
    taps = difference_taps(here, {m: rows(here[m], -1) for m in here}, 3)
    return [
        jnp.where((row + m >= 0) & (row + m < count), taps[m], 0.0) for m in range(-3, 4)
    ]


def pick(x, index):
    return jnp.take_along_axis(x, index, axis=1, mode="promise_in_bounds")


def position():
    return lax.axis_index("tracer")


def prepare_kernel(*refs):
    sources, (keep, send, *fields, sems) = refs[:6], refs[6:]
    copies = [
        pltpu.make_async_copy(source, place, sems.at[k])
        for k, (source, place) in enumerate(zip(sources, fields))
    ]
    for copy in copies:
        copy.start()
    for copy in copies:
        copy.wait()
    thick, fe, fn, ce, cn, ne = fields
    core = position() % 2
    levels, count, width = thick.shape[1:]
    lane = lane_index((count, width))
    row = row_index((count, width))
    edge_rows = jnp.zeros((count, width), jnp.float32)
    for l in range(levels):
        east_mass = fe[0, l]
        north_mass = jnp.where(row == 0, 0.0, fn[0, l])
        thickness = (
            thick[0, l]
            + (east_mass - jnp.where(lane == width - 1, 0.0, lanes(east_mass, -1)))
            + (north_mass - rows(north_mass, -1))
        )
        whole = ne[0, l].astype(jnp.float32)
        first = (thickness, ce[0, l])
        second = (cn[0, l], whole)
        for k in range(2):
            start = (k * levels + l) * count
            keep[start : start + count, :] = jnp.where(core == 0, first[k], second[k])
            send[start : start + count, :] = jnp.where(core == 0, second[k], first[k])
        edges = jnp.where(lane < SEG, lanes(cn[0, l], EDGE), 0.0)
        for k, value in enumerate((ce[0, l], whole, east_mass)):
            edges = jnp.where(lane == SEG + k, lanes(value, SEG + k), edges)
        edge_rows = edge_rows + lanes(jnp.where(lane < MET_SEG, edges, 0.0), MET_SEG * l)
    base = 2 * levels * count
    keep[base : base + count, :] = edge_rows
    send[base : base + count, :] = edge_rows


def prepare(thick, fe, fn, ce, cn, ne):
    levels, count, width = thick.shape[1:]
    vmem = pl.BlockSpec(memory_space=pltpu.VMEM)
    half = pltpu.VMEM(((2 * levels + 1) * count, width), jnp.float32)
    return pl.pallas_call(
        prepare_kernel,
        out_shape=(half, half),
        in_specs=[pl.BlockSpec(memory_space=pl.ANY)] * 6,
        out_specs=(vmem, vmem),
        scratch_shapes=[pltpu.VMEM(thick.shape, jnp.float32)] * 5
        + [pltpu.VMEM(ne.shape, jnp.int32), pltpu.SemaphoreType.DMA((6,))],
        name="prepare",
    )(thick, fe, fn, ce, cn, ne)


def pack_kernel(mass, last, first, padded, moved):
    tracers, levels, count, width = mass.shape
    lane = lane_index((count, width))
    zero_rows = jnp.zeros((PAD, width), jnp.float32)

    def level(l, carry):
        a = jnp.zeros((count, width), jnp.float32)
        b = a
        for t in range(tracers):
            value = mass[t, l]
            inside = (lane >= EDGE * t) & (lane < EDGE * (t + 1))
            a = jnp.where(inside, lanes(value, EDGE * (t + 1)), a)
            b = jnp.where(inside, lanes(value, EDGE * t), b)
            padded[t, l, :PAD, :] = zero_rows
            padded[t, l, PAD : PAD + count, :] = value
            padded[t, l, PAD + count :, :] = zero_rows
            for k, shift in enumerate(NEAR):
                moved[k, t, l] = lanes(value, -shift)
        last[l] = a
        first[l] = b
        return carry

    lax.fori_loop(0, levels, level, 0)


def pack(mass):
    tracers, levels, count, width = mass.shape
    vmem = pl.BlockSpec(memory_space=pltpu.VMEM)
    packed = pltpu.VMEM((levels, count, width), jnp.float32)
    last, first, padded, moved = pl.pallas_call(
        pack_kernel,
        out_shape=(
            packed,
            packed,
            pltpu.VMEM((tracers, levels, count + 2 * PAD, width), jnp.float32),
            pltpu.VMEM((len(NEAR),) + mass.shape, jnp.float32),
        ),
        in_specs=[vmem],
        out_specs=(vmem,) * 4,
        compiler_params=pltpu.CompilerParams(vmem_limit_bytes=24 * 1024 * 1024),
        cost_estimate=pl.CostEstimate(flops=2000000, bytes_accessed=1000000, transcendentals=0),
        name="pack",
    )(mass)
    rows_flat = (levels * count, width)
    return last.reshape(rows_flat), first.reshape(rows_flat), padded, moved


def segments(shape):
    lane = lane_index(shape)
    segment = sum(
        ((lane >= SEG * k).astype(jnp.int32) for k in range(1, PACK)), jnp.zeros(shape, jnp.int32)
    )
    return segment, lane - SEG * segment, lane < SEG * PACK


def moved_places(held):
    return {shift: lanes(held, shift) if shift else held for shift in (-STEP, 0, STEP)}


def east_parts(taps, near, parts=None):
    parts = dict(parts or {})
    for m in taps:
        shift = east_group(m)
        term = taps[m] * near[m - shift]
        parts[shift] = parts[shift] + term if shift in parts else term
    return parts


def moved_sum(parts):
    return parts[0] + (lanes(parts[-STEP], STEP) + lanes(parts[STEP], -STEP))


def near_cells(x):
    return {0: x, **{shift: lanes(x, -shift) for shift in NEAR}}


def inner_kernel(
    mine, other, padded, shifted, sums, outer_c, edge_c, thickness,
    east_c, north_c, inners, middle, partial,
):
    tracers, levels, count, width = sums.shape
    shape = (count, width)
    lane = lane_index(shape)
    low = position() % 2 == 0
    _, in_segment, packed_lane = segments(shape)
    zero_rows = jnp.zeros((PAD, width), jnp.float32)
    for slot in range(2):
        for j in range(GROUP):
            middle[slot, j, :PAD, :] = zero_rows
            middle[slot, j, PAD + count :, :] = zero_rows
    edge_index = jnp.where(packed_lane, in_segment + (width - EDGE), 0)
    edge_index = jnp.where(edge_index >= width, edge_index - width, edge_index)
    moved_index = moved_places(edge_index)
    moved_segment = moved_places(jnp.where(packed_lane, in_segment, -2 * SEG))

    def level(l, carry):
        fields = []
        for half in range(2):
            for k in range(2):
                place = pl.ds(pl.multiple_of((k * levels + l) * count, count), count)
                a = mine[place, :]
                b = other[place, :]
                fields.append(jnp.where(low, a, b) if half == 0 else jnp.where(low, b, a))
        thick, east_courant, north_courant, whole = fields
        thickness[l] = thick
        here = east_taps(east_courant, whole)
        ahead = {m: jnp.where(lane == width - 1, 0.0, lanes(here[m], -1)) for m in here}
        taps = difference_taps(here, ahead, EDGE)
        for m in range(-EDGE, EDGE + 1):
            value = taps[m]
            if m != 0:
                q = moved_segment[east_group(m)]
                crosses = ((q < EDGE) != (q + m < EDGE)) & (q >= 0)
                outer_c[m + EDGE, l] = jnp.where(crosses, pick(value, moved_index[east_group(m)]), 0.0)
            if m < 0:
                value = jnp.where(lane >= -m, value, 0.0)
            if m > 0:
                value = jnp.where(lane < width - m, value, 0.0)
            shift = east_group(m)
            east_c[m + EDGE, l] = lanes(value, shift) if shift else value
        for m, value in enumerate(north_coefficients(north_courant)):
            north_c[m, l] = value
        for m, value in enumerate(north_coefficients(pick(north_courant, edge_index))):
            edge_c[m, l] = value
        return carry

    lax.fori_loop(0, levels, level, 0)
    steps = levels * (tracers // GROUP)

    def block(b):
        return slice(b * BLOCK, (b + 1) * BLOCK)

    def padded_block(b, m=0):
        return slice(PAD + b * BLOCK + m, PAD + (b + 1) * BLOCK + m)

    def place(step):
        step = jnp.clip(step, 0, steps - 1)
        return step % levels, (step // levels) * GROUP

    def weights(ref, l, b, reach):
        return {m: ref[m + reach, l, block(b), :] for m in range(-reach, reach + 1)}

    def front(step):
        l, t0 = place(step)
        slot = (step + 2) % 2
        for b in range(count // BLOCK):
            taps = weights(east_c, l, b, EDGE)
            north = weights(north_c, l, b, 3)
            for j in range(GROUP):
                x = padded[t0 + j, l, padded_block(b), :]
                inner = x + north[0] * x
                for m in (-3, -2, -1, 1, 2, 3):
                    inner = inner + north[m] * padded[t0 + j, l, padded_block(b, m), :]
                inners[slot, j, block(b), :] = inner
                near = {0: x}
                for k, shift in enumerate(NEAR):
                    near[shift] = shifted[k, t0 + j, l, block(b), :]
                middle[slot, j, padded_block(b), :] = x + moved_sum(east_parts(taps, near))

    def back(step):
        l, t0 = place(step)
        slot = (step + 2) % 2
        for b in range(count // BLOCK):
            taps = weights(east_c, l, b, EDGE)
            north = weights(north_c, l, b, 3)
            for j in range(GROUP):
                parts = east_parts(taps, near_cells(inners[slot, j, block(b), :]))
                total = 0.5 * padded[t0 + j, l, padded_block(b), :] + parts[0]
                for m in range(-3, 4):
                    total = total + north[m] * middle[slot, j, padded_block(b, m), :]
                partial[slot, 0, j, block(b), :] = total
                partial[slot, 1, j, block(b), :] = parts[-STEP]
                partial[slot, 2, j, block(b), :] = parts[STEP]

    def finish(step):
        l, t0 = place(step)
        slot = (step + 2) % 2
        for b in range(count // BLOCK):
            for j in range(GROUP):
                sums[t0 + j, l, block(b), :] = partial[slot, 0, j, block(b), :] + (
                    lanes(partial[slot, 1, j, block(b), :], STEP)
                    + lanes(partial[slot, 2, j, block(b), :], -STEP)
                )

    def step_of_three(step, carry):
        finish(step - 1)
        back(step)
        front(step + 1)
        return carry

    lax.fori_loop(-1, steps + 1, step_of_three, 0)


def inner_update(mine, other, padded, shifted):
    tracers, levels, count, width = shifted.shape[1:]
    vmem = pl.BlockSpec(memory_space=pltpu.VMEM)
    level = (levels, count, width)
    return pl.pallas_call(
        inner_kernel,
        out_shape=(
            pltpu.VMEM((tracers,) + level, jnp.float32),
            pltpu.VMEM((2 * EDGE + 1,) + level, jnp.float32),
            pltpu.VMEM((7,) + level, jnp.float32),
            pltpu.VMEM(level, jnp.float32),
        ),
        in_specs=[vmem] * 4,
        out_specs=(vmem,) * 4,
        scratch_shapes=[
            pltpu.VMEM((2 * EDGE + 1,) + level, jnp.float32),
            pltpu.VMEM((7,) + level, jnp.float32),
            pltpu.VMEM((2, GROUP, count, width), jnp.float32),
            pltpu.VMEM((2, GROUP, count + 2 * PAD, width), jnp.float32),
            pltpu.VMEM((2, 3, GROUP, count, width), jnp.float32),
        ],
        compiler_params=pltpu.CompilerParams(vmem_limit_bytes=24 * 1024 * 1024),
        cost_estimate=pl.CostEstimate(flops=20000000, bytes_accessed=6000000, transcendentals=0),
        name="inner",
    )(mine, other, padded, shifted)


def edge_kernel(west, east, own, sums, outer_c, edge_c, thickness, out, stage, sems):
    tracers, levels, count, width = sums.shape
    shape = (count, width)
    lane = lane_index(shape)
    segment, in_segment, packed_lane = segments(shape)
    from_west_lane = in_segment < EDGE
    at_edge = (lane < EDGE) | (lane >= width - EDGE)
    last_face = {
        shift: q == EDGE - 1
        for shift, q in moved_places(jnp.where(packed_lane, in_segment, -2 * SEG)).items()
    }
    base = levels * count
    met_east = east[base : base + count, :]
    met_west = west[base : base + count, :]

    def copy(l):
        return pltpu.make_async_copy(stage.at[:, l], out.at[:, l], sems.at[l])

    def level(l, carry):
        level_rows = pl.ds(pl.multiple_of(l * count, count), count)
        met_lane = jnp.where(packed_lane, in_segment + MET_SEG * l, 0)
        met = jnp.where(lane - MET_SEG * l < EDGE, met_west, met_east)
        beyond = east_taps(
            pick(met_east, jnp.full(shape, SEG, jnp.int32) + MET_SEG * l),
            pick(met_east, jnp.full(shape, SEG + 1, jnp.int32) + MET_SEG * l),
        )
        mass_flux = pick(met_east, jnp.full(shape, SEG + 2, jnp.int32) + MET_SEG * l)
        inverse = 2.0 / (thickness[l] - jnp.where(lane == width - 1, mass_flux, 0.0))
        face = {
            m: jnp.where(last_face[east_group(m)], -beyond[m - 1], 0.0)
            for m in range(1 - EDGE, EDGE + 1)
        }
        outer = {m: outer_c[m + EDGE, l] for m in range(-EDGE, EDGE + 1) if m != 0}
        for m in range(1, EDGE + 1):
            outer[m] = outer[m] + face[m]
        inside = {m: face[m] for m in range(1 - EDGE, 1)}
        edge_taps = [edge_c[m, l] for m in range(7)]
        packed_taps = north_coefficients(pick(met, met_lane))
        for half in range(2):
            first_lane = EDGE * (segment + PACK * half) + in_segment
            west_index = jnp.where(packed_lane & from_west_lane, first_lane, 0)
            east_index = jnp.where(packed_lane & ~from_west_lane, first_lane - EDGE, 0)
            own_cells = pick(own[level_rows, :], west_index)
            cells = jnp.where(
                from_west_lane,
                pick(west[level_rows, :], west_index),
                pick(east[level_rows, :], east_index),
            )
            inner = cells
            own_inner = own_cells
            for m in range(-3, 4):
                inner = inner + packed_taps[m + 3] * rows(cells, -m)
                own_inner = own_inner + edge_taps[m + 3] * rows(own_cells, -m)
            first = moved_sum(
                east_parts(inside, near_cells(own_cells), east_parts(outer, near_cells(cells)))
            )
            total = moved_sum(
                east_parts(inside, near_cells(own_inner), east_parts(outer, near_cells(inner)))
            )
            for m in range(-3, 4):
                total = total + edge_taps[m + 3] * rows(first, -m)
            for k in range(PACK):
                t = half * PACK + k
                moved = jnp.where(at_edge, lanes(total, width - EDGE - SEG * k), 0.0)
                stage[t, l] = (sums[t, l] + moved) * inverse
        copy(l).start()
        return carry

    lax.fori_loop(0, levels, level, 0)
    for l in range(levels):
        copy(l).wait()


def edge_update(west, east, own, sums, outer_c, edge_c, thickness):
    tracers, levels, count, width = sums.shape
    vmem = pl.BlockSpec(memory_space=pltpu.VMEM)
    return pl.pallas_call(
        edge_kernel,
        out_shape=jax.ShapeDtypeStruct(sums.shape, jnp.float32),
        in_specs=[vmem] * 7,
        out_specs=pl.BlockSpec(memory_space=pl.ANY),
        scratch_shapes=[pltpu.VMEM(sums.shape, jnp.float32), pltpu.SemaphoreType.DMA((levels,))],
        compiler_params=pltpu.CompilerParams(vmem_limit_bytes=24 * 1024 * 1024),
        name="edges",
    )(west, east, own, sums, outer_c, edge_c, thickness)


def east_group(m):
    return -STEP if m < -1 else (STEP if m > 2 else 0)


def ring(x, by):
    size = lax.axis_size("space")
    return lax.ppermute(x, "space", [(i, (i + by) % size) for i in range(size)])


def exchange(x, flip):
    size = lax.axis_size("tracer")
    return lax.ppermute(x, "tracer", [(i, i ^ flip) for i in range(size)])


def turn(x, by):
    size = lax.axis_size("tracer")
    return lax.ppermute(x, "tracer", [(i, i // 8 * 8 + (i + 2 * by) % 8) for i in range(size)])


def shards(mass, thick, fe, fn, ce, cn, ne, owner):
    keep, send = prepare(thick, fe, fn, ce, cn, ne)
    last, first, padded, shifted = pack(mass)
    me, chosen = position(), owner[0]
    other_core = exchange(send, 1)
    total = jnp.where(chosen == me, keep, jnp.where(chosen == me ^ 1, other_core, 0.0))
    total = total + (turn(total, 1) + turn(total, -1) + turn(total, 2))
    total = total + exchange(total, 8)
    main = 2 * mass.shape[1] * mass.shape[2]
    mine = total[:main]
    edges = total[main:]
    other = exchange(mine, 1)
    west = ring(jnp.concatenate([last, edges]), 1)
    east = ring(jnp.concatenate([first, edges]), -1)
    return edge_update(west, east, last, *inner_update(mine, other, padded, shifted))


def solution(mesh):
    spec = P("tracer", None, None, "space")
    return jax.shard_map(
        shards, mesh=mesh, in_specs=(spec,) * 7 + (P("space"),), out_specs=spec, check_vma=False
    )
```

```python
import jax
import jax.numpy as jnp
from jax import lax
from jax.experimental import pallas as pl
from jax.experimental.pallas import tpu as pltpu
from jax.sharding import PartitionSpec as P

NS = 2
EDGE = NS + 3
SEG = 2 * EDGE
PACK = 9
STEP = 4
GROUP = 3
PAD = 8
BLOCK = 8
NEAR = (-1, 1, 2)
MET_SEG = 16


def lane_index(shape):
    return lax.broadcasted_iota(jnp.int32, shape, len(shape) - 1)


def row_index(shape):
    return lax.broadcasted_iota(jnp.int32, shape, len(shape) - 2)


def lanes(x, shift):
    return pltpu.roll(x, shift % x.shape[-1], x.ndim - 1)


def rows(x, shift):
    return pltpu.roll(x, shift % x.shape[-2], x.ndim - 2)


def face_weights(courant):
    fraction = jnp.abs(courant)
    ramp = 1.5 * fraction * (1.0 - 2.0 / 3.0 * fraction)
    near = 0.5 * courant * (1.0 - 0.5 * fraction - ramp)
    far = 0.5 * courant * (0.5 * fraction - ramp)
    mean = courant * ramp
    far_outer = far * (1.0 / 12.0)
    near_outer = near * (1.0 / 12.0)
    return (
        -near_outer,
        7.0 * near_outer - far_outer,
        7.0 * (near_outer + far_outer) + mean,
        7.0 * far_outer - near_outer,
        -far_outer,
    )


def north_taps(courant):
    down1, up0, up1, up2, up3 = (w for w in face_weights(courant))
    forward = courant >= 0.0
    zero = jnp.zeros_like(courant)
    f = {1: down1, 0: up0, -1: up1, -2: up2, -3: up3}
    b = {-2: down1, -1: up0, 0: up1, 1: up2, 2: up3}
    return {m: jnp.where(forward, f.get(m, zero), b.get(m, zero)) for m in range(-3, 3)}


def east_taps(courant, whole):
    weights = face_weights(courant)
    forward = courant >= 0.0
    zero = jnp.zeros_like(courant)
    one = whole == 1.0
    two = whole == 2.0
    some = whole > 0.5
    taps = {}
    for m in range(-EDGE, EDGE):
        ahead = []
        behind = []
        for n in range(NS + 1):
            place = 1 - n - m
            ahead.append(weights[place] if 0 <= place < 5 else zero)
            place = m + 2 - n
            behind.append(weights[place] if 0 <= place < 5 else zero)
        f = jnp.where(two, ahead[2], jnp.where(one, ahead[1], ahead[0]))
        b = jnp.where(two, behind[2], jnp.where(one, behind[1], behind[0]))
        if m == -1:
            f = f + jnp.where(some, 0.5, 0.0)
        if m == -2:
            f = f + jnp.where(two, 0.5, 0.0)
        if m == 0:
            b = b - jnp.where(some, 0.5, 0.0)
        if m == 1:
            b = b - jnp.where(two, 0.5, 0.0)
        taps[m] = jnp.where(forward, f, b)
    return taps


def difference_taps(here, ahead, reach):
    out = {}
    for m in range(-reach, reach + 1):
        if m in here and m - 1 in ahead:
            out[m] = here[m] - ahead[m - 1]
        elif m in here:
            out[m] = here[m]
        else:
            out[m] = -ahead[m - 1]
    return out


def north_coefficients(courant):
    count = courant.shape[0]
    row = row_index(courant.shape)
    here = north_taps(jnp.where(row == 0, 0.0, courant))
    taps = difference_taps(here, {m: rows(here[m], -1) for m in here}, 3)
    return [
        jnp.where((row + m >= 0) & (row + m < count), taps[m], 0.0) for m in range(-3, 4)
    ]


def pick(x, index):
    return jnp.take_along_axis(x, index, axis=1, mode="promise_in_bounds")


def position():
    return lax.axis_index("tracer")


def prepare_kernel(*refs):
    sources, (keep, send, *fields, sems) = refs[:6], refs[6:]
    copies = [
        pltpu.make_async_copy(source, place, sems.at[k])
        for k, (source, place) in enumerate(zip(sources, fields))
    ]
    for copy in copies:
        copy.start()
    for copy in copies:
        copy.wait()
    thick, fe, fn, ce, cn, ne = fields
    core = position() % 2
    levels, count, width = thick.shape[1:]
    lane = lane_index((count, width))
    row = row_index((count, width))
    edge_rows = jnp.zeros((count, width), jnp.float32)
    for l in range(levels):
        east_mass = fe[0, l]
        north_mass = jnp.where(row == 0, 0.0, fn[0, l])
        thickness = (
            thick[0, l]
            + (east_mass - jnp.where(lane == width - 1, 0.0, lanes(east_mass, -1)))
            + (north_mass - rows(north_mass, -1))
        )
        whole = ne[0, l].astype(jnp.float32)
        first = (thickness, ce[0, l])
        second = (cn[0, l], whole)
        for k in range(2):
            start = (k * levels + l) * count
            keep[start : start + count, :] = jnp.where(core == 0, first[k], second[k])
            send[start : start + count, :] = jnp.where(core == 0, second[k], first[k])
        edges = jnp.where(lane < SEG, lanes(cn[0, l], EDGE), 0.0)
        for k, value in enumerate((ce[0, l], whole, east_mass)):
            edges = jnp.where(lane == SEG + k, lanes(value, SEG + k), edges)
        edge_rows = edge_rows + lanes(jnp.where(lane < MET_SEG, edges, 0.0), MET_SEG * l)
    base = 2 * levels * count
    folded = edge_rows[: count // 2] + lanes(edge_rows[count // 2 :], MET_SEG * levels)
    keep[base:, :] = folded
    send[base:, :] = folded


def prepare(thick, fe, fn, ce, cn, ne):
    levels, count, width = thick.shape[1:]
    vmem = pl.BlockSpec(memory_space=pltpu.VMEM)
    half = pltpu.VMEM((2 * levels * count + count // 2, width), jnp.float32)
    return pl.pallas_call(
        prepare_kernel,
        out_shape=(half, half),
        in_specs=[pl.BlockSpec(memory_space=pl.ANY)] * 6,
        out_specs=(vmem, vmem),
        scratch_shapes=[pltpu.VMEM(thick.shape, jnp.float32)] * 5
        + [pltpu.VMEM(ne.shape, jnp.int32), pltpu.SemaphoreType.DMA((6,))],
        name="prepare",
    )(thick, fe, fn, ce, cn, ne)


def pack_kernel(mass, last, first, padded, moved):
    tracers, levels, count, width = mass.shape
    lane = lane_index((count, width))
    zero_rows = jnp.zeros((PAD, width), jnp.float32)

    def level(l, carry):
        a = jnp.zeros((count, width), jnp.float32)
        b = a
        for t in range(tracers):
            value = mass[t, l]
            inside = (lane >= EDGE * t) & (lane < EDGE * (t + 1))
            a = jnp.where(inside, lanes(value, EDGE * (t + 1)), a)
            b = jnp.where(inside, lanes(value, EDGE * t), b)
            padded[t, l, :PAD, :] = zero_rows
            padded[t, l, PAD : PAD + count, :] = value
            padded[t, l, PAD + count :, :] = zero_rows
            for k, shift in enumerate(NEAR):
                moved[k, t, l] = lanes(value, -shift)
        last[l] = a
        first[l] = b
        return carry

    lax.fori_loop(0, levels, level, 0)


def pack(mass):
    tracers, levels, count, width = mass.shape
    vmem = pl.BlockSpec(memory_space=pltpu.VMEM)
    packed = pltpu.VMEM((levels, count, width), jnp.float32)
    last, first, padded, moved = pl.pallas_call(
        pack_kernel,
        out_shape=(
            packed,
            packed,
            pltpu.VMEM((tracers, levels, count + 2 * PAD, width), jnp.float32),
            pltpu.VMEM((len(NEAR),) + mass.shape, jnp.float32),
        ),
        in_specs=[vmem],
        out_specs=(vmem,) * 4,
        compiler_params=pltpu.CompilerParams(vmem_limit_bytes=24 * 1024 * 1024),
        cost_estimate=pl.CostEstimate(flops=2000000, bytes_accessed=1000000, transcendentals=0),
        name="pack",
    )(mass)
    rows_flat = (levels * count, width)
    return last.reshape(rows_flat), first.reshape(rows_flat), padded, moved


def segments(shape):
    lane = lane_index(shape)
    segment = sum(
        ((lane >= SEG * k).astype(jnp.int32) for k in range(1, PACK)), jnp.zeros(shape, jnp.int32)
    )
    return segment, lane - SEG * segment, lane < SEG * PACK


def moved_places(held):
    return {shift: lanes(held, shift) if shift else held for shift in (-STEP, 0, STEP)}


def east_parts(taps, near, parts=None):
    parts = dict(parts or {})
    for m in taps:
        shift = east_group(m)
        term = taps[m] * near[m - shift]
        parts[shift] = parts[shift] + term if shift in parts else term
    return parts


def moved_sum(parts):
    return parts[0] + (lanes(parts[-STEP], STEP) + lanes(parts[STEP], -STEP))


def near_cells(x):
    return {0: x, **{shift: lanes(x, -shift) for shift in NEAR}}


def inner_kernel(
    mine, other, padded, shifted, sums, outer_c, edge_c, thickness,
    east_c, north_c, inners, middle, partial,
):
    tracers, levels, count, width = sums.shape
    shape = (count, width)
    lane = lane_index(shape)
    low = position() % 2 == 0
    _, in_segment, packed_lane = segments(shape)
    zero_rows = jnp.zeros((PAD, width), jnp.float32)
    for slot in range(2):
        for j in range(GROUP):
            middle[slot, j, :PAD, :] = zero_rows
            middle[slot, j, PAD + count :, :] = zero_rows
    edge_index = jnp.where(packed_lane, in_segment + (width - EDGE), 0)
    edge_index = jnp.where(edge_index >= width, edge_index - width, edge_index)
    moved_index = moved_places(edge_index)
    moved_segment = moved_places(jnp.where(packed_lane, in_segment, -2 * SEG))

    def level(l, carry):
        fields = []
        for half in range(2):
            for k in range(2):
                place = pl.ds(pl.multiple_of((k * levels + l) * count, count), count)
                a = mine[place, :]
                b = other[place, :]
                fields.append(jnp.where(low, a, b) if half == 0 else jnp.where(low, b, a))
        thick, east_courant, north_courant, whole = fields
        thickness[l] = thick
        here = east_taps(east_courant, whole)
        ahead = {m: jnp.where(lane == width - 1, 0.0, lanes(here[m], -1)) for m in here}
        taps = difference_taps(here, ahead, EDGE)
        for m in range(-EDGE, EDGE + 1):
            value = taps[m]
            if m != 0:
                q = moved_segment[east_group(m)]
                crosses = ((q < EDGE) != (q + m < EDGE)) & (q >= 0)
                outer_c[m + EDGE, l] = jnp.where(crosses, pick(value, moved_index[east_group(m)]), 0.0)
            if m < 0:
                value = jnp.where(lane >= -m, value, 0.0)
            if m > 0:
                value = jnp.where(lane < width - m, value, 0.0)
            shift = east_group(m)
            east_c[m + EDGE, l] = lanes(value, shift) if shift else value
        for m, value in enumerate(north_coefficients(north_courant)):
            north_c[m, l] = value
        for m, value in enumerate(north_coefficients(pick(north_courant, edge_index))):
            edge_c[m, l] = value
        return carry

    lax.fori_loop(0, levels, level, 0)
    steps = levels * (tracers // GROUP)

    def block(b):
        return slice(b * BLOCK, (b + 1) * BLOCK)

    def padded_block(b, m=0):
        return slice(PAD + b * BLOCK + m, PAD + (b + 1) * BLOCK + m)

    def place(step):
        step = jnp.clip(step, 0, steps - 1)
        return step % levels, (step // levels) * GROUP

    def weights(ref, l, b, reach):
        return {m: ref[m + reach, l, block(b), :] for m in range(-reach, reach + 1)}

    def front(step):
        l, t0 = place(step)
        slot = (step + 2) % 2
        for b in range(count // BLOCK):
            taps = weights(east_c, l, b, EDGE)
            north = weights(north_c, l, b, 3)
            for j in range(GROUP):
                x = padded[t0 + j, l, padded_block(b), :]
                inner = x + north[0] * x
                for m in (-3, -2, -1, 1, 2, 3):
                    inner = inner + north[m] * padded[t0 + j, l, padded_block(b, m), :]
                inners[slot, j, block(b), :] = inner
                near = {0: x}
                for k, shift in enumerate(NEAR):
                    near[shift] = shifted[k, t0 + j, l, block(b), :]
                middle[slot, j, padded_block(b), :] = x + moved_sum(east_parts(taps, near))

    def back(step):
        l, t0 = place(step)
        slot = (step + 2) % 2
        for b in range(count // BLOCK):
            taps = weights(east_c, l, b, EDGE)
            north = weights(north_c, l, b, 3)
            for j in range(GROUP):
                parts = east_parts(taps, near_cells(inners[slot, j, block(b), :]))
                total = 0.5 * padded[t0 + j, l, padded_block(b), :] + parts[0]
                for m in range(-3, 4):
                    total = total + north[m] * middle[slot, j, padded_block(b, m), :]
                partial[slot, 0, j, block(b), :] = total
                partial[slot, 1, j, block(b), :] = parts[-STEP]
                partial[slot, 2, j, block(b), :] = parts[STEP]

    def finish(step):
        l, t0 = place(step)
        slot = (step + 2) % 2
        for b in range(count // BLOCK):
            for j in range(GROUP):
                sums[t0 + j, l, block(b), :] = partial[slot, 0, j, block(b), :] + (
                    lanes(partial[slot, 1, j, block(b), :], STEP)
                    + lanes(partial[slot, 2, j, block(b), :], -STEP)
                )

    def step_of_three(step, carry):
        finish(step - 1)
        back(step)
        front(step + 1)
        return carry

    lax.fori_loop(-1, steps + 1, step_of_three, 0)


def inner_update(mine, other, padded, shifted):
    tracers, levels, count, width = shifted.shape[1:]
    vmem = pl.BlockSpec(memory_space=pltpu.VMEM)
    level = (levels, count, width)
    return pl.pallas_call(
        inner_kernel,
        out_shape=(
            pltpu.VMEM((tracers,) + level, jnp.float32),
            pltpu.VMEM((2 * EDGE + 1,) + level, jnp.float32),
            pltpu.VMEM((7,) + level, jnp.float32),
            pltpu.VMEM(level, jnp.float32),
        ),
        in_specs=[vmem] * 4,
        out_specs=(vmem,) * 4,
        scratch_shapes=[
            pltpu.VMEM((2 * EDGE + 1,) + level, jnp.float32),
            pltpu.VMEM((7,) + level, jnp.float32),
            pltpu.VMEM((2, GROUP, count, width), jnp.float32),
            pltpu.VMEM((2, GROUP, count + 2 * PAD, width), jnp.float32),
            pltpu.VMEM((2, 3, GROUP, count, width), jnp.float32),
        ],
        compiler_params=pltpu.CompilerParams(vmem_limit_bytes=24 * 1024 * 1024),
        cost_estimate=pl.CostEstimate(flops=20000000, bytes_accessed=6000000, transcendentals=0),
        name="inner",
    )(mine, other, padded, shifted)


def edge_kernel(west, east, wrapped, own, sums, outer_c, edge_c, thickness, out, stage, sems):
    tracers, levels, count, width = sums.shape
    shape = (count, width)
    lane = lane_index(shape)
    segment, in_segment, packed_lane = segments(shape)
    from_west_lane = in_segment < EDGE
    at_edge = (lane < EDGE) | (lane >= width - EDGE)
    last_face = {
        shift: q == EDGE - 1
        for shift, q in moved_places(jnp.where(packed_lane, in_segment, -2 * SEG)).items()
    }
    base = levels * count

    def unfolded(x):
        return jnp.concatenate([x, lanes(x, -MET_SEG * levels)])

    met_east = unfolded(east[base:, :] + wrapped[base:, :])
    met_west = unfolded(west[base:, :])

    def copy(l):
        return pltpu.make_async_copy(stage.at[:, l], out.at[:, l], sems.at[l])

    def level(l, carry):
        level_rows = pl.ds(pl.multiple_of(l * count, count), count)
        met_lane = jnp.where(packed_lane, in_segment + MET_SEG * l, 0)
        met = jnp.where(lane - MET_SEG * l < EDGE, met_west, met_east)
        beyond = east_taps(
            pick(met_east, jnp.full(shape, SEG, jnp.int32) + MET_SEG * l),
            pick(met_east, jnp.full(shape, SEG + 1, jnp.int32) + MET_SEG * l),
        )
        mass_flux = pick(met_east, jnp.full(shape, SEG + 2, jnp.int32) + MET_SEG * l)
        inverse = 2.0 / (thickness[l] - jnp.where(lane == width - 1, mass_flux, 0.0))
        face = {
            m: jnp.where(last_face[east_group(m)], -beyond[m - 1], 0.0)
            for m in range(1 - EDGE, EDGE + 1)
        }
        outer = {m: outer_c[m + EDGE, l] for m in range(-EDGE, EDGE + 1) if m != 0}
        for m in range(1, EDGE + 1):
            outer[m] = outer[m] + face[m]
        inside = {m: face[m] for m in range(1 - EDGE, 1)}
        edge_taps = [edge_c[m, l] for m in range(7)]
        packed_taps = north_coefficients(pick(met, met_lane))
        for half in range(2):
            first_lane = EDGE * (segment + PACK * half) + in_segment
            west_index = jnp.where(packed_lane & from_west_lane, first_lane, 0)
            east_index = jnp.where(packed_lane & ~from_west_lane, first_lane - EDGE, 0)
            own_cells = pick(own[level_rows, :], west_index)
            cells = jnp.where(
                from_west_lane,
                pick(west[level_rows, :], west_index),
                pick(east[level_rows, :] + wrapped[level_rows, :], east_index),
            )
            inner = cells
            own_inner = own_cells
            for m in range(-3, 4):
                inner = inner + packed_taps[m + 3] * rows(cells, -m)
                own_inner = own_inner + edge_taps[m + 3] * rows(own_cells, -m)
            first = moved_sum(
                east_parts(inside, near_cells(own_cells), east_parts(outer, near_cells(cells)))
            )
            total = moved_sum(
                east_parts(inside, near_cells(own_inner), east_parts(outer, near_cells(inner)))
            )
            for m in range(-3, 4):
                total = total + edge_taps[m + 3] * rows(first, -m)
            for k in range(PACK):
                t = half * PACK + k
                moved = jnp.where(at_edge, lanes(total, width - EDGE - SEG * k), 0.0)
                stage[t, l] = (sums[t, l] + moved) * inverse
        copy(l).start()
        return carry

    lax.fori_loop(0, levels, level, 0)
    for l in range(levels):
        copy(l).wait()


def edge_update(west, east, wrapped, own, sums, outer_c, edge_c, thickness):
    tracers, levels, count, width = sums.shape
    vmem = pl.BlockSpec(memory_space=pltpu.VMEM)
    return pl.pallas_call(
        edge_kernel,
        out_shape=jax.ShapeDtypeStruct(sums.shape, jnp.float32),
        in_specs=[vmem] * 8,
        out_specs=pl.BlockSpec(memory_space=pl.ANY),
        scratch_shapes=[pltpu.VMEM(sums.shape, jnp.float32), pltpu.SemaphoreType.DMA((levels,))],
        compiler_params=pltpu.CompilerParams(vmem_limit_bytes=24 * 1024 * 1024),
        name="edges",
    )(west, east, wrapped, own, sums, outer_c, edge_c, thickness)


def east_group(m):
    return -STEP if m < -1 else (STEP if m > 2 else 0)


def along(x, pairs):
    return lax.ppermute(x, "space", pairs)


def exchange(x, flip):
    size = lax.axis_size("tracer")
    return lax.ppermute(x, "tracer", [(i, i ^ flip) for i in range(size)])


def turn(x, by):
    size = lax.axis_size("tracer")
    return lax.ppermute(x, "tracer", [(i, i // 8 * 8 + (i + 2 * by) % 8) for i in range(size)])


def shards(mass, thick, fe, fn, ce, cn, ne, owner):
    keep, send = prepare(thick, fe, fn, ce, cn, ne)
    last, first, padded, shifted = pack(mass)
    me, chosen = position(), owner[0]
    other_core = exchange(send, 1)
    total = jnp.where(chosen == me, keep, jnp.where(chosen == me ^ 1, other_core, 0.0))
    total = total + (turn(total, 1) + turn(total, -1) + turn(total, 2))
    total = total + exchange(total, 8)
    main = 2 * mass.shape[1] * mass.shape[2]
    mine = total[:main]
    edges = total[main:]
    size = lax.axis_size("space")
    to_east = jnp.concatenate([last, edges])
    to_west = jnp.concatenate([first, edges])
    west = along(to_east, [(i, (i + 1) % size) for i in range(size)])
    other = exchange(mine, 1)
    east = along(to_west, [(i, i - 1) for i in range(1, size)])
    inner = inner_update(mine, other, padded, shifted)
    to_west, inner = lax.optimization_barrier((to_west, inner))
    wrapped = along(to_west, [(0, size - 1)])
    return edge_update(west, east, wrapped, last, *inner)


def solution(mesh):
    spec = P("tracer", None, None, "space")
    return jax.shard_map(
        shards, mesh=mesh, in_specs=(spec,) * 7 + (P("space"),), out_specs=spec, check_vma=False
    )
```

```python
import functools

import jax
import jax.numpy as jnp
from jax import lax
from jax.experimental import pallas as pl
from jax.experimental.pallas import tpu as pltpu
from jax.sharding import PartitionSpec as P

NS = 2
EDGE = NS + 3
SEG = 2 * EDGE
PACK = 9
STEP = 4
GROUP = 3
PAD = 8
BLOCK = 8
NEAR = (-1, 1, 2)
MET_SEG = 16


def lane_index(shape):
    return lax.broadcasted_iota(jnp.int32, shape, len(shape) - 1)


def row_index(shape):
    return lax.broadcasted_iota(jnp.int32, shape, len(shape) - 2)


def lanes(x, shift):
    return pltpu.roll(x, shift % x.shape[-1], x.ndim - 1)


def rows(x, shift):
    return pltpu.roll(x, shift % x.shape[-2], x.ndim - 2)


def face_weights(courant):
    fraction = jnp.abs(courant)
    ramp = 1.5 * fraction * (1.0 - 2.0 / 3.0 * fraction)
    near = 0.5 * courant * (1.0 - 0.5 * fraction - ramp)
    far = 0.5 * courant * (0.5 * fraction - ramp)
    mean = courant * ramp
    far_outer = far * (1.0 / 12.0)
    near_outer = near * (1.0 / 12.0)
    return (
        -near_outer,
        7.0 * near_outer - far_outer,
        7.0 * (near_outer + far_outer) + mean,
        7.0 * far_outer - near_outer,
        -far_outer,
    )


def north_taps(courant):
    down1, up0, up1, up2, up3 = (w for w in face_weights(courant))
    forward = courant >= 0.0
    zero = jnp.zeros_like(courant)
    f = {1: down1, 0: up0, -1: up1, -2: up2, -3: up3}
    b = {-2: down1, -1: up0, 0: up1, 1: up2, 2: up3}
    return {m: jnp.where(forward, f.get(m, zero), b.get(m, zero)) for m in range(-3, 3)}


def east_taps(courant, whole):
    weights = face_weights(courant)
    forward = courant >= 0.0
    zero = jnp.zeros_like(courant)
    one = whole == 1.0
    two = whole == 2.0
    some = whole > 0.5
    taps = {}
    for m in range(-EDGE, EDGE):
        ahead = []
        behind = []
        for n in range(NS + 1):
            place = 1 - n - m
            ahead.append(weights[place] if 0 <= place < 5 else zero)
            place = m + 2 - n
            behind.append(weights[place] if 0 <= place < 5 else zero)
        f = jnp.where(two, ahead[2], jnp.where(one, ahead[1], ahead[0]))
        b = jnp.where(two, behind[2], jnp.where(one, behind[1], behind[0]))
        if m == -1:
            f = f + jnp.where(some, 0.5, 0.0)
        if m == -2:
            f = f + jnp.where(two, 0.5, 0.0)
        if m == 0:
            b = b - jnp.where(some, 0.5, 0.0)
        if m == 1:
            b = b - jnp.where(two, 0.5, 0.0)
        taps[m] = jnp.where(forward, f, b)
    return taps


def difference_taps(here, ahead, reach):
    out = {}
    for m in range(-reach, reach + 1):
        if m in here and m - 1 in ahead:
            out[m] = here[m] - ahead[m - 1]
        elif m in here:
            out[m] = here[m]
        else:
            out[m] = -ahead[m - 1]
    return out


def north_coefficients(courant):
    count = courant.shape[0]
    row = row_index(courant.shape)
    here = north_taps(jnp.where(row == 0, 0.0, courant))
    taps = difference_taps(here, {m: rows(here[m], -1) for m in here}, 3)
    return [
        jnp.where((row + m >= 0) & (row + m < count), taps[m], 0.0) for m in range(-3, 4)
    ]


def pick(x, index):
    return jnp.take_along_axis(x, index, axis=1, mode="promise_in_bounds")


def position():
    return lax.axis_index("tracer")


def tile():
    return lax.axis_index("space")


def prepare_kernel(*refs):
    sources, (keep, send, *fields, sems) = refs[:6], refs[6:]
    copies = [
        pltpu.make_async_copy(source, place, sems.at[k])
        for k, (source, place) in enumerate(zip(sources, fields))
    ]
    for copy in copies:
        copy.start()
    for copy in copies:
        copy.wait()
    thick, fe, fn, ce, cn, ne = fields
    core = position() % 2
    levels, count, width = thick.shape[1:]
    lane = lane_index((count, width))
    row = row_index((count, width))
    edge_rows = jnp.zeros((count, width), jnp.float32)
    for l in range(levels):
        east_mass = fe[0, l]
        north_mass = jnp.where(row == 0, 0.0, fn[0, l])
        thickness = (
            thick[0, l]
            + (east_mass - jnp.where(lane == width - 1, 0.0, lanes(east_mass, -1)))
            + (north_mass - rows(north_mass, -1))
        )
        whole = ne[0, l].astype(jnp.float32)
        first = (thickness, ce[0, l])
        second = (cn[0, l], whole)
        for k in range(2):
            start = (k * levels + l) * count
            keep[start : start + count, :] = jnp.where(core == 0, first[k], second[k])
            send[start : start + count, :] = jnp.where(core == 0, second[k], first[k])
        edges = jnp.where(lane < SEG, lanes(cn[0, l], EDGE), 0.0)
        for k, value in enumerate((ce[0, l], whole, east_mass)):
            edges = jnp.where(lane == SEG + k, lanes(value, SEG + k), edges)
        edge_rows = edge_rows + lanes(jnp.where(lane < MET_SEG, edges, 0.0), MET_SEG * l)
    base = 2 * levels * count
    folded = edge_rows[: count // 2] + lanes(edge_rows[count // 2 :], MET_SEG * levels)
    keep[base:, :] = folded
    send[base:, :] = folded


def prepare(thick, fe, fn, ce, cn, ne):
    levels, count, width = thick.shape[1:]
    vmem = pl.BlockSpec(memory_space=pltpu.VMEM)
    half = pltpu.VMEM((2 * levels * count + count // 2, width), jnp.float32)
    return pl.pallas_call(
        prepare_kernel,
        out_shape=(half, half),
        in_specs=[pl.BlockSpec(memory_space=pl.ANY)] * 6,
        out_specs=(vmem, vmem),
        scratch_shapes=[pltpu.VMEM(thick.shape, jnp.float32)] * 5
        + [pltpu.VMEM(ne.shape, jnp.int32), pltpu.SemaphoreType.DMA((6,))],
        name="prepare",
    )(thick, fe, fn, ce, cn, ne)


def pack_kernel(mass, last, first, padded, moved):
    tracers, levels, count, width = mass.shape
    lane = lane_index((count, width))
    zero_rows = jnp.zeros((PAD, width), jnp.float32)

    def level(l, carry):
        a = jnp.zeros((count, width), jnp.float32)
        b = a
        for t in range(tracers):
            value = mass[t, l]
            inside = (lane >= EDGE * t) & (lane < EDGE * (t + 1))
            a = jnp.where(inside, lanes(value, EDGE * (t + 1)), a)
            b = jnp.where(inside, lanes(value, EDGE * t), b)
            padded[t, l, :PAD, :] = zero_rows
            padded[t, l, PAD : PAD + count, :] = value
            padded[t, l, PAD + count :, :] = zero_rows
            for k, shift in enumerate(NEAR):
                moved[k, t, l] = lanes(value, -shift)
        last[l] = a
        first[l] = b
        return carry

    lax.fori_loop(0, levels, level, 0)


def pack(mass):
    tracers, levels, count, width = mass.shape
    vmem = pl.BlockSpec(memory_space=pltpu.VMEM)
    packed = pltpu.VMEM((levels, count, width), jnp.float32)
    last, first, padded, moved = pl.pallas_call(
        pack_kernel,
        out_shape=(
            packed,
            packed,
            pltpu.VMEM((tracers, levels, count + 2 * PAD, width), jnp.float32),
            pltpu.VMEM((len(NEAR),) + mass.shape, jnp.float32),
        ),
        in_specs=[vmem],
        out_specs=(vmem,) * 4,
        compiler_params=pltpu.CompilerParams(vmem_limit_bytes=24 * 1024 * 1024),
        cost_estimate=pl.CostEstimate(flops=2000000, bytes_accessed=1000000, transcendentals=0),
        name="pack",
    )(mass)
    rows_flat = (levels * count, width)
    return last.reshape(rows_flat), first.reshape(rows_flat), padded, moved


def segments(shape):
    lane = lane_index(shape)
    segment = sum(
        ((lane >= SEG * k).astype(jnp.int32) for k in range(1, PACK)), jnp.zeros(shape, jnp.int32)
    )
    return segment, lane - SEG * segment, lane < SEG * PACK


def moved_places(held):
    return {shift: lanes(held, shift) if shift else held for shift in (-STEP, 0, STEP)}


def east_parts(taps, near, parts=None):
    parts = dict(parts or {})
    for m in taps:
        shift = east_group(m)
        term = taps[m] * near[m - shift]
        parts[shift] = parts[shift] + term if shift in parts else term
    return parts


def moved_sum(parts):
    return parts[0] + (lanes(parts[-STEP], STEP) + lanes(parts[STEP], -STEP))


def near_cells(x):
    return {0: x, **{shift: lanes(x, -shift) for shift in NEAR}}


def inner_kernel(tiles, mine, other, padded, shifted, *refs):
    @pl.when(tiles(tile()))
    def _():
        inner_body(mine, other, padded, shifted, *refs)


def inner_body(
    mine, other, padded, shifted, sums, outer_c, edge_c, thickness,
    east_c, north_c, inners, middle, partial,
):
    tracers, levels, count, width = sums.shape
    shape = (count, width)
    lane = lane_index(shape)
    low = position() % 2 == 0
    _, in_segment, packed_lane = segments(shape)
    zero_rows = jnp.zeros((PAD, width), jnp.float32)
    for slot in range(2):
        for j in range(GROUP):
            middle[slot, j, :PAD, :] = zero_rows
            middle[slot, j, PAD + count :, :] = zero_rows
    edge_index = jnp.where(packed_lane, in_segment + (width - EDGE), 0)
    edge_index = jnp.where(edge_index >= width, edge_index - width, edge_index)
    moved_index = moved_places(edge_index)
    moved_segment = moved_places(jnp.where(packed_lane, in_segment, -2 * SEG))

    def level(l, carry):
        fields = []
        for half in range(2):
            for k in range(2):
                place = pl.ds(pl.multiple_of((k * levels + l) * count, count), count)
                a = mine[place, :]
                b = other[place, :]
                fields.append(jnp.where(low, a, b) if half == 0 else jnp.where(low, b, a))
        thick, east_courant, north_courant, whole = fields
        thickness[l] = thick
        here = east_taps(east_courant, whole)
        ahead = {m: jnp.where(lane == width - 1, 0.0, lanes(here[m], -1)) for m in here}
        taps = difference_taps(here, ahead, EDGE)
        for m in range(-EDGE, EDGE + 1):
            value = taps[m]
            if m != 0:
                q = moved_segment[east_group(m)]
                crosses = ((q < EDGE) != (q + m < EDGE)) & (q >= 0)
                outer_c[m + EDGE, l] = jnp.where(crosses, pick(value, moved_index[east_group(m)]), 0.0)
            if m < 0:
                value = jnp.where(lane >= -m, value, 0.0)
            if m > 0:
                value = jnp.where(lane < width - m, value, 0.0)
            shift = east_group(m)
            east_c[m + EDGE, l] = lanes(value, shift) if shift else value
        for m, value in enumerate(north_coefficients(north_courant)):
            north_c[m, l] = value
        for m, value in enumerate(north_coefficients(pick(north_courant, edge_index))):
            edge_c[m, l] = value
        return carry

    lax.fori_loop(0, levels, level, 0)
    steps = levels * (tracers // GROUP)

    def block(b):
        return slice(b * BLOCK, (b + 1) * BLOCK)

    def padded_block(b, m=0):
        return slice(PAD + b * BLOCK + m, PAD + (b + 1) * BLOCK + m)

    def place(step):
        step = jnp.clip(step, 0, steps - 1)
        return step % levels, (step // levels) * GROUP

    def weights(ref, l, b, reach):
        return {m: ref[m + reach, l, block(b), :] for m in range(-reach, reach + 1)}

    def front(step):
        l, t0 = place(step)
        slot = (step + 2) % 2
        for b in range(count // BLOCK):
            taps = weights(east_c, l, b, EDGE)
            north = weights(north_c, l, b, 3)
            for j in range(GROUP):
                x = padded[t0 + j, l, padded_block(b), :]
                inner = x + north[0] * x
                for m in (-3, -2, -1, 1, 2, 3):
                    inner = inner + north[m] * padded[t0 + j, l, padded_block(b, m), :]
                inners[slot, j, block(b), :] = inner
                near = {0: x}
                for k, shift in enumerate(NEAR):
                    near[shift] = shifted[k, t0 + j, l, block(b), :]
                middle[slot, j, padded_block(b), :] = x + moved_sum(east_parts(taps, near))

    def back(step):
        l, t0 = place(step)
        slot = (step + 2) % 2
        for b in range(count // BLOCK):
            taps = weights(east_c, l, b, EDGE)
            north = weights(north_c, l, b, 3)
            for j in range(GROUP):
                parts = east_parts(taps, near_cells(inners[slot, j, block(b), :]))
                total = 0.5 * padded[t0 + j, l, padded_block(b), :] + parts[0]
                for m in range(-3, 4):
                    total = total + north[m] * middle[slot, j, padded_block(b, m), :]
                partial[slot, 0, j, block(b), :] = total
                partial[slot, 1, j, block(b), :] = parts[-STEP]
                partial[slot, 2, j, block(b), :] = parts[STEP]

    def finish(step):
        l, t0 = place(step)
        slot = (step + 2) % 2
        for b in range(count // BLOCK):
            for j in range(GROUP):
                sums[t0 + j, l, block(b), :] = partial[slot, 0, j, block(b), :] + (
                    lanes(partial[slot, 1, j, block(b), :], STEP)
                    + lanes(partial[slot, 2, j, block(b), :], -STEP)
                )

    def step_of_three(step, carry):
        finish(step - 1)
        back(step)
        front(step + 1)
        return carry

    lax.fori_loop(-1, steps + 1, step_of_three, 0)


def inner_update(tiles, mine, other, padded, shifted):
    tracers, levels, count, width = shifted.shape[1:]
    vmem = pl.BlockSpec(memory_space=pltpu.VMEM)
    level = (levels, count, width)
    return pl.pallas_call(
        functools.partial(inner_kernel, tiles),
        out_shape=(
            pltpu.VMEM((tracers,) + level, jnp.float32),
            pltpu.VMEM((2 * EDGE + 1,) + level, jnp.float32),
            pltpu.VMEM((7,) + level, jnp.float32),
            pltpu.VMEM(level, jnp.float32),
        ),
        in_specs=[vmem] * 4,
        out_specs=(vmem,) * 4,
        scratch_shapes=[
            pltpu.VMEM((2 * EDGE + 1,) + level, jnp.float32),
            pltpu.VMEM((7,) + level, jnp.float32),
            pltpu.VMEM((2, GROUP, count, width), jnp.float32),
            pltpu.VMEM((2, GROUP, count + 2 * PAD, width), jnp.float32),
            pltpu.VMEM((2, 3, GROUP, count, width), jnp.float32),
        ],
        compiler_params=pltpu.CompilerParams(vmem_limit_bytes=24 * 1024 * 1024),
        cost_estimate=pl.CostEstimate(flops=20000000, bytes_accessed=6000000, transcendentals=0),
        name="inner",
    )(mine, other, padded, shifted)


def edge_kernel(early, west, east, own, *refs):
    before, after, rest = refs[:4], refs[4:8], refs[8:]

    @pl.when(early(tile()))
    def _():
        edge_body(west, east, own, *before, *rest)

    @pl.when(jnp.logical_not(early(tile())))
    def _():
        edge_body(west, east, own, *after, *rest)


def edge_body(west, east, own, sums, outer_c, edge_c, thickness, out, stage, sems):
    tracers, levels, count, width = sums.shape
    shape = (count, width)
    lane = lane_index(shape)
    segment, in_segment, packed_lane = segments(shape)
    from_west_lane = in_segment < EDGE
    at_edge = (lane < EDGE) | (lane >= width - EDGE)
    last_face = {
        shift: q == EDGE - 1
        for shift, q in moved_places(jnp.where(packed_lane, in_segment, -2 * SEG)).items()
    }
    base = levels * count

    def unfolded(x):
        return jnp.concatenate([x, lanes(x, -MET_SEG * levels)])

    met_east = unfolded(east[base:, :])
    met_west = unfolded(west[base:, :])

    def copy(l):
        return pltpu.make_async_copy(stage.at[:, l], out.at[:, l], sems.at[l])

    def level(l, carry):
        level_rows = pl.ds(pl.multiple_of(l * count, count), count)
        met_lane = jnp.where(packed_lane, in_segment + MET_SEG * l, 0)
        met = jnp.where(lane - MET_SEG * l < EDGE, met_west, met_east)
        beyond = east_taps(
            pick(met_east, jnp.full(shape, SEG, jnp.int32) + MET_SEG * l),
            pick(met_east, jnp.full(shape, SEG + 1, jnp.int32) + MET_SEG * l),
        )
        mass_flux = pick(met_east, jnp.full(shape, SEG + 2, jnp.int32) + MET_SEG * l)
        inverse = 2.0 / (thickness[l] - jnp.where(lane == width - 1, mass_flux, 0.0))
        face = {
            m: jnp.where(last_face[east_group(m)], -beyond[m - 1], 0.0)
            for m in range(1 - EDGE, EDGE + 1)
        }
        outer = {m: outer_c[m + EDGE, l] for m in range(-EDGE, EDGE + 1) if m != 0}
        for m in range(1, EDGE + 1):
            outer[m] = outer[m] + face[m]
        inside = {m: face[m] for m in range(1 - EDGE, 1)}
        edge_taps = [edge_c[m, l] for m in range(7)]
        packed_taps = north_coefficients(pick(met, met_lane))
        for half in range(2):
            first_lane = EDGE * (segment + PACK * half) + in_segment
            west_index = jnp.where(packed_lane & from_west_lane, first_lane, 0)
            east_index = jnp.where(packed_lane & ~from_west_lane, first_lane - EDGE, 0)
            own_cells = pick(own[level_rows, :], west_index)
            cells = jnp.where(
                from_west_lane,
                pick(west[level_rows, :], west_index),
                pick(east[level_rows, :], east_index),
            )
            inner = cells
            own_inner = own_cells
            for m in range(-3, 4):
                inner = inner + packed_taps[m + 3] * rows(cells, -m)
                own_inner = own_inner + edge_taps[m + 3] * rows(own_cells, -m)
            first = moved_sum(
                east_parts(inside, near_cells(own_cells), east_parts(outer, near_cells(cells)))
            )
            total = moved_sum(
                east_parts(inside, near_cells(own_inner), east_parts(outer, near_cells(inner)))
            )
            for m in range(-3, 4):
                total = total + edge_taps[m + 3] * rows(first, -m)
            for k in range(PACK):
                t = half * PACK + k
                moved = jnp.where(at_edge, lanes(total, width - EDGE - SEG * k), 0.0)
                stage[t, l] = (sums[t, l] + moved) * inverse
        copy(l).start()
        return carry

    lax.fori_loop(0, levels, level, 0)
    for l in range(levels):
        copy(l).wait()


def edge_update(early, west, east, own, before, after):
    sums = before[0]
    tracers, levels, count, width = sums.shape
    vmem = pl.BlockSpec(memory_space=pltpu.VMEM)
    return pl.pallas_call(
        functools.partial(edge_kernel, early),
        out_shape=jax.ShapeDtypeStruct(sums.shape, jnp.float32),
        in_specs=[vmem] * 11,
        out_specs=pl.BlockSpec(memory_space=pl.ANY),
        scratch_shapes=[pltpu.VMEM(sums.shape, jnp.float32), pltpu.SemaphoreType.DMA((levels,))],
        compiler_params=pltpu.CompilerParams(vmem_limit_bytes=24 * 1024 * 1024),
        name="edges",
    )(west, east, own, *before, *after)


def east_group(m):
    return -STEP if m < -1 else (STEP if m > 2 else 0)


def along(x, pairs):
    return lax.ppermute(x, "space", pairs)


def exchange(x, flip):
    size = lax.axis_size("tracer")
    return lax.ppermute(x, "tracer", [(i, i ^ flip) for i in range(size)])


def turn(x, by):
    size = lax.axis_size("tracer")
    return lax.ppermute(x, "tracer", [(i, i // 8 * 8 + (i + 2 * by) % 8) for i in range(size)])


def early(i):
    return i == 0


def shards(mass, thick, fe, fn, ce, cn, ne, owner):
    keep, send = prepare(thick, fe, fn, ce, cn, ne)
    last, first, padded, shifted = pack(mass)
    me, chosen = position(), owner[0]
    other_core = exchange(send, 1)
    total = jnp.where(chosen == me, keep, jnp.where(chosen == me ^ 1, other_core, 0.0))
    total = total + (turn(total, 1) + turn(total, -1) + turn(total, 2))
    total = total + exchange(total, 8)
    main = 2 * mass.shape[1] * mass.shape[2]
    mine = total[:main]
    edges = total[main:]
    size = lax.axis_size("space")
    to_east = jnp.concatenate([last, edges])
    to_west = jnp.concatenate([first, edges])
    west = along(to_east, [(i, (i + 1) % size) for i in range(size)])
    other = exchange(mine, 1)
    before = inner_update(early, mine, other, padded, shifted)
    to_west, before = lax.optimization_barrier((to_west, before))
    east = along(to_west, [(i, (i - 1) % size) for i in range(size)])
    after = inner_update(lambda i: jnp.logical_not(early(i)), mine, other, padded, shifted)
    return edge_update(early, west, east, last, before, after)


def solution(mesh):
    spec = P("tracer", None, None, "space")
    return jax.shard_map(
        shards, mesh=mesh, in_specs=(spec,) * 7 + (P("space"),), out_specs=spec, check_vma=False
    )
```

```python
import functools

import jax
import jax.numpy as jnp
from jax import lax
from jax.experimental import pallas as pl
from jax.experimental.pallas import tpu as pltpu
from jax.sharding import PartitionSpec as P

NS = 2
EDGE = NS + 3
SEG = 2 * EDGE
PACK = 9
STEP = 4
GROUP = 3
PAD = 8
BLOCK = 8
NEAR = (-1, 1, 2)
MET_SEG = 16


def lane_index(shape):
    return lax.broadcasted_iota(jnp.int32, shape, len(shape) - 1)


def row_index(shape):
    return lax.broadcasted_iota(jnp.int32, shape, len(shape) - 2)


def lanes(x, shift):
    return pltpu.roll(x, shift % x.shape[-1], x.ndim - 1)


def rows(x, shift):
    return pltpu.roll(x, shift % x.shape[-2], x.ndim - 2)


def face_weights(courant):
    fraction = jnp.abs(courant)
    ramp = 1.5 * fraction * (1.0 - 2.0 / 3.0 * fraction)
    near = 0.5 * courant * (1.0 - 0.5 * fraction - ramp)
    far = 0.5 * courant * (0.5 * fraction - ramp)
    mean = courant * ramp
    far_outer = far * (1.0 / 12.0)
    near_outer = near * (1.0 / 12.0)
    return (
        -near_outer,
        7.0 * near_outer - far_outer,
        7.0 * (near_outer + far_outer) + mean,
        7.0 * far_outer - near_outer,
        -far_outer,
    )


def north_taps(courant):
    down1, up0, up1, up2, up3 = (w for w in face_weights(courant))
    forward = courant >= 0.0
    zero = jnp.zeros_like(courant)
    f = {1: down1, 0: up0, -1: up1, -2: up2, -3: up3}
    b = {-2: down1, -1: up0, 0: up1, 1: up2, 2: up3}
    return {m: jnp.where(forward, f.get(m, zero), b.get(m, zero)) for m in range(-3, 3)}


def east_taps(courant, whole):
    weights = face_weights(courant)
    forward = courant >= 0.0
    zero = jnp.zeros_like(courant)
    one = whole == 1.0
    two = whole == 2.0
    some = whole > 0.5
    taps = {}
    for m in range(-EDGE, EDGE):
        ahead = []
        behind = []
        for n in range(NS + 1):
            place = 1 - n - m
            ahead.append(weights[place] if 0 <= place < 5 else zero)
            place = m + 2 - n
            behind.append(weights[place] if 0 <= place < 5 else zero)
        f = jnp.where(two, ahead[2], jnp.where(one, ahead[1], ahead[0]))
        b = jnp.where(two, behind[2], jnp.where(one, behind[1], behind[0]))
        if m == -1:
            f = f + jnp.where(some, 0.5, 0.0)
        if m == -2:
            f = f + jnp.where(two, 0.5, 0.0)
        if m == 0:
            b = b - jnp.where(some, 0.5, 0.0)
        if m == 1:
            b = b - jnp.where(two, 0.5, 0.0)
        taps[m] = jnp.where(forward, f, b)
    return taps


def difference_taps(here, ahead, reach):
    out = {}
    for m in range(-reach, reach + 1):
        if m in here and m - 1 in ahead:
            out[m] = here[m] - ahead[m - 1]
        elif m in here:
            out[m] = here[m]
        else:
            out[m] = -ahead[m - 1]
    return out


def north_coefficients(courant):
    count = courant.shape[0]
    row = row_index(courant.shape)
    here = north_taps(jnp.where(row == 0, 0.0, courant))
    taps = difference_taps(here, {m: rows(here[m], -1) for m in here}, 3)
    return [
        jnp.where((row + m >= 0) & (row + m < count), taps[m], 0.0) for m in range(-3, 4)
    ]


def pick(x, index):
    return jnp.take_along_axis(x, index, axis=1, mode="promise_in_bounds")


def position():
    return lax.axis_index("tracer")


def tile():
    return lax.axis_index("space")


def early_levels(levels):
    return jnp.clip(levels - tile(), 0, levels - 1)


def prepare_kernel(*refs):
    sources, (keep, send, *fields, sems) = refs[:6], refs[6:]
    copies = [
        pltpu.make_async_copy(source, place, sems.at[k])
        for k, (source, place) in enumerate(zip(sources, fields))
    ]
    for copy in copies:
        copy.start()
    for copy in copies:
        copy.wait()
    thick, fe, fn, ce, cn, ne = fields
    core = position() % 2
    levels, count, width = thick.shape[1:]
    lane = lane_index((count, width))
    row = row_index((count, width))
    edge_rows = jnp.zeros((count, width), jnp.float32)
    for l in range(levels):
        east_mass = fe[0, l]
        north_mass = jnp.where(row == 0, 0.0, fn[0, l])
        thickness = (
            thick[0, l]
            + (east_mass - jnp.where(lane == width - 1, 0.0, lanes(east_mass, -1)))
            + (north_mass - rows(north_mass, -1))
        )
        whole = ne[0, l].astype(jnp.float32)
        first = (thickness, ce[0, l])
        second = (cn[0, l], whole)
        for k in range(2):
            start = (k * levels + l) * count
            keep[start : start + count, :] = jnp.where(core == 0, first[k], second[k])
            send[start : start + count, :] = jnp.where(core == 0, second[k], first[k])
        edges = jnp.where(lane < SEG, lanes(cn[0, l], EDGE), 0.0)
        for k, value in enumerate((ce[0, l], whole, east_mass)):
            edges = jnp.where(lane == SEG + k, lanes(value, SEG + k), edges)
        edge_rows = edge_rows + lanes(jnp.where(lane < MET_SEG, edges, 0.0), MET_SEG * l)
    base = 2 * levels * count
    folded = edge_rows[: count // 2] + lanes(edge_rows[count // 2 :], MET_SEG * levels)
    keep[base:, :] = folded
    send[base:, :] = folded


def prepare(thick, fe, fn, ce, cn, ne):
    levels, count, width = thick.shape[1:]
    vmem = pl.BlockSpec(memory_space=pltpu.VMEM)
    half = pltpu.VMEM((2 * levels * count + count // 2, width), jnp.float32)
    return pl.pallas_call(
        prepare_kernel,
        out_shape=(half, half),
        in_specs=[pl.BlockSpec(memory_space=pl.ANY)] * 6,
        out_specs=(vmem, vmem),
        scratch_shapes=[pltpu.VMEM(thick.shape, jnp.float32)] * 5
        + [pltpu.VMEM(ne.shape, jnp.int32), pltpu.SemaphoreType.DMA((6,))],
        name="prepare",
    )(thick, fe, fn, ce, cn, ne)


def pack_kernel(mass, last, first, padded, moved):
    tracers, levels, count, width = mass.shape
    lane = lane_index((count, width))
    zero_rows = jnp.zeros((PAD, width), jnp.float32)

    def level(l, carry):
        a = jnp.zeros((count, width), jnp.float32)
        b = a
        for t in range(tracers):
            value = mass[t, l]
            inside = (lane >= EDGE * t) & (lane < EDGE * (t + 1))
            a = jnp.where(inside, lanes(value, EDGE * (t + 1)), a)
            b = jnp.where(inside, lanes(value, EDGE * t), b)
            padded[t, l, :PAD, :] = zero_rows
            padded[t, l, PAD : PAD + count, :] = value
            padded[t, l, PAD + count :, :] = zero_rows
            for k, shift in enumerate(NEAR):
                moved[k, t, l] = lanes(value, -shift)
        last[l] = a
        first[l] = b
        return carry

    lax.fori_loop(0, levels, level, 0)


def pack(mass):
    tracers, levels, count, width = mass.shape
    vmem = pl.BlockSpec(memory_space=pltpu.VMEM)
    packed = pltpu.VMEM((levels, count, width), jnp.float32)
    last, first, padded, moved = pl.pallas_call(
        pack_kernel,
        out_shape=(
            packed,
            packed,
            pltpu.VMEM((tracers, levels, count + 2 * PAD, width), jnp.float32),
            pltpu.VMEM((len(NEAR),) + mass.shape, jnp.float32),
        ),
        in_specs=[vmem],
        out_specs=(vmem,) * 4,
        compiler_params=pltpu.CompilerParams(vmem_limit_bytes=24 * 1024 * 1024),
        cost_estimate=pl.CostEstimate(flops=2000000, bytes_accessed=1000000, transcendentals=0),
        name="pack",
    )(mass)
    rows_flat = (levels * count, width)
    return last.reshape(rows_flat), first.reshape(rows_flat), padded, moved


def segments(shape):
    lane = lane_index(shape)
    segment = sum(
        ((lane >= SEG * k).astype(jnp.int32) for k in range(1, PACK)), jnp.zeros(shape, jnp.int32)
    )
    return segment, lane - SEG * segment, lane < SEG * PACK


def moved_places(held):
    return {shift: lanes(held, shift) if shift else held for shift in (-STEP, 0, STEP)}


def east_parts(taps, near, parts=None):
    parts = dict(parts or {})
    for m in taps:
        shift = east_group(m)
        term = taps[m] * near[m - shift]
        parts[shift] = parts[shift] + term if shift in parts else term
    return parts


def moved_sum(parts):
    return parts[0] + (lanes(parts[-STEP], STEP) + lanes(parts[STEP], -STEP))


def near_cells(x):
    return {0: x, **{shift: lanes(x, -shift) for shift in NEAR}}


def inner_kernel(span, mine, other, padded, shifted, *refs):
    low_level, high_level = span(refs[0].shape[1])

    @pl.when(low_level < high_level)
    def _():
        inner_body(low_level, high_level, mine, other, padded, shifted, *refs)


def inner_body(
    low_level, high_level, mine, other, padded, shifted, sums, outer_c, edge_c, thickness,
    east_c, north_c, inners, middle, partial,
):
    tracers, levels, count, width = sums.shape
    shape = (count, width)
    lane = lane_index(shape)
    low = position() % 2 == 0
    _, in_segment, packed_lane = segments(shape)
    zero_rows = jnp.zeros((PAD, width), jnp.float32)
    for slot in range(2):
        for j in range(GROUP):
            middle[slot, j, :PAD, :] = zero_rows
            middle[slot, j, PAD + count :, :] = zero_rows
    edge_index = jnp.where(packed_lane, in_segment + (width - EDGE), 0)
    edge_index = jnp.where(edge_index >= width, edge_index - width, edge_index)
    moved_index = moved_places(edge_index)
    moved_segment = moved_places(jnp.where(packed_lane, in_segment, -2 * SEG))

    def level(l, carry):
        fields = []
        for half in range(2):
            for k in range(2):
                place = pl.ds(pl.multiple_of((k * levels + l) * count, count), count)
                a = mine[place, :]
                b = other[place, :]
                fields.append(jnp.where(low, a, b) if half == 0 else jnp.where(low, b, a))
        thick, east_courant, north_courant, whole = fields
        thickness[l] = thick
        here = east_taps(east_courant, whole)
        ahead = {m: jnp.where(lane == width - 1, 0.0, lanes(here[m], -1)) for m in here}
        taps = difference_taps(here, ahead, EDGE)
        for m in range(-EDGE, EDGE + 1):
            value = taps[m]
            if m != 0:
                q = moved_segment[east_group(m)]
                crosses = ((q < EDGE) != (q + m < EDGE)) & (q >= 0)
                outer_c[m + EDGE, l] = jnp.where(crosses, pick(value, moved_index[east_group(m)]), 0.0)
            if m < 0:
                value = jnp.where(lane >= -m, value, 0.0)
            if m > 0:
                value = jnp.where(lane < width - m, value, 0.0)
            shift = east_group(m)
            east_c[m + EDGE, l] = lanes(value, shift) if shift else value
        for m, value in enumerate(north_coefficients(north_courant)):
            north_c[m, l] = value
        for m, value in enumerate(north_coefficients(pick(north_courant, edge_index))):
            edge_c[m, l] = value
        return carry

    lax.fori_loop(low_level, high_level, level, 0)
    groups = tracers // GROUP

    def block(b):
        return slice(b * BLOCK, (b + 1) * BLOCK)

    def padded_block(b, m=0):
        return slice(PAD + b * BLOCK + m, PAD + (b + 1) * BLOCK + m)

    def place(step):
        step = jnp.clip(step, 0, levels * groups - 1)
        return step // groups, (step % groups) * GROUP

    def weights(ref, l, b, reach):
        return {m: ref[m + reach, l, block(b), :] for m in range(-reach, reach + 1)}

    def front(step):
        l, t0 = place(step)
        slot = (step + 2) % 2
        for b in range(count // BLOCK):
            taps = weights(east_c, l, b, EDGE)
            north = weights(north_c, l, b, 3)
            for j in range(GROUP):
                x = padded[t0 + j, l, padded_block(b), :]
                inner = x + north[0] * x
                for m in (-3, -2, -1, 1, 2, 3):
                    inner = inner + north[m] * padded[t0 + j, l, padded_block(b, m), :]
                inners[slot, j, block(b), :] = inner
                near = {0: x}
                for k, shift in enumerate(NEAR):
                    near[shift] = shifted[k, t0 + j, l, block(b), :]
                middle[slot, j, padded_block(b), :] = x + moved_sum(east_parts(taps, near))

    def back(step):
        l, t0 = place(step)
        slot = (step + 2) % 2
        for b in range(count // BLOCK):
            taps = weights(east_c, l, b, EDGE)
            north = weights(north_c, l, b, 3)
            for j in range(GROUP):
                parts = east_parts(taps, near_cells(inners[slot, j, block(b), :]))
                total = 0.5 * padded[t0 + j, l, padded_block(b), :] + parts[0]
                for m in range(-3, 4):
                    total = total + north[m] * middle[slot, j, padded_block(b, m), :]
                partial[slot, 0, j, block(b), :] = total
                partial[slot, 1, j, block(b), :] = parts[-STEP]
                partial[slot, 2, j, block(b), :] = parts[STEP]

    def finish(step):
        l, t0 = place(step)
        slot = (step + 2) % 2
        for b in range(count // BLOCK):
            for j in range(GROUP):
                sums[t0 + j, l, block(b), :] = partial[slot, 0, j, block(b), :] + (
                    lanes(partial[slot, 1, j, block(b), :], STEP)
                    + lanes(partial[slot, 2, j, block(b), :], -STEP)
                )

    def step_of_three(step, carry):
        finish(step - 1)
        back(step)
        front(step + 1)
        return carry

    lax.fori_loop(low_level * groups - 1, high_level * groups + 1, step_of_three, 0)


def inner_update(span, mine, other, padded, shifted):
    tracers, levels, count, width = shifted.shape[1:]
    vmem = pl.BlockSpec(memory_space=pltpu.VMEM)
    level = (levels, count, width)
    return pl.pallas_call(
        functools.partial(inner_kernel, span),
        out_shape=(
            pltpu.VMEM((tracers,) + level, jnp.float32),
            pltpu.VMEM((2 * EDGE + 1,) + level, jnp.float32),
            pltpu.VMEM((7,) + level, jnp.float32),
            pltpu.VMEM(level, jnp.float32),
        ),
        in_specs=[vmem] * 4,
        out_specs=(vmem,) * 4,
        scratch_shapes=[
            pltpu.VMEM((2 * EDGE + 1,) + level, jnp.float32),
            pltpu.VMEM((7,) + level, jnp.float32),
            pltpu.VMEM((2, GROUP, count, width), jnp.float32),
            pltpu.VMEM((2, GROUP, count + 2 * PAD, width), jnp.float32),
            pltpu.VMEM((2, 3, GROUP, count, width), jnp.float32),
        ],
        compiler_params=pltpu.CompilerParams(vmem_limit_bytes=24 * 1024 * 1024),
        cost_estimate=pl.CostEstimate(flops=20000000, bytes_accessed=6000000, transcendentals=0),
        name="inner",
    )(mine, other, padded, shifted)


def edge_kernel(west, east, own, *refs):
    before, after, (out, stage, sems) = refs[:4], refs[4:8], refs[8:]
    tracers, levels, count, width = stage.shape
    first_levels = early_levels(levels)
    shape = (count, width)
    lane = lane_index(shape)
    segment, in_segment, packed_lane = segments(shape)
    from_west_lane = in_segment < EDGE
    at_edge = (lane < EDGE) | (lane >= width - EDGE)
    last_face = {
        shift: q == EDGE - 1
        for shift, q in moved_places(jnp.where(packed_lane, in_segment, -2 * SEG)).items()
    }
    base = levels * count

    def unfolded(x):
        return jnp.concatenate([x, lanes(x, -MET_SEG * levels)])

    met_east = unfolded(east[base:, :])
    met_west = unfolded(west[base:, :])

    def copy(l):
        return pltpu.make_async_copy(stage.at[:, l], out.at[:, l], sems.at[l])

    def level(l, sums, outer_c, edge_c, thickness):
        level_rows = pl.ds(pl.multiple_of(l * count, count), count)
        met_lane = jnp.where(packed_lane, in_segment + MET_SEG * l, 0)
        met = jnp.where(lane - MET_SEG * l < EDGE, met_west, met_east)
        beyond = east_taps(
            pick(met_east, jnp.full(shape, SEG, jnp.int32) + MET_SEG * l),
            pick(met_east, jnp.full(shape, SEG + 1, jnp.int32) + MET_SEG * l),
        )
        mass_flux = pick(met_east, jnp.full(shape, SEG + 2, jnp.int32) + MET_SEG * l)
        inverse = 2.0 / (thickness[l] - jnp.where(lane == width - 1, mass_flux, 0.0))
        face = {
            m: jnp.where(last_face[east_group(m)], -beyond[m - 1], 0.0)
            for m in range(1 - EDGE, EDGE + 1)
        }
        outer = {m: outer_c[m + EDGE, l] for m in range(-EDGE, EDGE + 1) if m != 0}
        for m in range(1, EDGE + 1):
            outer[m] = outer[m] + face[m]
        inside = {m: face[m] for m in range(1 - EDGE, 1)}
        edge_taps = [edge_c[m, l] for m in range(7)]
        packed_taps = north_coefficients(pick(met, met_lane))
        for half in range(2):
            first_lane = EDGE * (segment + PACK * half) + in_segment
            west_index = jnp.where(packed_lane & from_west_lane, first_lane, 0)
            east_index = jnp.where(packed_lane & ~from_west_lane, first_lane - EDGE, 0)
            own_cells = pick(own[level_rows, :], west_index)
            cells = jnp.where(
                from_west_lane,
                pick(west[level_rows, :], west_index),
                pick(east[level_rows, :], east_index),
            )
            inner = cells
            own_inner = own_cells
            for m in range(-3, 4):
                inner = inner + packed_taps[m + 3] * rows(cells, -m)
                own_inner = own_inner + edge_taps[m + 3] * rows(own_cells, -m)
            first = moved_sum(
                east_parts(inside, near_cells(own_cells), east_parts(outer, near_cells(cells)))
            )
            total = moved_sum(
                east_parts(inside, near_cells(own_inner), east_parts(outer, near_cells(inner)))
            )
            for m in range(-3, 4):
                total = total + edge_taps[m + 3] * rows(first, -m)
            for k in range(PACK):
                t = half * PACK + k
                moved = jnp.where(at_edge, lanes(total, width - EDGE - SEG * k), 0.0)
                stage[t, l] = (sums[t, l] + moved) * inverse
        copy(l).start()

    def either(l, carry):
        @pl.when(l < first_levels)
        def _():
            level(l, *before)

        @pl.when(l >= first_levels)
        def _():
            level(l, *after)

        return carry

    lax.fori_loop(0, levels, either, 0)
    for l in range(levels):
        copy(l).wait()


def edge_update(west, east, own, before, after):
    sums = before[0]
    tracers, levels, count, width = sums.shape
    vmem = pl.BlockSpec(memory_space=pltpu.VMEM)
    return pl.pallas_call(
        edge_kernel,
        out_shape=jax.ShapeDtypeStruct(sums.shape, jnp.float32),
        in_specs=[vmem] * 11,
        out_specs=pl.BlockSpec(memory_space=pl.ANY),
        scratch_shapes=[pltpu.VMEM(sums.shape, jnp.float32), pltpu.SemaphoreType.DMA((levels,))],
        compiler_params=pltpu.CompilerParams(vmem_limit_bytes=24 * 1024 * 1024),
        name="edges",
    )(west, east, own, *before, *after)


def east_group(m):
    return -STEP if m < -1 else (STEP if m > 2 else 0)


def along(x, pairs):
    return lax.ppermute(x, "space", pairs)


def exchange(x, flip):
    size = lax.axis_size("tracer")
    return lax.ppermute(x, "tracer", [(i, i ^ flip) for i in range(size)])


def turn(x, by):
    size = lax.axis_size("tracer")
    return lax.ppermute(x, "tracer", [(i, i // 8 * 8 + (i + 2 * by) % 8) for i in range(size)])


def shards(mass, thick, fe, fn, ce, cn, ne, owner):
    keep, send = prepare(thick, fe, fn, ce, cn, ne)
    last, first, padded, shifted = pack(mass)
    me, chosen = position(), owner[0]
    other_core = exchange(send, 1)
    total = jnp.where(chosen == me, keep, jnp.where(chosen == me ^ 1, other_core, 0.0))
    total = total + (turn(total, 1) + turn(total, -1) + turn(total, 2))
    total = total + exchange(total, 8)
    main = 2 * mass.shape[1] * mass.shape[2]
    mine = total[:main]
    edges = total[main:]
    size = lax.axis_size("space")
    to_east = jnp.concatenate([last, edges])
    to_west = jnp.concatenate([first, edges])
    west = along(to_east, [(i, (i + 1) % size) for i in range(size)])
    other = exchange(mine, 1)
    before = inner_update(lambda levels: (0, early_levels(levels)), mine, other, padded, shifted)
    to_west, before = lax.optimization_barrier((to_west, before))
    east = along(to_west, [(i, (i - 1) % size) for i in range(size)])
    after = inner_update(lambda levels: (early_levels(levels), levels), mine, other, padded, shifted)
    return edge_update(west, east, last, before, after)


def solution(mesh):
    spec = P("tracer", None, None, "space")
    return jax.shard_map(
        shards, mesh=mesh, in_specs=(spec,) * 7 + (P("space"),), out_specs=spec, check_vma=False
    )
```

```python
import functools

import jax
import jax.numpy as jnp
from jax import lax
from jax.experimental import pallas as pl
from jax.experimental.pallas import tpu as pltpu
from jax.sharding import PartitionSpec as P

NS = 2
EDGE = NS + 3
SEG = 2 * EDGE
PACK = 9
STEP = 4
GROUP = 3
PAD = 8
BLOCK = 8
NEAR = (-1, 1, 2)
MET_SEG = 16


def lane_index(shape):
    return lax.broadcasted_iota(jnp.int32, shape, len(shape) - 1)


def row_index(shape):
    return lax.broadcasted_iota(jnp.int32, shape, len(shape) - 2)


def lanes(x, shift):
    return pltpu.roll(x, shift % x.shape[-1], x.ndim - 1)


def rows(x, shift):
    return pltpu.roll(x, shift % x.shape[-2], x.ndim - 2)


def face_weights(courant):
    fraction = jnp.abs(courant)
    ramp = 1.5 * fraction * (1.0 - 2.0 / 3.0 * fraction)
    near = 0.5 * courant * (1.0 - 0.5 * fraction - ramp)
    far = 0.5 * courant * (0.5 * fraction - ramp)
    mean = courant * ramp
    far_outer = far * (1.0 / 12.0)
    near_outer = near * (1.0 / 12.0)
    return (
        -near_outer,
        7.0 * near_outer - far_outer,
        7.0 * (near_outer + far_outer) + mean,
        7.0 * far_outer - near_outer,
        -far_outer,
    )


def north_taps(courant):
    down1, up0, up1, up2, up3 = (w for w in face_weights(courant))
    forward = courant >= 0.0
    zero = jnp.zeros_like(courant)
    f = {1: down1, 0: up0, -1: up1, -2: up2, -3: up3}
    b = {-2: down1, -1: up0, 0: up1, 1: up2, 2: up3}
    return {m: jnp.where(forward, f.get(m, zero), b.get(m, zero)) for m in range(-3, 3)}


def east_taps(courant, whole):
    weights = face_weights(courant)
    forward = courant >= 0.0
    zero = jnp.zeros_like(courant)
    one = whole == 1.0
    two = whole == 2.0
    some = whole > 0.5
    taps = {}
    for m in range(-EDGE, EDGE):
        ahead = []
        behind = []
        for n in range(NS + 1):
            place = 1 - n - m
            ahead.append(weights[place] if 0 <= place < 5 else zero)
            place = m + 2 - n
            behind.append(weights[place] if 0 <= place < 5 else zero)
        f = jnp.where(two, ahead[2], jnp.where(one, ahead[1], ahead[0]))
        b = jnp.where(two, behind[2], jnp.where(one, behind[1], behind[0]))
        if m == -1:
            f = f + jnp.where(some, 0.5, 0.0)
        if m == -2:
            f = f + jnp.where(two, 0.5, 0.0)
        if m == 0:
            b = b - jnp.where(some, 0.5, 0.0)
        if m == 1:
            b = b - jnp.where(two, 0.5, 0.0)
        taps[m] = jnp.where(forward, f, b)
    return taps


def difference_taps(here, ahead, reach):
    out = {}
    for m in range(-reach, reach + 1):
        if m in here and m - 1 in ahead:
            out[m] = here[m] - ahead[m - 1]
        elif m in here:
            out[m] = here[m]
        else:
            out[m] = -ahead[m - 1]
    return out


def north_coefficients(courant):
    count = courant.shape[0]
    row = row_index(courant.shape)
    here = north_taps(jnp.where(row == 0, 0.0, courant))
    taps = difference_taps(here, {m: rows(here[m], -1) for m in here}, 3)
    return [
        jnp.where((row + m >= 0) & (row + m < count), taps[m], 0.0) for m in range(-3, 4)
    ]


def pick(x, index):
    return jnp.take_along_axis(x, index, axis=1, mode="promise_in_bounds")


def position():
    return lax.axis_index("tracer")


def tile():
    return lax.axis_index("space")


def early_levels(levels):
    return jnp.clip(levels - tile(), 0, levels - 1)


def prepare_kernel(*refs):
    sources, (keep, send, *fields, sems) = refs[:6], refs[6:]
    copies = [
        pltpu.make_async_copy(source, place, sems.at[k])
        for k, (source, place) in enumerate(zip(sources, fields))
    ]
    for copy in copies:
        copy.start()
    for copy in copies:
        copy.wait()
    thick, fe, fn, ce, cn, ne = fields
    core = position() % 2
    levels, count, width = thick.shape[1:]
    lane = lane_index((count, width))
    row = row_index((count, width))
    edge_rows = jnp.zeros((count, width), jnp.float32)
    for l in range(levels):
        east_mass = fe[0, l]
        north_mass = jnp.where(row == 0, 0.0, fn[0, l])
        thickness = (
            thick[0, l]
            + (east_mass - jnp.where(lane == width - 1, 0.0, lanes(east_mass, -1)))
            + (north_mass - rows(north_mass, -1))
        )
        whole = ne[0, l].astype(jnp.float32)
        first = (thickness, ce[0, l])
        second = (cn[0, l], whole)
        for k in range(2):
            start = (k * levels + l) * count
            keep[start : start + count, :] = jnp.where(core == 0, first[k], second[k])
            send[start : start + count, :] = jnp.where(core == 0, second[k], first[k])
        edges = jnp.where(lane < SEG, lanes(cn[0, l], EDGE), 0.0)
        for k, value in enumerate((ce[0, l], whole, east_mass)):
            edges = jnp.where(lane == SEG + k, lanes(value, SEG + k), edges)
        edge_rows = edge_rows + lanes(jnp.where(lane < MET_SEG, edges, 0.0), MET_SEG * l)
    base = 2 * levels * count
    folded = edge_rows[: count // 2] + lanes(edge_rows[count // 2 :], MET_SEG * levels)
    keep[base:, :] = folded
    send[base:, :] = folded


def prepare(thick, fe, fn, ce, cn, ne):
    levels, count, width = thick.shape[1:]
    vmem = pl.BlockSpec(memory_space=pltpu.VMEM)
    half = pltpu.VMEM((2 * levels * count + count // 2, width), jnp.float32)
    return pl.pallas_call(
        prepare_kernel,
        out_shape=(half, half),
        in_specs=[pl.BlockSpec(memory_space=pl.ANY)] * 6,
        out_specs=(vmem, vmem),
        scratch_shapes=[pltpu.VMEM(thick.shape, jnp.float32)] * 5
        + [pltpu.VMEM(ne.shape, jnp.int32), pltpu.SemaphoreType.DMA((6,))],
        name="prepare",
    )(thick, fe, fn, ce, cn, ne)


def pack_kernel(mass, last, first):
    tracers, levels, count, width = mass.shape
    lane = lane_index((count, width))

    def level(l, carry):
        a = jnp.zeros((count, width), jnp.float32)
        b = a
        for t in range(tracers):
            inside = (lane >= EDGE * t) & (lane < EDGE * (t + 1))
            a = jnp.where(inside, lanes(mass[t, l], EDGE * (t + 1)), a)
            b = jnp.where(inside, lanes(mass[t, l], EDGE * t), b)
        place = pl.ds(pl.multiple_of(l * count, count), count)
        last[place, :] = a
        first[place, :] = b
        return carry

    lax.fori_loop(0, levels, level, 0)


def copies_kernel(mass, padded, moved):
    tracers, levels, count, width = mass.shape
    zero_rows = jnp.zeros((PAD, width), jnp.float32)

    def level(l, carry):
        for t in range(tracers):
            value = mass[t, l]
            padded[t, l, :PAD, :] = zero_rows
            padded[t, l, PAD : PAD + count, :] = value
            padded[t, l, PAD + count :, :] = zero_rows
            for k, shift in enumerate(NEAR):
                moved[k, t, l] = lanes(value, -shift)
        return carry

    lax.fori_loop(0, levels, level, 0)


def in_vmem(kernel, name, shapes, *operands):
    vmem = pl.BlockSpec(memory_space=pltpu.VMEM)
    return pl.pallas_call(
        kernel,
        out_shape=tuple(pltpu.VMEM(shape, jnp.float32) for shape in shapes),
        in_specs=[vmem] * len(operands),
        out_specs=(vmem,) * len(shapes),
        compiler_params=pltpu.CompilerParams(vmem_limit_bytes=24 * 1024 * 1024),
        cost_estimate=pl.CostEstimate(flops=2000000, bytes_accessed=1000000, transcendentals=0),
        name=name,
    )(*operands)


def pack(mass):
    _, levels, count, width = mass.shape
    return in_vmem(pack_kernel, "pack", ((levels * count, width),) * 2, mass)


def copies(mass):
    tracers, levels, count, width = mass.shape
    padded = (tracers, levels, count + 2 * PAD, width)
    return in_vmem(copies_kernel, "copies", (padded, (len(NEAR),) + mass.shape), mass)


def segments(shape):
    lane = lane_index(shape)
    segment = sum(
        ((lane >= SEG * k).astype(jnp.int32) for k in range(1, PACK)), jnp.zeros(shape, jnp.int32)
    )
    return segment, lane - SEG * segment, lane < SEG * PACK


def moved_places(held):
    return {shift: lanes(held, shift) if shift else held for shift in (-STEP, 0, STEP)}


def east_parts(taps, near, parts=None):
    parts = dict(parts or {})
    for m in taps:
        shift = east_group(m)
        term = taps[m] * near[m - shift]
        parts[shift] = parts[shift] + term if shift in parts else term
    return parts


def moved_sum(parts):
    return parts[0] + (lanes(parts[-STEP], STEP) + lanes(parts[STEP], -STEP))


def near_cells(x):
    return {0: x, **{shift: lanes(x, -shift) for shift in NEAR}}


def inner_kernel(span, mine, other, padded, shifted, *refs):
    low_level, high_level = span(refs[0].shape[1])

    @pl.when(low_level < high_level)
    def _():
        inner_body(low_level, high_level, mine, other, padded, shifted, *refs)


def inner_body(
    low_level, high_level, mine, other, padded, shifted, sums, outer_c, edge_c, thickness,
    east_c, north_c, inners, middle, partial,
):
    tracers, levels, count, width = sums.shape
    shape = (count, width)
    lane = lane_index(shape)
    low = position() % 2 == 0
    _, in_segment, packed_lane = segments(shape)
    zero_rows = jnp.zeros((PAD, width), jnp.float32)
    for slot in range(2):
        for j in range(GROUP):
            middle[slot, j, :PAD, :] = zero_rows
            middle[slot, j, PAD + count :, :] = zero_rows
    edge_index = jnp.where(packed_lane, in_segment + (width - EDGE), 0)
    edge_index = jnp.where(edge_index >= width, edge_index - width, edge_index)
    moved_index = moved_places(edge_index)
    moved_segment = moved_places(jnp.where(packed_lane, in_segment, -2 * SEG))

    def level(l, carry):
        fields = []
        for half in range(2):
            for k in range(2):
                place = pl.ds(pl.multiple_of((k * levels + l) * count, count), count)
                a = mine[place, :]
                b = other[place, :]
                fields.append(jnp.where(low, a, b) if half == 0 else jnp.where(low, b, a))
        thick, east_courant, north_courant, whole = fields
        thickness[l] = thick
        here = east_taps(east_courant, whole)
        ahead = {m: jnp.where(lane == width - 1, 0.0, lanes(here[m], -1)) for m in here}
        taps = difference_taps(here, ahead, EDGE)
        for m in range(-EDGE, EDGE + 1):
            value = taps[m]
            if m != 0:
                q = moved_segment[east_group(m)]
                crosses = ((q < EDGE) != (q + m < EDGE)) & (q >= 0)
                outer_c[m + EDGE, l] = jnp.where(crosses, pick(value, moved_index[east_group(m)]), 0.0)
            if m < 0:
                value = jnp.where(lane >= -m, value, 0.0)
            if m > 0:
                value = jnp.where(lane < width - m, value, 0.0)
            shift = east_group(m)
            east_c[m + EDGE, l] = lanes(value, shift) if shift else value
        for m, value in enumerate(north_coefficients(north_courant)):
            north_c[m, l] = value
        for m, value in enumerate(north_coefficients(pick(north_courant, edge_index))):
            edge_c[m, l] = value
        return carry

    lax.fori_loop(low_level, high_level, level, 0)
    groups = tracers // GROUP

    def block(b):
        return slice(b * BLOCK, (b + 1) * BLOCK)

    def padded_block(b, m=0):
        return slice(PAD + b * BLOCK + m, PAD + (b + 1) * BLOCK + m)

    def place(step):
        step = jnp.clip(step, 0, levels * groups - 1)
        return step // groups, (step % groups) * GROUP

    def weights(ref, l, b, reach):
        return {m: ref[m + reach, l, block(b), :] for m in range(-reach, reach + 1)}

    def front(step):
        l, t0 = place(step)
        slot = (step + 2) % 2
        for b in range(count // BLOCK):
            taps = weights(east_c, l, b, EDGE)
            north = weights(north_c, l, b, 3)
            taps[0] = 1.0 + taps[0]
            north[0] = 1.0 + north[0]
            for j in range(GROUP):
                x = padded[t0 + j, l, padded_block(b), :]
                inner = north[0] * x
                for m in (-3, -2, -1, 1, 2, 3):
                    inner = inner + north[m] * padded[t0 + j, l, padded_block(b, m), :]
                inners[slot, j, block(b), :] = inner
                near = {0: x}
                for k, shift in enumerate(NEAR):
                    near[shift] = shifted[k, t0 + j, l, block(b), :]
                middle[slot, j, padded_block(b), :] = moved_sum(east_parts(taps, near))

    def back(step):
        l, t0 = place(step)
        slot = (step + 2) % 2
        for b in range(count // BLOCK):
            taps = weights(east_c, l, b, EDGE)
            north = weights(north_c, l, b, 3)
            for j in range(GROUP):
                parts = east_parts(taps, near_cells(inners[slot, j, block(b), :]))
                total = 0.5 * padded[t0 + j, l, padded_block(b), :] + parts[0]
                for m in range(-3, 4):
                    total = total + north[m] * middle[slot, j, padded_block(b, m), :]
                partial[slot, 0, j, block(b), :] = total
                partial[slot, 1, j, block(b), :] = parts[-STEP]
                partial[slot, 2, j, block(b), :] = parts[STEP]

    def finish(step):
        l, t0 = place(step)
        slot = (step + 2) % 2
        for b in range(count // BLOCK):
            for j in range(GROUP):
                sums[t0 + j, l, block(b), :] = partial[slot, 0, j, block(b), :] + (
                    lanes(partial[slot, 1, j, block(b), :], STEP)
                    + lanes(partial[slot, 2, j, block(b), :], -STEP)
                )

    def step_of_three(step, carry):
        finish(step - 1)
        back(step)
        front(step + 1)
        return carry

    front(low_level * groups)
    lax.fori_loop(low_level * groups, high_level * groups, step_of_three, 0)
    finish(high_level * groups - 1)


def inner_update(span, mine, other, padded, shifted):
    tracers, levels, count, width = shifted.shape[1:]
    vmem = pl.BlockSpec(memory_space=pltpu.VMEM)
    level = (levels, count, width)
    return pl.pallas_call(
        functools.partial(inner_kernel, span),
        out_shape=(
            pltpu.VMEM((tracers,) + level, jnp.float32),
            pltpu.VMEM((2 * EDGE + 1,) + level, jnp.float32),
            pltpu.VMEM((7,) + level, jnp.float32),
            pltpu.VMEM(level, jnp.float32),
        ),
        in_specs=[vmem] * 4,
        out_specs=(vmem,) * 4,
        scratch_shapes=[
            pltpu.VMEM((2 * EDGE + 1,) + level, jnp.float32),
            pltpu.VMEM((7,) + level, jnp.float32),
            pltpu.VMEM((2, GROUP, count, width), jnp.float32),
            pltpu.VMEM((2, GROUP, count + 2 * PAD, width), jnp.float32),
            pltpu.VMEM((2, 3, GROUP, count, width), jnp.float32),
        ],
        compiler_params=pltpu.CompilerParams(vmem_limit_bytes=24 * 1024 * 1024),
        cost_estimate=pl.CostEstimate(flops=20000000, bytes_accessed=6000000, transcendentals=0),
        name="inner",
    )(mine, other, padded, shifted)


def edge_kernel(west, east, own, *refs):
    before, after, (out, stage, sems) = refs[:4], refs[4:8], refs[8:]
    tracers, levels, count, width = stage.shape
    first_levels = early_levels(levels)
    shape = (count, width)
    lane = lane_index(shape)
    segment, in_segment, packed_lane = segments(shape)
    from_west_lane = in_segment < EDGE
    at_edge = (lane < EDGE) | (lane >= width - EDGE)
    last_face = {
        shift: q == EDGE - 1
        for shift, q in moved_places(jnp.where(packed_lane, in_segment, -2 * SEG)).items()
    }
    base = levels * count

    def unfolded(x):
        return jnp.concatenate([x, lanes(x, -MET_SEG * levels)])

    met_east = unfolded(east[base:, :])
    met_west = unfolded(west[base:, :])

    def copy(l, half):
        place = pl.ds(half * PACK, PACK)
        return pltpu.make_async_copy(stage.at[place, l], out.at[place, l], sems.at[l, half])

    def level(l, sums, outer_c, edge_c, thickness):
        level_rows = pl.ds(pl.multiple_of(l * count, count), count)
        met_lane = jnp.where(packed_lane, in_segment + MET_SEG * l, 0)
        met = jnp.where(lane - MET_SEG * l < EDGE, met_west, met_east)
        beyond = east_taps(
            pick(met_east, jnp.full(shape, SEG, jnp.int32) + MET_SEG * l),
            pick(met_east, jnp.full(shape, SEG + 1, jnp.int32) + MET_SEG * l),
        )
        mass_flux = pick(met_east, jnp.full(shape, SEG + 2, jnp.int32) + MET_SEG * l)
        inverse = 2.0 / (thickness[l] - jnp.where(lane == width - 1, mass_flux, 0.0))
        face = {
            m: jnp.where(last_face[east_group(m)], -beyond[m - 1], 0.0)
            for m in range(1 - EDGE, EDGE + 1)
        }
        outer = {m: outer_c[m + EDGE, l] for m in range(-EDGE, EDGE + 1) if m != 0}
        for m in range(1, EDGE + 1):
            outer[m] = outer[m] + face[m]
        inside = {m: face[m] for m in range(1 - EDGE, 1)}
        edge_taps = [edge_c[m, l] for m in range(7)]
        packed_taps = north_coefficients(pick(met, met_lane))
        for half in range(2):
            first_lane = EDGE * (segment + PACK * half) + in_segment
            west_index = jnp.where(packed_lane & from_west_lane, first_lane, 0)
            east_index = jnp.where(packed_lane & ~from_west_lane, first_lane - EDGE, 0)
            own_cells = pick(own[level_rows, :], west_index)
            cells = jnp.where(
                from_west_lane,
                pick(west[level_rows, :], west_index),
                pick(east[level_rows, :], east_index),
            )
            inner = cells
            own_inner = own_cells
            for m in range(-3, 4):
                inner = inner + packed_taps[m + 3] * rows(cells, -m)
                own_inner = own_inner + edge_taps[m + 3] * rows(own_cells, -m)
            first = moved_sum(
                east_parts(inside, near_cells(own_cells), east_parts(outer, near_cells(cells)))
            )
            total = moved_sum(
                east_parts(inside, near_cells(own_inner), east_parts(outer, near_cells(inner)))
            )
            for m in range(-3, 4):
                total = total + edge_taps[m + 3] * rows(first, -m)
            for k in range(PACK):
                t = half * PACK + k
                moved = jnp.where(at_edge, lanes(total, width - EDGE - SEG * k), 0.0)
                stage[t, l] = (sums[t, l] + moved) * inverse
            copy(l, half).start()

    def either(l, carry):
        @pl.when(l < first_levels)
        def _():
            level(l, *before)

        @pl.when(l >= first_levels)
        def _():
            level(l, *after)

        return carry

    lax.fori_loop(0, levels, either, 0)
    for l in range(levels):
        for half in range(2):
            copy(l, half).wait()


def edge_update(west, east, own, before, after):
    sums = before[0]
    tracers, levels, count, width = sums.shape
    vmem = pl.BlockSpec(memory_space=pltpu.VMEM)
    return pl.pallas_call(
        edge_kernel,
        out_shape=jax.ShapeDtypeStruct(sums.shape, jnp.float32),
        in_specs=[vmem] * 11,
        out_specs=pl.BlockSpec(memory_space=pl.ANY),
        scratch_shapes=[pltpu.VMEM(sums.shape, jnp.float32), pltpu.SemaphoreType.DMA((levels, 2))],
        compiler_params=pltpu.CompilerParams(vmem_limit_bytes=24 * 1024 * 1024),
        name="edges",
    )(west, east, own, *before, *after)


def east_group(m):
    return -STEP if m < -1 else (STEP if m > 2 else 0)


def along(x, pairs):
    return lax.ppermute(x, "space", pairs)


def exchange(x, flip):
    size = lax.axis_size("tracer")
    return lax.ppermute(x, "tracer", [(i, i ^ flip) for i in range(size)])


def turn(x, by):
    size = lax.axis_size("tracer")
    return lax.ppermute(x, "tracer", [(i, i // 8 * 8 + (i + 2 * by) % 8) for i in range(size)])


def shards(mass, thick, fe, fn, ce, cn, ne, owner):
    keep, send = prepare(thick, fe, fn, ce, cn, ne)
    last, first = pack(mass)
    me, chosen = position(), owner[0]
    other_core = exchange(send, 1)
    total = jnp.where(chosen == me, keep, jnp.where(chosen == me ^ 1, other_core, 0.0))
    total = total + (turn(total, 1) + turn(total, -1) + turn(total, 2))
    total, last, first = lax.optimization_barrier((total, last, first))
    total = total + exchange(total, 8)
    padded, shifted = copies(mass)
    main = 2 * mass.shape[1] * mass.shape[2]
    mine = total[:main]
    edges = total[main:]
    size = lax.axis_size("space")
    to_east = jnp.concatenate([last, edges])
    to_west = jnp.concatenate([first, edges])
    west = along(to_east, [(i, (i + 1) % size) for i in range(size)])
    other = exchange(mine, 1)
    before = inner_update(lambda levels: (0, early_levels(levels)), mine, other, padded, shifted)
    to_west, before = lax.optimization_barrier((to_west, before))
    east = along(to_west, [(i, (i - 1) % size) for i in range(size)])
    after = inner_update(lambda levels: (early_levels(levels), levels), mine, other, padded, shifted)
    return edge_update(west, east, last, before, after)


def solution(mesh):
    spec = P("tracer", None, None, "space")
    return jax.shard_map(
        shards, mesh=mesh, in_specs=(spec,) * 7 + (P("space"),), out_specs=spec, check_vma=False
    )
```

```python
import functools

import jax
import jax.numpy as jnp
from jax import lax
from jax.experimental import pallas as pl
from jax.experimental.pallas import tpu as pltpu
from jax.sharding import PartitionSpec as P

NS = 2
EDGE = NS + 3
SEG = 2 * EDGE
PACK = 9
STEP = 4
GROUP = 3
PAD = 8
BLOCK = 8
NEAR = (-1, 1, 2)
MET_SEG = 16


def lane_index(shape):
    return lax.broadcasted_iota(jnp.int32, shape, len(shape) - 1)


def row_index(shape):
    return lax.broadcasted_iota(jnp.int32, shape, len(shape) - 2)


def lanes(x, shift):
    return pltpu.roll(x, shift % x.shape[-1], x.ndim - 1)


def rows(x, shift):
    return pltpu.roll(x, shift % x.shape[-2], x.ndim - 2)


def face_weights(courant):
    fraction = jnp.abs(courant)
    ramp = 1.5 * fraction * (1.0 - 2.0 / 3.0 * fraction)
    near = 0.5 * courant * (1.0 - 0.5 * fraction - ramp)
    far = 0.5 * courant * (0.5 * fraction - ramp)
    mean = courant * ramp
    far_outer = far * (1.0 / 12.0)
    near_outer = near * (1.0 / 12.0)
    return (
        -near_outer,
        7.0 * near_outer - far_outer,
        7.0 * (near_outer + far_outer) + mean,
        7.0 * far_outer - near_outer,
        -far_outer,
    )


def north_taps(courant):
    down1, up0, up1, up2, up3 = (w for w in face_weights(courant))
    forward = courant >= 0.0
    zero = jnp.zeros_like(courant)
    f = {1: down1, 0: up0, -1: up1, -2: up2, -3: up3}
    b = {-2: down1, -1: up0, 0: up1, 1: up2, 2: up3}
    return {m: jnp.where(forward, f.get(m, zero), b.get(m, zero)) for m in range(-3, 3)}


def east_taps(courant, whole):
    weights = face_weights(courant)
    forward = courant >= 0.0
    zero = jnp.zeros_like(courant)
    one = whole == 1.0
    two = whole == 2.0
    some = whole > 0.5
    taps = {}
    for m in range(-EDGE, EDGE):
        ahead = []
        behind = []
        for n in range(NS + 1):
            place = 1 - n - m
            ahead.append(weights[place] if 0 <= place < 5 else zero)
            place = m + 2 - n
            behind.append(weights[place] if 0 <= place < 5 else zero)
        f = jnp.where(two, ahead[2], jnp.where(one, ahead[1], ahead[0]))
        b = jnp.where(two, behind[2], jnp.where(one, behind[1], behind[0]))
        if m == -1:
            f = f + jnp.where(some, 0.5, 0.0)
        if m == -2:
            f = f + jnp.where(two, 0.5, 0.0)
        if m == 0:
            b = b - jnp.where(some, 0.5, 0.0)
        if m == 1:
            b = b - jnp.where(two, 0.5, 0.0)
        taps[m] = jnp.where(forward, f, b)
    return taps


def difference_taps(here, ahead, reach):
    out = {}
    for m in range(-reach, reach + 1):
        if m in here and m - 1 in ahead:
            out[m] = here[m] - ahead[m - 1]
        elif m in here:
            out[m] = here[m]
        else:
            out[m] = -ahead[m - 1]
    return out


def north_coefficients(courant):
    count = courant.shape[0]
    row = row_index(courant.shape)
    here = north_taps(jnp.where(row == 0, 0.0, courant))
    taps = difference_taps(here, {m: rows(here[m], -1) for m in here}, 3)
    return [
        jnp.where((row + m >= 0) & (row + m < count), taps[m], 0.0) for m in range(-3, 4)
    ]


def pick(x, index):
    return jnp.take_along_axis(x, index, axis=1, mode="promise_in_bounds")


def position():
    return lax.axis_index("tracer")


def tile():
    return lax.axis_index("space")


def early_levels(levels):
    return jnp.clip(levels - tile(), 0, levels - 1)


def prepare_kernel(*refs):
    sources, (keep, send, *fields, sems) = refs[:6], refs[6:]
    copies = [
        pltpu.make_async_copy(source, place, sems.at[k])
        for k, (source, place) in enumerate(zip(sources, fields))
    ]
    for copy in copies:
        copy.start()
    for copy in copies:
        copy.wait()
    thick, fe, fn, ce, cn, ne = fields
    core = position() % 2
    levels, count, width = thick.shape[1:]
    lane = lane_index((count, width))
    row = row_index((count, width))
    edge_rows = jnp.zeros((count, width), jnp.float32)
    for l in range(levels):
        east_mass = fe[0, l]
        north_mass = jnp.where(row == 0, 0.0, fn[0, l])
        thickness = (
            thick[0, l]
            + (east_mass - jnp.where(lane == width - 1, 0.0, lanes(east_mass, -1)))
            + (north_mass - rows(north_mass, -1))
        )
        whole = ne[0, l].astype(jnp.float32)
        first = (thickness, ce[0, l])
        second = (cn[0, l], whole)
        for k in range(2):
            start = (k * levels + l) * count
            keep[start : start + count, :] = jnp.where(core == 0, first[k], second[k])
            send[start : start + count, :] = jnp.where(core == 0, second[k], first[k])
        edges = jnp.where(lane < SEG, lanes(cn[0, l], EDGE), 0.0)
        for k, value in enumerate((ce[0, l], whole, east_mass)):
            edges = jnp.where(lane == SEG + k, lanes(value, SEG + k), edges)
        edge_rows = edge_rows + lanes(jnp.where(lane < MET_SEG, edges, 0.0), MET_SEG * l)
    base = 2 * levels * count
    folded = edge_rows[: count // 2] + lanes(edge_rows[count // 2 :], MET_SEG * levels)
    keep[base:, :] = folded
    send[base:, :] = folded


def prepare(thick, fe, fn, ce, cn, ne):
    levels, count, width = thick.shape[1:]
    vmem = pl.BlockSpec(memory_space=pltpu.VMEM)
    half = pltpu.VMEM((2 * levels * count + count // 2, width), jnp.float32)
    return pl.pallas_call(
        prepare_kernel,
        out_shape=(half, half),
        in_specs=[pl.BlockSpec(memory_space=pl.ANY)] * 6,
        out_specs=(vmem, vmem),
        scratch_shapes=[pltpu.VMEM(thick.shape, jnp.float32)] * 5
        + [pltpu.VMEM(ne.shape, jnp.int32), pltpu.SemaphoreType.DMA((6,))],
        name="prepare",
    )(thick, fe, fn, ce, cn, ne)


def pack_kernel(mass, last, first):
    tracers, levels, count, width = mass.shape
    lane = lane_index((count, width))

    def level(l, carry):
        a = jnp.zeros((count, width), jnp.float32)
        b = a
        for t in range(tracers):
            inside = (lane >= EDGE * t) & (lane < EDGE * (t + 1))
            a = jnp.where(inside, lanes(mass[t, l], EDGE * (t + 1)), a)
            b = jnp.where(inside, lanes(mass[t, l], EDGE * t), b)
        place = pl.ds(pl.multiple_of(l * count, count), count)
        last[place, :] = a
        first[place, :] = b
        return carry

    lax.fori_loop(0, levels, level, 0)


def copies_kernel(mass, padded, moved):
    tracers, levels, count, width = mass.shape
    zero_rows = jnp.zeros((PAD, width), jnp.float32)

    def level(l, carry):
        for t in range(tracers):
            value = mass[t, l]
            padded[t, l, :PAD, :] = zero_rows
            padded[t, l, PAD : PAD + count, :] = value
            padded[t, l, PAD + count :, :] = zero_rows
            for k, shift in enumerate(NEAR):
                moved[k, t, l] = lanes(value, -shift)
        return carry

    lax.fori_loop(0, levels, level, 0)


def in_vmem(kernel, name, shapes, *operands):
    vmem = pl.BlockSpec(memory_space=pltpu.VMEM)
    return pl.pallas_call(
        kernel,
        out_shape=tuple(pltpu.VMEM(shape, jnp.float32) for shape in shapes),
        in_specs=[vmem] * len(operands),
        out_specs=(vmem,) * len(shapes),
        compiler_params=pltpu.CompilerParams(vmem_limit_bytes=24 * 1024 * 1024),
        cost_estimate=pl.CostEstimate(flops=2000000, bytes_accessed=1000000, transcendentals=0),
        name=name,
    )(*operands)


def pack(mass):
    _, levels, count, width = mass.shape
    return in_vmem(pack_kernel, "pack", ((levels * count, width),) * 2, mass)


def copies(mass):
    tracers, levels, count, width = mass.shape
    padded = (tracers, levels, count + 2 * PAD, width)
    return in_vmem(copies_kernel, "copies", (padded, (len(NEAR),) + mass.shape), mass)


def segments(shape):
    lane = lane_index(shape)
    segment = sum(
        ((lane >= SEG * k).astype(jnp.int32) for k in range(1, PACK)), jnp.zeros(shape, jnp.int32)
    )
    return segment, lane - SEG * segment, lane < SEG * PACK


def moved_places(held):
    return {shift: lanes(held, shift) if shift else held for shift in (-STEP, 0, STEP)}


def east_parts(taps, near, parts=None):
    parts = dict(parts or {})
    for m in taps:
        shift = east_group(m)
        term = taps[m] * near[m - shift]
        parts[shift] = parts[shift] + term if shift in parts else term
    return parts


def moved_sum(parts):
    return parts[0] + (lanes(parts[-STEP], STEP) + lanes(parts[STEP], -STEP))


def near_cells(x):
    return {0: x, **{shift: lanes(x, -shift) for shift in NEAR}}


def inner_kernel(span, mine, other, padded, shifted, *refs):
    low_level, high_level = span(refs[0].shape[1])

    @pl.when(low_level < high_level)
    def _():
        inner_body(low_level, high_level, mine, other, padded, shifted, *refs)


def inner_body(
    low_level, high_level, mine, other, padded, shifted, sums, outer_c, edge_c, thickness,
    east_c, north_c, inners, middle, partial,
):
    tracers, levels, count, width = sums.shape
    shape = (count, width)
    lane = lane_index(shape)
    low = position() % 2 == 0
    _, in_segment, packed_lane = segments(shape)
    zero_rows = jnp.zeros((PAD, width), jnp.float32)
    for slot in range(2):
        for j in range(GROUP):
            middle[slot, j, :PAD, :] = zero_rows
            middle[slot, j, PAD + count :, :] = zero_rows
    edge_index = jnp.where(packed_lane, in_segment + (width - EDGE), 0)
    edge_index = jnp.where(edge_index >= width, edge_index - width, edge_index)
    moved_index = moved_places(edge_index)
    moved_segment = moved_places(jnp.where(packed_lane, in_segment, -2 * SEG))

    def level(l, carry):
        fields = []
        for half in range(2):
            for k in range(2):
                place = pl.ds(pl.multiple_of((k * levels + l) * count, count), count)
                a = mine[place, :]
                b = other[place, :]
                fields.append(jnp.where(low, a, b) if half == 0 else jnp.where(low, b, a))
        thick, east_courant, north_courant, whole = fields
        thickness[l] = thick
        here = east_taps(east_courant, whole)
        ahead = {m: jnp.where(lane == width - 1, 0.0, lanes(here[m], -1)) for m in here}
        taps = difference_taps(here, ahead, EDGE)
        for m in range(-EDGE, EDGE + 1):
            value = taps[m]
            if m != 0:
                q = moved_segment[east_group(m)]
                crosses = ((q < EDGE) != (q + m < EDGE)) & (q >= 0)
                outer_c[m + EDGE, l] = jnp.where(crosses, pick(value, moved_index[east_group(m)]), 0.0)
            if m < 0:
                value = jnp.where(lane >= -m, value, 0.0)
            if m > 0:
                value = jnp.where(lane < width - m, value, 0.0)
            shift = east_group(m)
            east_c[m + EDGE, l] = lanes(value, shift) if shift else value
        for m, value in enumerate(north_coefficients(north_courant)):
            north_c[m, l] = value
        for m, value in enumerate(north_coefficients(pick(north_courant, edge_index))):
            edge_c[m, l] = value
        return carry

    lax.fori_loop(low_level, high_level, level, 0)
    groups = tracers // GROUP

    def block(b):
        return slice(b * BLOCK, (b + 1) * BLOCK)

    def padded_block(b, m=0):
        return slice(PAD + b * BLOCK + m, PAD + (b + 1) * BLOCK + m)

    def place(step):
        step = jnp.clip(step, 0, levels * groups - 1)
        return step // groups, (step % groups) * GROUP

    def weights(ref, l, b, reach):
        return {m: ref[m + reach, l, block(b), :] for m in range(-reach, reach + 1)}

    def front(step):
        l, t0 = place(step)
        slot = (step + 2) % 2
        for b in range(count // BLOCK):
            taps = weights(east_c, l, b, EDGE)
            north = weights(north_c, l, b, 3)
            taps[0] = 1.0 + taps[0]
            north[0] = 1.0 + north[0]
            for j in range(GROUP):
                x = padded[t0 + j, l, padded_block(b), :]
                inner = north[0] * x
                for m in (-3, -2, -1, 1, 2, 3):
                    inner = inner + north[m] * padded[t0 + j, l, padded_block(b, m), :]
                inners[slot, j, block(b), :] = inner
                near = {0: x}
                for k, shift in enumerate(NEAR):
                    near[shift] = shifted[k, t0 + j, l, block(b), :]
                middle[slot, j, padded_block(b), :] = moved_sum(east_parts(taps, near))

    def back(step):
        l, t0 = place(step)
        slot = (step + 2) % 2
        for b in range(count // BLOCK):
            taps = weights(east_c, l, b, EDGE)
            north = weights(north_c, l, b, 3)
            for j in range(GROUP):
                parts = east_parts(taps, near_cells(inners[slot, j, block(b), :]))
                total = 0.5 * padded[t0 + j, l, padded_block(b), :] + parts[0]
                for m in range(-3, 4):
                    total = total + north[m] * middle[slot, j, padded_block(b, m), :]
                partial[slot, 0, j, block(b), :] = total
                partial[slot, 1, j, block(b), :] = parts[-STEP]
                partial[slot, 2, j, block(b), :] = parts[STEP]

    def finish(step):
        l, t0 = place(step)
        slot = (step + 2) % 2
        for b in range(count // BLOCK):
            for j in range(GROUP):
                sums[t0 + j, l, block(b), :] = partial[slot, 0, j, block(b), :] + (
                    lanes(partial[slot, 1, j, block(b), :], STEP)
                    + lanes(partial[slot, 2, j, block(b), :], -STEP)
                )

    def step_of_three(step, carry):
        finish(step - 1)
        back(step)
        front(step + 1)
        return carry

    front(low_level * groups)
    lax.fori_loop(low_level * groups, high_level * groups, step_of_three, 0)
    finish(high_level * groups - 1)


def inner_update(span, mine, other, padded, shifted):
    tracers, levels, count, width = shifted.shape[1:]
    vmem = pl.BlockSpec(memory_space=pltpu.VMEM)
    level = (levels, count, width)
    return pl.pallas_call(
        functools.partial(inner_kernel, span),
        out_shape=(
            pltpu.VMEM((tracers,) + level, jnp.float32),
            pltpu.VMEM((2 * EDGE + 1,) + level, jnp.float32),
            pltpu.VMEM((7,) + level, jnp.float32),
            pltpu.VMEM(level, jnp.float32),
        ),
        in_specs=[vmem] * 4,
        out_specs=(vmem,) * 4,
        scratch_shapes=[
            pltpu.VMEM((2 * EDGE + 1,) + level, jnp.float32),
            pltpu.VMEM((7,) + level, jnp.float32),
            pltpu.VMEM((2, GROUP, count, width), jnp.float32),
            pltpu.VMEM((2, GROUP, count + 2 * PAD, width), jnp.float32),
            pltpu.VMEM((2, 3, GROUP, count, width), jnp.float32),
        ],
        compiler_params=pltpu.CompilerParams(vmem_limit_bytes=24 * 1024 * 1024),
        cost_estimate=pl.CostEstimate(flops=20000000, bytes_accessed=6000000, transcendentals=0),
        name="inner",
    )(mine, other, padded, shifted)


def edge_kernel(west, west_rest, east, own, *refs):
    before, after, (out, stage, sems) = refs[:4], refs[4:8], refs[8:]
    tracers, levels, count, width = stage.shape
    first_levels = early_levels(levels)
    shape = (count, width)
    lane = lane_index(shape)
    segment, in_segment, packed_lane = segments(shape)
    from_west_lane = in_segment < EDGE
    at_edge = (lane < EDGE) | (lane >= width - EDGE)
    last_face = {
        shift: q == EDGE - 1
        for shift, q in moved_places(jnp.where(packed_lane, in_segment, -2 * SEG)).items()
    }
    base = levels * count

    def unfolded(x):
        return jnp.concatenate([x, lanes(x, -MET_SEG * levels)])

    met_east = unfolded(east[base:, :])
    met_west = unfolded(west[base:, :] + west_rest[:, :])

    def copy(l, half):
        place = pl.ds(half * PACK, PACK)
        return pltpu.make_async_copy(stage.at[place, l], out.at[place, l], sems.at[l, half])

    def level(l, sums, outer_c, edge_c, thickness):
        level_rows = pl.ds(pl.multiple_of(l * count, count), count)
        met_lane = jnp.where(packed_lane, in_segment + MET_SEG * l, 0)
        met = jnp.where(lane - MET_SEG * l < EDGE, met_west, met_east)
        beyond = east_taps(
            pick(met_east, jnp.full(shape, SEG, jnp.int32) + MET_SEG * l),
            pick(met_east, jnp.full(shape, SEG + 1, jnp.int32) + MET_SEG * l),
        )
        mass_flux = pick(met_east, jnp.full(shape, SEG + 2, jnp.int32) + MET_SEG * l)
        inverse = 2.0 / (thickness[l] - jnp.where(lane == width - 1, mass_flux, 0.0))
        face = {
            m: jnp.where(last_face[east_group(m)], -beyond[m - 1], 0.0)
            for m in range(1 - EDGE, EDGE + 1)
        }
        outer = {m: outer_c[m + EDGE, l] for m in range(-EDGE, EDGE + 1) if m != 0}
        for m in range(1, EDGE + 1):
            outer[m] = outer[m] + face[m]
        inside = {m: face[m] for m in range(1 - EDGE, 1)}
        edge_taps = [edge_c[m, l] for m in range(7)]
        packed_taps = north_coefficients(pick(met, met_lane))
        for half in range(2):
            first_lane = EDGE * (segment + PACK * half) + in_segment
            west_index = jnp.where(packed_lane & from_west_lane, first_lane, 0)
            east_index = jnp.where(packed_lane & ~from_west_lane, first_lane - EDGE, 0)
            own_cells = pick(own[level_rows, :], west_index)
            cells = jnp.where(
                from_west_lane,
                pick(west[level_rows, :], west_index),
                pick(east[level_rows, :], east_index),
            )
            inner = cells
            own_inner = own_cells
            for m in range(-3, 4):
                inner = inner + packed_taps[m + 3] * rows(cells, -m)
                own_inner = own_inner + edge_taps[m + 3] * rows(own_cells, -m)
            first = moved_sum(
                east_parts(inside, near_cells(own_cells), east_parts(outer, near_cells(cells)))
            )
            total = moved_sum(
                east_parts(inside, near_cells(own_inner), east_parts(outer, near_cells(inner)))
            )
            for m in range(-3, 4):
                total = total + edge_taps[m + 3] * rows(first, -m)
            for k in range(PACK):
                t = half * PACK + k
                moved = jnp.where(at_edge, lanes(total, width - EDGE - SEG * k), 0.0)
                stage[t, l] = (sums[t, l] + moved) * inverse
            copy(l, half).start()

    def either(l, carry):
        @pl.when(l < first_levels)
        def _():
            level(l, *before)

        @pl.when(l >= first_levels)
        def _():
            level(l, *after)

        return carry

    lax.fori_loop(0, levels, either, 0)
    for l in range(levels):
        for half in range(2):
            copy(l, half).wait()


def edge_update(west, west_rest, east, own, before, after):
    sums = before[0]
    tracers, levels, count, width = sums.shape
    vmem = pl.BlockSpec(memory_space=pltpu.VMEM)
    return pl.pallas_call(
        edge_kernel,
        out_shape=jax.ShapeDtypeStruct(sums.shape, jnp.float32),
        in_specs=[vmem] * 12,
        out_specs=pl.BlockSpec(memory_space=pl.ANY),
        scratch_shapes=[pltpu.VMEM(sums.shape, jnp.float32), pltpu.SemaphoreType.DMA((levels, 2))],
        compiler_params=pltpu.CompilerParams(vmem_limit_bytes=24 * 1024 * 1024),
        name="edges",
    )(west, west_rest, east, own, *before, *after)


def east_group(m):
    return -STEP if m < -1 else (STEP if m > 2 else 0)


def along(x, pairs):
    return lax.ppermute(x, "space", pairs)


def exchange(x, flip):
    size = lax.axis_size("tracer")
    return lax.ppermute(x, "tracer", [(i, i ^ flip) for i in range(size)])


def turn(x, by):
    size = lax.axis_size("tracer")
    return lax.ppermute(x, "tracer", [(i, i // 8 * 8 + (i + 2 * by) % 8) for i in range(size)])


def shards(mass, thick, fe, fn, ce, cn, ne, owner):
    keep, send = prepare(thick, fe, fn, ce, cn, ne)
    last, first = pack(mass)
    me, chosen = position(), owner[0]
    other_core = exchange(send, 1)
    total = jnp.where(chosen == me, keep, jnp.where(chosen == me ^ 1, other_core, 0.0))
    total = total + (turn(total, 1) + turn(total, -1) + turn(total, 2))
    total, last, first, mass = lax.optimization_barrier((total, last, first, mass))
    main = 2 * mass.shape[1] * mass.shape[2]
    size, tracers = lax.axis_size("space"), lax.axis_size("tracer")
    part = total[main:]
    total = total + exchange(total, 8)
    west = along(jnp.concatenate([last, part]), [(i, (i + 1) % size) for i in range(size)])
    west_rest = lax.ppermute(
        part,
        ("space", "tracer"),
        [
            (i * tracers + t, (i + 1) % size * tracers + (t ^ 8))
            for i in range(size)
            for t in range(tracers)
        ],
    )
    padded, shifted = copies(mass)
    mine = total[:main]
    to_west = jnp.concatenate([first, total[main:]])
    other, west_rest = lax.optimization_barrier((exchange(mine, 1), west_rest))
    before = inner_update(lambda levels: (0, early_levels(levels)), mine, other, padded, shifted)
    to_west, before = lax.optimization_barrier((to_west, before))
    east = along(to_west, [(i, (i - 1) % size) for i in range(size)])
    after = inner_update(lambda levels: (early_levels(levels), levels), mine, other, padded, shifted)
    return edge_update(west, west_rest, east, last, before, after)


def solution(mesh):
    spec = P("tracer", None, None, "space")
    return jax.shard_map(
        shards, mesh=mesh, in_specs=(spec,) * 7 + (P("space"),), out_specs=spec, check_vma=False
    )
```

```python
import functools

import jax
import jax.numpy as jnp
from jax import lax
from jax.experimental import pallas as pl
from jax.experimental.pallas import tpu as pltpu
from jax.sharding import PartitionSpec as P

NS = 2
EDGE = NS + 3
SEG = 2 * EDGE
PACK = 9
STEP = 4
GROUP = 3
PAD = 8
BLOCK = 8
NEAR = (-1, 1, 2)
MET_SEG = 16


def lane_index(shape):
    return lax.broadcasted_iota(jnp.int32, shape, len(shape) - 1)


def row_index(shape):
    return lax.broadcasted_iota(jnp.int32, shape, len(shape) - 2)


def lanes(x, shift):
    return pltpu.roll(x, shift % x.shape[-1], x.ndim - 1)


def rows(x, shift):
    return pltpu.roll(x, shift % x.shape[-2], x.ndim - 2)


def face_weights(courant):
    fraction = jnp.abs(courant)
    ramp = 1.5 * fraction * (1.0 - 2.0 / 3.0 * fraction)
    near = 0.5 * courant * (1.0 - 0.5 * fraction - ramp)
    far = 0.5 * courant * (0.5 * fraction - ramp)
    mean = courant * ramp
    far_outer = far * (1.0 / 12.0)
    near_outer = near * (1.0 / 12.0)
    return (
        -near_outer,
        7.0 * near_outer - far_outer,
        7.0 * (near_outer + far_outer) + mean,
        7.0 * far_outer - near_outer,
        -far_outer,
    )


def north_taps(courant):
    down1, up0, up1, up2, up3 = (w for w in face_weights(courant))
    forward = courant >= 0.0
    zero = jnp.zeros_like(courant)
    f = {1: down1, 0: up0, -1: up1, -2: up2, -3: up3}
    b = {-2: down1, -1: up0, 0: up1, 1: up2, 2: up3}
    return {m: jnp.where(forward, f.get(m, zero), b.get(m, zero)) for m in range(-3, 3)}


def east_taps(courant, whole):
    weights = face_weights(courant)
    forward = courant >= 0.0
    zero = jnp.zeros_like(courant)
    one = whole == 1.0
    two = whole == 2.0
    some = whole > 0.5
    taps = {}
    for m in range(-EDGE, EDGE):
        ahead = []
        behind = []
        for n in range(NS + 1):
            place = 1 - n - m
            ahead.append(weights[place] if 0 <= place < 5 else zero)
            place = m + 2 - n
            behind.append(weights[place] if 0 <= place < 5 else zero)
        f = jnp.where(two, ahead[2], jnp.where(one, ahead[1], ahead[0]))
        b = jnp.where(two, behind[2], jnp.where(one, behind[1], behind[0]))
        if m == -1:
            f = f + jnp.where(some, 0.5, 0.0)
        if m == -2:
            f = f + jnp.where(two, 0.5, 0.0)
        if m == 0:
            b = b - jnp.where(some, 0.5, 0.0)
        if m == 1:
            b = b - jnp.where(two, 0.5, 0.0)
        taps[m] = jnp.where(forward, f, b)
    return taps


def difference_taps(here, ahead, reach):
    out = {}
    for m in range(-reach, reach + 1):
        if m in here and m - 1 in ahead:
            out[m] = here[m] - ahead[m - 1]
        elif m in here:
            out[m] = here[m]
        else:
            out[m] = -ahead[m - 1]
    return out


def north_coefficients(courant):
    count = courant.shape[0]
    row = row_index(courant.shape)
    here = north_taps(jnp.where(row == 0, 0.0, courant))
    taps = difference_taps(here, {m: rows(here[m], -1) for m in here}, 3)
    return [
        jnp.where((row + m >= 0) & (row + m < count), taps[m], 0.0) for m in range(-3, 4)
    ]


def pick(x, index):
    return jnp.take_along_axis(x, index, axis=1, mode="promise_in_bounds")


def position():
    return lax.axis_index("tracer")


def tile():
    return lax.axis_index("space")


def early_levels(levels):
    return jnp.clip(levels - tile(), 0, levels - 1)


def prepare_kernel(*refs):
    sources, (keep, send, *fields, sems) = refs[:6], refs[6:]
    copies = [
        pltpu.make_async_copy(source, place, sems.at[k])
        for k, (source, place) in enumerate(zip(sources, fields))
    ]
    for copy in copies:
        copy.start()
    for copy in copies:
        copy.wait()
    thick, fe, fn, ce, cn, ne = fields
    core = position() % 2
    levels, count, width = thick.shape[1:]
    lane = lane_index((count, width))
    row = row_index((count, width))
    half_lane = lane_index((count // 2, width))
    folded = jnp.zeros((count // 2, width), jnp.float32)
    for l in range(levels):
        east_mass = fe[0, l]
        north_mass = jnp.where(row == 0, 0.0, fn[0, l])
        thickness = (
            thick[0, l]
            + (east_mass - jnp.where(lane == width - 1, 0.0, lanes(east_mass, -1)))
            + (north_mass - rows(north_mass, -1))
        )
        whole = ne[0, l].astype(jnp.float32)
        first = (thickness, ce[0, l])
        second = (cn[0, l], whole)
        for k in range(2):
            start = (k * levels + l) * count
            keep[start : start + count, :] = jnp.where(core == 0, first[k], second[k])
            send[start : start + count, :] = jnp.where(core == 0, second[k], first[k])
        for part, start in enumerate((MET_SEG * l, MET_SEG * (levels + l))):
            here = slice(part * count // 2, (part + 1) * count // 2)
            inside = (half_lane >= start) & (half_lane < start + SEG)
            folded = jnp.where(inside, lanes(cn[0, l, here, :], start + EDGE), folded)
            for k, value in enumerate((ce[0, l, here, :], whole[here], east_mass[here])):
                at = start + SEG + k
                folded = jnp.where(half_lane == at, lanes(value, at), folded)
    base = 2 * levels * count
    keep[base:, :] = folded
    send[base:, :] = folded


def prepare(thick, fe, fn, ce, cn, ne):
    levels, count, width = thick.shape[1:]
    vmem = pl.BlockSpec(memory_space=pltpu.VMEM)
    half = pltpu.VMEM((2 * levels * count + count // 2, width), jnp.float32)
    return pl.pallas_call(
        prepare_kernel,
        out_shape=(half, half),
        in_specs=[pl.BlockSpec(memory_space=pl.ANY)] * 6,
        out_specs=(vmem, vmem),
        scratch_shapes=[pltpu.VMEM(thick.shape, jnp.float32)] * 5
        + [pltpu.VMEM(ne.shape, jnp.int32), pltpu.SemaphoreType.DMA((6,))],
        name="prepare",
    )(thick, fe, fn, ce, cn, ne)


def pack_kernel(mass, last, first):
    tracers, levels, count, width = mass.shape
    lane = lane_index((count, width))

    def level(l, carry):
        a = jnp.zeros((count, width), jnp.float32)
        b = a
        for t in range(tracers):
            inside = (lane >= EDGE * t) & (lane < EDGE * (t + 1))
            a = jnp.where(inside, lanes(mass[t, l], EDGE * (t + 1)), a)
            b = jnp.where(inside, lanes(mass[t, l], EDGE * t), b)
        place = pl.ds(pl.multiple_of(l * count, count), count)
        last[place, :] = a
        first[place, :] = b
        return carry

    lax.fori_loop(0, levels, level, 0)


def copies_kernel(mass, padded, moved):
    tracers, levels, count, width = mass.shape
    zero_rows = jnp.zeros((PAD, width), jnp.float32)

    def level(l, carry):
        for t in range(tracers):
            value = mass[t, l]
            padded[t, l, :PAD, :] = zero_rows
            padded[t, l, PAD : PAD + count, :] = value
            padded[t, l, PAD + count :, :] = zero_rows
            for k, shift in enumerate(NEAR):
                moved[k, t, l] = lanes(value, -shift)
        return carry

    lax.fori_loop(0, levels, level, 0)


def in_vmem(kernel, name, shapes, *operands):
    vmem = pl.BlockSpec(memory_space=pltpu.VMEM)
    return pl.pallas_call(
        kernel,
        out_shape=tuple(pltpu.VMEM(shape, jnp.float32) for shape in shapes),
        in_specs=[vmem] * len(operands),
        out_specs=(vmem,) * len(shapes),
        compiler_params=pltpu.CompilerParams(vmem_limit_bytes=24 * 1024 * 1024),
        cost_estimate=pl.CostEstimate(flops=2000000, bytes_accessed=1000000, transcendentals=0),
        name=name,
    )(*operands)


def pack(mass):
    _, levels, count, width = mass.shape
    return in_vmem(pack_kernel, "pack", ((levels * count, width),) * 2, mass)


def copies(mass):
    tracers, levels, count, width = mass.shape
    padded = (tracers, levels, count + 2 * PAD, width)
    return in_vmem(copies_kernel, "copies", (padded, (len(NEAR),) + mass.shape), mass)


def segments(shape):
    lane = lane_index(shape)
    segment = sum(
        ((lane >= SEG * k).astype(jnp.int32) for k in range(1, PACK)), jnp.zeros(shape, jnp.int32)
    )
    return segment, lane - SEG * segment, lane < SEG * PACK


def moved_places(held):
    return {shift: lanes(held, shift) if shift else held for shift in (-STEP, 0, STEP)}


def east_parts(taps, near, parts=None):
    parts = dict(parts or {})
    for m in taps:
        shift = east_group(m)
        term = taps[m] * near[m - shift]
        parts[shift] = parts[shift] + term if shift in parts else term
    return parts


def moved_sum(parts):
    return parts[0] + (lanes(parts[-STEP], STEP) + lanes(parts[STEP], -STEP))


def near_cells(x):
    return {0: x, **{shift: lanes(x, -shift) for shift in NEAR}}


def inner_kernel(span, mine, other, padded, shifted, *refs):
    low_level, high_level = span(refs[0].shape[1])

    @pl.when(low_level < high_level)
    def _():
        inner_body(low_level, high_level, mine, other, padded, shifted, *refs)


def inner_body(
    low_level, high_level, mine, other, padded, shifted, sums, outer_c, edge_c, thickness,
    east_c, north_c, inners, middle, partial,
):
    tracers, levels, count, width = sums.shape
    shape = (count, width)
    lane = lane_index(shape)
    low = position() % 2 == 0
    _, in_segment, packed_lane = segments(shape)
    zero_rows = jnp.zeros((PAD, width), jnp.float32)
    for slot in range(2):
        for j in range(GROUP):
            middle[slot, j, :PAD, :] = zero_rows
            middle[slot, j, PAD + count :, :] = zero_rows
    edge_index = jnp.where(packed_lane, in_segment + (width - EDGE), 0)
    edge_index = jnp.where(edge_index >= width, edge_index - width, edge_index)
    moved_index = moved_places(edge_index)
    moved_segment = moved_places(jnp.where(packed_lane, in_segment, -2 * SEG))

    def level(l, carry):
        fields = []
        for half in range(2):
            for k in range(2):
                place = pl.ds(pl.multiple_of((k * levels + l) * count, count), count)
                a = mine[place, :]
                b = other[place, :]
                fields.append(jnp.where(low, a, b) if half == 0 else jnp.where(low, b, a))
        thick, east_courant, north_courant, whole = fields
        thickness[l] = thick
        here = east_taps(east_courant, whole)
        ahead = {m: jnp.where(lane == width - 1, 0.0, lanes(here[m], -1)) for m in here}
        taps = difference_taps(here, ahead, EDGE)
        for m in range(-EDGE, EDGE + 1):
            value = taps[m]
            if m != 0:
                q = moved_segment[east_group(m)]
                crosses = ((q < EDGE) != (q + m < EDGE)) & (q >= 0)
                outer_c[m + EDGE, l] = jnp.where(crosses, pick(value, moved_index[east_group(m)]), 0.0)
            if m < 0:
                value = jnp.where(lane >= -m, value, 0.0)
            if m > 0:
                value = jnp.where(lane < width - m, value, 0.0)
            shift = east_group(m)
            east_c[m + EDGE, l] = lanes(value, shift) if shift else value
        for m, value in enumerate(north_coefficients(north_courant)):
            north_c[m, l] = value
        for m, value in enumerate(north_coefficients(pick(north_courant, edge_index))):
            edge_c[m, l] = value
        return carry

    lax.fori_loop(low_level, high_level, level, 0)
    groups = tracers // GROUP

    def block(b):
        return slice(b * BLOCK, (b + 1) * BLOCK)

    def padded_block(b, m=0):
        return slice(PAD + b * BLOCK + m, PAD + (b + 1) * BLOCK + m)

    def place(step):
        step = jnp.clip(step, 0, levels * groups - 1)
        return step // groups, (step % groups) * GROUP

    def weights(ref, l, b, reach):
        return {m: ref[m + reach, l, block(b), :] for m in range(-reach, reach + 1)}

    def front(step):
        l, t0 = place(step)
        slot = (step + 2) % 2
        for b in range(count // BLOCK):
            taps = weights(east_c, l, b, EDGE)
            north = weights(north_c, l, b, 3)
            taps[0] = 1.0 + taps[0]
            north[0] = 1.0 + north[0]
            for j in range(GROUP):
                x = padded[t0 + j, l, padded_block(b), :]
                inner = north[0] * x
                for m in (-3, -2, -1, 1, 2, 3):
                    inner = inner + north[m] * padded[t0 + j, l, padded_block(b, m), :]
                inners[slot, j, block(b), :] = inner
                near = {0: x}
                for k, shift in enumerate(NEAR):
                    near[shift] = shifted[k, t0 + j, l, block(b), :]
                middle[slot, j, padded_block(b), :] = moved_sum(east_parts(taps, near))

    def back(step):
        l, t0 = place(step)
        slot = (step + 2) % 2
        for b in range(count // BLOCK):
            taps = weights(east_c, l, b, EDGE)
            north = weights(north_c, l, b, 3)
            for j in range(GROUP):
                parts = east_parts(taps, near_cells(inners[slot, j, block(b), :]))
                total = 0.5 * padded[t0 + j, l, padded_block(b), :] + parts[0]
                for m in range(-3, 4):
                    total = total + north[m] * middle[slot, j, padded_block(b, m), :]
                partial[slot, 0, j, block(b), :] = total
                partial[slot, 1, j, block(b), :] = parts[-STEP]
                partial[slot, 2, j, block(b), :] = parts[STEP]

    def finish(step):
        l, t0 = place(step)
        slot = (step + 2) % 2
        for b in range(count // BLOCK):
            for j in range(GROUP):
                sums[t0 + j, l, block(b), :] = partial[slot, 0, j, block(b), :] + (
                    lanes(partial[slot, 1, j, block(b), :], STEP)
                    + lanes(partial[slot, 2, j, block(b), :], -STEP)
                )

    def step_of_three(step, carry):
        finish(step - 1)
        back(step)
        front(step + 1)
        return carry

    front(low_level * groups)
    lax.fori_loop(low_level * groups, high_level * groups, step_of_three, 0)
    finish(high_level * groups - 1)


def inner_update(span, mine, other, padded, shifted):
    tracers, levels, count, width = shifted.shape[1:]
    vmem = pl.BlockSpec(memory_space=pltpu.VMEM)
    level = (levels, count, width)
    return pl.pallas_call(
        functools.partial(inner_kernel, span),
        out_shape=(
            pltpu.VMEM((tracers,) + level, jnp.float32),
            pltpu.VMEM((2 * EDGE + 1,) + level, jnp.float32),
            pltpu.VMEM((7,) + level, jnp.float32),
            pltpu.VMEM(level, jnp.float32),
        ),
        in_specs=[vmem] * 4,
        out_specs=(vmem,) * 4,
        scratch_shapes=[
            pltpu.VMEM((2 * EDGE + 1,) + level, jnp.float32),
            pltpu.VMEM((7,) + level, jnp.float32),
            pltpu.VMEM((2, GROUP, count, width), jnp.float32),
            pltpu.VMEM((2, GROUP, count + 2 * PAD, width), jnp.float32),
            pltpu.VMEM((2, 3, GROUP, count, width), jnp.float32),
        ],
        compiler_params=pltpu.CompilerParams(vmem_limit_bytes=24 * 1024 * 1024),
        cost_estimate=pl.CostEstimate(flops=20000000, bytes_accessed=6000000, transcendentals=0),
        name="inner",
    )(mine, other, padded, shifted)


def edge_kernel(west, east, own, *refs):
    before, after, (out, stage, sems) = refs[:4], refs[4:8], refs[8:]
    tracers, levels, count, width = stage.shape
    first_levels = early_levels(levels)
    shape = (count, width)
    lane = lane_index(shape)
    segment, in_segment, packed_lane = segments(shape)
    from_west_lane = in_segment < EDGE
    at_edge = (lane < EDGE) | (lane >= width - EDGE)
    last_face = {
        shift: q == EDGE - 1
        for shift, q in moved_places(jnp.where(packed_lane, in_segment, -2 * SEG)).items()
    }
    base = levels * count

    def unfolded(x):
        return jnp.concatenate([x, lanes(x, -MET_SEG * levels)])

    met_east = unfolded(east[base:, :])
    met_west = unfolded(west[base:, :])

    def copy(l, half):
        place = pl.ds(half * PACK, PACK)
        return pltpu.make_async_copy(stage.at[place, l], out.at[place, l], sems.at[l, half])

    def level(l, sums, outer_c, edge_c, thickness):
        level_rows = pl.ds(pl.multiple_of(l * count, count), count)
        met_lane = jnp.where(packed_lane, in_segment + MET_SEG * l, 0)
        met = jnp.where(lane - MET_SEG * l < EDGE, met_west, met_east)
        beyond = east_taps(
            pick(met_east, jnp.full(shape, SEG, jnp.int32) + MET_SEG * l),
            pick(met_east, jnp.full(shape, SEG + 1, jnp.int32) + MET_SEG * l),
        )
        mass_flux = pick(met_east, jnp.full(shape, SEG + 2, jnp.int32) + MET_SEG * l)
        inverse = 2.0 / (thickness[l] - jnp.where(lane == width - 1, mass_flux, 0.0))
        face = {
            m: jnp.where(last_face[east_group(m)], -beyond[m - 1], 0.0)
            for m in range(1 - EDGE, EDGE + 1)
        }
        outer = {m: outer_c[m + EDGE, l] for m in range(-EDGE, EDGE + 1) if m != 0}
        for m in range(1, EDGE + 1):
            outer[m] = outer[m] + face[m]
        inside = {m: face[m] for m in range(1 - EDGE, 1)}
        edge_taps = [edge_c[m, l] for m in range(7)]
        packed_taps = north_coefficients(pick(met, met_lane))
        for half in range(2):
            first_lane = EDGE * (segment + PACK * half) + in_segment
            west_index = jnp.where(packed_lane & from_west_lane, first_lane, 0)
            east_index = jnp.where(packed_lane & ~from_west_lane, first_lane - EDGE, 0)
            own_cells = pick(own[level_rows, :], west_index)
            cells = jnp.where(
                from_west_lane,
                pick(west[level_rows, :], west_index),
                pick(east[level_rows, :], east_index),
            )
            inner = cells
            own_inner = own_cells
            for m in range(-3, 4):
                inner = inner + packed_taps[m + 3] * rows(cells, -m)
                own_inner = own_inner + edge_taps[m + 3] * rows(own_cells, -m)
            first = moved_sum(
                east_parts(inside, near_cells(own_cells), east_parts(outer, near_cells(cells)))
            )
            total = moved_sum(
                east_parts(inside, near_cells(own_inner), east_parts(outer, near_cells(inner)))
            )
            for m in range(-3, 4):
                total = total + edge_taps[m + 3] * rows(first, -m)
            for k in range(PACK):
                t = half * PACK + k
                moved = jnp.where(at_edge, lanes(total, width - EDGE - SEG * k), 0.0)
                stage[t, l] = (sums[t, l] + moved) * inverse
            copy(l, half).start()

    def either(l, carry):
        @pl.when(l < first_levels)
        def _():
            level(l, *before)

        @pl.when(l >= first_levels)
        def _():
            level(l, *after)

        return carry

    lax.fori_loop(0, levels, either, 0)
    for l in range(levels):
        for half in range(2):
            copy(l, half).wait()


def edge_update(west, east, own, before, after):
    sums = before[0]
    tracers, levels, count, width = sums.shape
    vmem = pl.BlockSpec(memory_space=pltpu.VMEM)
    return pl.pallas_call(
        edge_kernel,
        out_shape=jax.ShapeDtypeStruct(sums.shape, jnp.float32),
        in_specs=[vmem] * 11,
        out_specs=pl.BlockSpec(memory_space=pl.ANY),
        scratch_shapes=[pltpu.VMEM(sums.shape, jnp.float32), pltpu.SemaphoreType.DMA((levels, 2))],
        compiler_params=pltpu.CompilerParams(vmem_limit_bytes=24 * 1024 * 1024),
        name="edges",
    )(west, east, own, *before, *after)


def east_group(m):
    return -STEP if m < -1 else (STEP if m > 2 else 0)


def along(x, pairs):
    return lax.ppermute(x, "space", pairs)


def exchange(x, flip):
    size = lax.axis_size("tracer")
    return lax.ppermute(x, "tracer", [(i, i ^ flip) for i in range(size)])


def turn(x, by):
    size = lax.axis_size("tracer")
    return lax.ppermute(x, "tracer", [(i, i // 8 * 8 + (i + 2 * by) % 8) for i in range(size)])


def shards(mass, thick, fe, fn, ce, cn, ne, owner):
    keep, send = prepare(thick, fe, fn, ce, cn, ne)
    last, first = pack(mass)
    me, chosen = position(), owner[0]
    other_core = exchange(send, 1)
    total = jnp.where(chosen == me, keep, jnp.where(chosen == me ^ 1, other_core, 0.0))
    total = total + turn(total, 2) + turn(total, -1) + turn(total, 1)
    total, last, first = lax.optimization_barrier((total, last, first))
    total = total + exchange(total, 8)
    padded, shifted = copies(mass)
    main = 2 * mass.shape[1] * mass.shape[2]
    mine = total[:main]
    edges = total[main:]
    size = lax.axis_size("space")
    to_east = jnp.concatenate([last, edges])
    to_west = jnp.concatenate([first, edges])
    west = along(to_east, [(i, (i + 1) % size) for i in range(size)])
    other = exchange(mine, 1)
    before = inner_update(lambda levels: (0, early_levels(levels)), mine, other, padded, shifted)
    to_west, before = lax.optimization_barrier((to_west, before))
    east = along(to_west, [(i, (i - 1) % size) for i in range(size)])
    after = inner_update(lambda levels: (early_levels(levels), levels), mine, other, padded, shifted)
    return edge_update(west, east, last, before, after)


def solution(mesh):
    spec = P("tracer", None, None, "space")
    return jax.shard_map(
        shards, mesh=mesh, in_specs=(spec,) * 7 + (P("space"),), out_specs=spec, check_vma=False
    )
```

```python
import functools

import jax
import jax.numpy as jnp
from jax import lax
from jax.experimental import pallas as pl
from jax.experimental.pallas import tpu as pltpu
from jax.sharding import PartitionSpec as P

NS = 2
EDGE = NS + 3
SEG = 2 * EDGE
PACK = 9
STEP = 4
GROUP = 3
PAD = 8
BLOCK = 8
NEAR = (-1, 1, 2)
MET_SEG = 16


def lane_index(shape):
    return lax.broadcasted_iota(jnp.int32, shape, len(shape) - 1)


def row_index(shape):
    return lax.broadcasted_iota(jnp.int32, shape, len(shape) - 2)


def lanes(x, shift):
    return pltpu.roll(x, shift % x.shape[-1], x.ndim - 1)


def rows(x, shift):
    return pltpu.roll(x, shift % x.shape[-2], x.ndim - 2)


def face_weights(courant):
    fraction = jnp.abs(courant)
    ramp = 1.5 * fraction * (1.0 - 2.0 / 3.0 * fraction)
    near = 0.5 * courant * (1.0 - 0.5 * fraction - ramp)
    far = 0.5 * courant * (0.5 * fraction - ramp)
    mean = courant * ramp
    far_outer = far * (1.0 / 12.0)
    near_outer = near * (1.0 / 12.0)
    return (
        -near_outer,
        7.0 * near_outer - far_outer,
        7.0 * (near_outer + far_outer) + mean,
        7.0 * far_outer - near_outer,
        -far_outer,
    )


def north_taps(courant):
    down1, up0, up1, up2, up3 = (w for w in face_weights(courant))
    forward = courant >= 0.0
    zero = jnp.zeros_like(courant)
    f = {1: down1, 0: up0, -1: up1, -2: up2, -3: up3}
    b = {-2: down1, -1: up0, 0: up1, 1: up2, 2: up3}
    return {m: jnp.where(forward, f.get(m, zero), b.get(m, zero)) for m in range(-3, 3)}


def east_taps(courant, whole):
    weights = face_weights(courant)
    forward = courant >= 0.0
    zero = jnp.zeros_like(courant)
    one = whole == 1.0
    two = whole == 2.0
    some = whole > 0.5
    taps = {}
    for m in range(-EDGE, EDGE):
        ahead = []
        behind = []
        for n in range(NS + 1):
            place = 1 - n - m
            ahead.append(weights[place] if 0 <= place < 5 else zero)
            place = m + 2 - n
            behind.append(weights[place] if 0 <= place < 5 else zero)
        f = jnp.where(two, ahead[2], jnp.where(one, ahead[1], ahead[0]))
        b = jnp.where(two, behind[2], jnp.where(one, behind[1], behind[0]))
        if m == -1:
            f = f + jnp.where(some, 0.5, 0.0)
        if m == -2:
            f = f + jnp.where(two, 0.5, 0.0)
        if m == 0:
            b = b - jnp.where(some, 0.5, 0.0)
        if m == 1:
            b = b - jnp.where(two, 0.5, 0.0)
        taps[m] = jnp.where(forward, f, b)
    return taps


def difference_taps(here, ahead, reach):
    out = {}
    for m in range(-reach, reach + 1):
        if m in here and m - 1 in ahead:
            out[m] = here[m] - ahead[m - 1]
        elif m in here:
            out[m] = here[m]
        else:
            out[m] = -ahead[m - 1]
    return out


def north_coefficients(courant):
    count = courant.shape[0]
    row = row_index(courant.shape)
    here = north_taps(jnp.where(row == 0, 0.0, courant))
    taps = difference_taps(here, {m: rows(here[m], -1) for m in here}, 3)
    return [
        jnp.where((row + m >= 0) & (row + m < count), taps[m], 0.0) for m in range(-3, 4)
    ]


def pick(x, index):
    return jnp.take_along_axis(x, index, axis=1, mode="promise_in_bounds")


def position():
    return lax.axis_index("tracer")


def tile():
    return lax.axis_index("space")


def early_parts(levels):
    return jnp.clip(levels + 1 - tile(), 0, levels)


def prepare_kernel(*refs):
    sources, (keep, send, *fields, sems) = refs[:6], refs[6:]
    copies = [
        pltpu.make_async_copy(source, place, sems.at[k])
        for k, (source, place) in enumerate(zip(sources, fields))
    ]
    for copy in copies:
        copy.start()
    for copy in copies:
        copy.wait()
    thick, fe, fn, ce, cn, ne = fields
    core = position() % 2
    levels, count, width = thick.shape[1:]
    lane = lane_index((count, width))
    row = row_index((count, width))
    half_lane = lane_index((count // 2, width))
    folded = jnp.zeros((count // 2, width), jnp.float32)
    for l in range(levels):
        east_mass = fe[0, l]
        north_mass = jnp.where(row == 0, 0.0, fn[0, l])
        thickness = (
            thick[0, l]
            + (east_mass - jnp.where(lane == width - 1, 0.0, lanes(east_mass, -1)))
            + (north_mass - rows(north_mass, -1))
        )
        whole = ne[0, l].astype(jnp.float32)
        first = (thickness, ce[0, l])
        second = (cn[0, l], whole)
        for k in range(2):
            start = (k * levels + l) * count
            keep[start : start + count, :] = jnp.where(core == 0, first[k], second[k])
            send[start : start + count, :] = jnp.where(core == 0, second[k], first[k])
        for part, start in enumerate((MET_SEG * l, MET_SEG * (levels + l))):
            here = slice(part * count // 2, (part + 1) * count // 2)
            inside = (half_lane >= start) & (half_lane < start + SEG)
            folded = jnp.where(inside, lanes(cn[0, l, here, :], start + EDGE), folded)
            for k, value in enumerate((ce[0, l, here, :], whole[here], east_mass[here])):
                at = start + SEG + k
                folded = jnp.where(half_lane == at, lanes(value, at), folded)
    base = 2 * levels * count
    keep[base:, :] = folded
    send[base:, :] = folded


def prepare(thick, fe, fn, ce, cn, ne):
    levels, count, width = thick.shape[1:]
    vmem = pl.BlockSpec(memory_space=pltpu.VMEM)
    half = pltpu.VMEM((2 * levels * count + count // 2, width), jnp.float32)
    return pl.pallas_call(
        prepare_kernel,
        out_shape=(half, half),
        in_specs=[pl.BlockSpec(memory_space=pl.ANY)] * 6,
        out_specs=(vmem, vmem),
        scratch_shapes=[pltpu.VMEM(thick.shape, jnp.float32)] * 5
        + [pltpu.VMEM(ne.shape, jnp.int32), pltpu.SemaphoreType.DMA((6,))],
        name="prepare",
    )(thick, fe, fn, ce, cn, ne)


def pack_kernel(mass, last, first):
    tracers, levels, count, width = mass.shape
    lane = lane_index((count, width))

    def level(l, carry):
        a = jnp.zeros((count, width), jnp.float32)
        b = a
        for t in range(tracers):
            inside = (lane >= EDGE * t) & (lane < EDGE * (t + 1))
            a = jnp.where(inside, lanes(mass[t, l], EDGE * (t + 1)), a)
            b = jnp.where(inside, lanes(mass[t, l], EDGE * t), b)
        place = pl.ds(pl.multiple_of(l * count, count), count)
        last[place, :] = a
        first[place, :] = b
        return carry

    lax.fori_loop(0, levels, level, 0)


def copies_kernel(mass, padded, moved):
    tracers, levels, count, width = mass.shape
    zero_rows = jnp.zeros((PAD, width), jnp.float32)

    def level(l, carry):
        for t in range(tracers):
            value = mass[t, l]
            padded[t, l, :PAD, :] = zero_rows
            padded[t, l, PAD : PAD + count, :] = value
            padded[t, l, PAD + count :, :] = zero_rows
            for k, shift in enumerate(NEAR):
                moved[k, t, l] = lanes(value, -shift)
        return carry

    lax.fori_loop(0, levels, level, 0)


def in_vmem(kernel, name, shapes, *operands):
    vmem = pl.BlockSpec(memory_space=pltpu.VMEM)
    return pl.pallas_call(
        kernel,
        out_shape=tuple(pltpu.VMEM(shape, jnp.float32) for shape in shapes),
        in_specs=[vmem] * len(operands),
        out_specs=(vmem,) * len(shapes),
        compiler_params=pltpu.CompilerParams(vmem_limit_bytes=24 * 1024 * 1024),
        cost_estimate=pl.CostEstimate(flops=2000000, bytes_accessed=1000000, transcendentals=0),
        name=name,
    )(*operands)


def pack(mass):
    _, levels, count, width = mass.shape
    return in_vmem(pack_kernel, "pack", ((levels * count, width),) * 2, mass)


def copies(mass):
    tracers, levels, count, width = mass.shape
    padded = (tracers, levels, count + 2 * PAD, width)
    return in_vmem(copies_kernel, "copies", (padded, (len(NEAR),) + mass.shape), mass)


def segments(shape):
    lane = lane_index(shape)
    segment = sum(
        ((lane >= SEG * k).astype(jnp.int32) for k in range(1, PACK)), jnp.zeros(shape, jnp.int32)
    )
    return segment, lane - SEG * segment, lane < SEG * PACK


def moved_places(held):
    return {shift: lanes(held, shift) if shift else held for shift in (-STEP, 0, STEP)}


def east_parts(taps, near, parts=None):
    parts = dict(parts or {})
    for m in taps:
        shift = east_group(m)
        term = taps[m] * near[m - shift]
        parts[shift] = parts[shift] + term if shift in parts else term
    return parts


def moved_sum(parts):
    return parts[0] + (lanes(parts[-STEP], STEP) + lanes(parts[STEP], -STEP))


def near_cells(x):
    return {0: x, **{shift: lanes(x, -shift) for shift in NEAR}}


def inner_kernel(span, mine, other, padded, shifted, *refs):
    low_part, high_part = span(refs[0].shape[1])

    @pl.when(low_part < high_part)
    def _():
        inner_body(low_part, high_part, mine, other, padded, shifted, *refs)


def inner_body(
    low_part, high_part, mine, other, padded, shifted, sums, outer_c, edge_c, thickness,
    east_c, north_c, inners, middle, partial,
):
    tracers, levels, count, width = sums.shape
    shape = (count, width)
    lane = lane_index(shape)
    low = position() % 2 == 0
    _, in_segment, packed_lane = segments(shape)
    zero_rows = jnp.zeros((PAD, width), jnp.float32)
    for slot in range(2):
        for j in range(GROUP):
            middle[slot, j, :PAD, :] = zero_rows
            middle[slot, j, PAD + count :, :] = zero_rows
    edge_index = jnp.where(packed_lane, in_segment + (width - EDGE), 0)
    edge_index = jnp.where(edge_index >= width, edge_index - width, edge_index)
    moved_index = moved_places(edge_index)
    moved_segment = moved_places(jnp.where(packed_lane, in_segment, -2 * SEG))

    def level(l, carry):
        fields = []
        for half in range(2):
            for k in range(2):
                place = pl.ds(pl.multiple_of((k * levels + l) * count, count), count)
                a = mine[place, :]
                b = other[place, :]
                fields.append(jnp.where(low, a, b) if half == 0 else jnp.where(low, b, a))
        thick, east_courant, north_courant, whole = fields
        thickness[l] = thick
        here = east_taps(east_courant, whole)
        ahead = {m: jnp.where(lane == width - 1, 0.0, lanes(here[m], -1)) for m in here}
        taps = difference_taps(here, ahead, EDGE)
        for m in range(-EDGE, EDGE + 1):
            value = taps[m]
            if m != 0:
                q = moved_segment[east_group(m)]
                crosses = ((q < EDGE) != (q + m < EDGE)) & (q >= 0)
                outer_c[m + EDGE, l] = jnp.where(crosses, pick(value, moved_index[east_group(m)]), 0.0)
            if m < 0:
                value = jnp.where(lane >= -m, value, 0.0)
            if m > 0:
                value = jnp.where(lane < width - m, value, 0.0)
            shift = east_group(m)
            east_c[m + EDGE, l] = lanes(value, shift) if shift else value
        for m, value in enumerate(north_coefficients(north_courant)):
            north_c[m, l] = value
        for m, value in enumerate(north_coefficients(pick(north_courant, edge_index))):
            edge_c[m, l] = value
        return carry

    lax.fori_loop(low_part // 2, (high_part + 1) // 2, level, 0)
    groups = tracers // GROUP
    low_step, high_step = low_part * (groups // 2), high_part * (groups // 2)

    def block(b):
        return slice(b * BLOCK, (b + 1) * BLOCK)

    def padded_block(b, m=0):
        return slice(PAD + b * BLOCK + m, PAD + (b + 1) * BLOCK + m)

    def place(step):
        step = jnp.clip(step, 0, levels * groups - 1)
        return step // groups, (step % groups) * GROUP

    def weights(ref, l, b, reach):
        return {m: ref[m + reach, l, block(b), :] for m in range(-reach, reach + 1)}

    def front(step):
        l, t0 = place(step)
        slot = (step + 2) % 2
        for b in range(count // BLOCK):
            taps = weights(east_c, l, b, EDGE)
            north = weights(north_c, l, b, 3)
            taps[0] = 1.0 + taps[0]
            north[0] = 1.0 + north[0]
            for j in range(GROUP):
                x = padded[t0 + j, l, padded_block(b), :]
                inner = north[0] * x
                for m in (-3, -2, -1, 1, 2, 3):
                    inner = inner + north[m] * padded[t0 + j, l, padded_block(b, m), :]
                inners[slot, j, block(b), :] = inner
                near = {0: x}
                for k, shift in enumerate(NEAR):
                    near[shift] = shifted[k, t0 + j, l, block(b), :]
                middle[slot, j, padded_block(b), :] = moved_sum(east_parts(taps, near))

    def back(step):
        l, t0 = place(step)
        slot = (step + 2) % 2
        for b in range(count // BLOCK):
            taps = weights(east_c, l, b, EDGE)
            north = weights(north_c, l, b, 3)
            for j in range(GROUP):
                parts = east_parts(taps, near_cells(inners[slot, j, block(b), :]))
                total = 0.5 * padded[t0 + j, l, padded_block(b), :] + parts[0]
                for m in range(-3, 4):
                    total = total + north[m] * middle[slot, j, padded_block(b, m), :]
                partial[slot, 0, j, block(b), :] = total
                partial[slot, 1, j, block(b), :] = parts[-STEP]
                partial[slot, 2, j, block(b), :] = parts[STEP]

    def finish(step):
        l, t0 = place(step)
        slot = (step + 2) % 2
        for b in range(count // BLOCK):
            for j in range(GROUP):
                sums[t0 + j, l, block(b), :] = partial[slot, 0, j, block(b), :] + (
                    lanes(partial[slot, 1, j, block(b), :], STEP)
                    + lanes(partial[slot, 2, j, block(b), :], -STEP)
                )

    def step_of_three(step, carry):
        finish(step - 1)
        back(step)
        front(step + 1)
        return carry

    front(low_step)
    lax.fori_loop(low_step, high_step, step_of_three, 0)
    finish(high_step - 1)


def inner_update(span, mine, other, padded, shifted):
    tracers, levels, count, width = shifted.shape[1:]
    vmem = pl.BlockSpec(memory_space=pltpu.VMEM)
    level = (levels, count, width)
    return pl.pallas_call(
        functools.partial(inner_kernel, span),
        out_shape=(
            pltpu.VMEM((tracers,) + level, jnp.float32),
            pltpu.VMEM((2 * EDGE + 1,) + level, jnp.float32),
            pltpu.VMEM((7,) + level, jnp.float32),
            pltpu.VMEM(level, jnp.float32),
        ),
        in_specs=[vmem] * 4,
        out_specs=(vmem,) * 4,
        scratch_shapes=[
            pltpu.VMEM((2 * EDGE + 1,) + level, jnp.float32),
            pltpu.VMEM((7,) + level, jnp.float32),
            pltpu.VMEM((2, GROUP, count, width), jnp.float32),
            pltpu.VMEM((2, GROUP, count + 2 * PAD, width), jnp.float32),
            pltpu.VMEM((2, 3, GROUP, count, width), jnp.float32),
        ],
        compiler_params=pltpu.CompilerParams(vmem_limit_bytes=24 * 1024 * 1024),
        cost_estimate=pl.CostEstimate(flops=20000000, bytes_accessed=6000000, transcendentals=0),
        name="inner",
    )(mine, other, padded, shifted)


def edge_kernel(west, east, own, *refs):
    before, after, (out, stage, sems) = refs[:4], refs[4:8], refs[8:]
    tracers, levels, count, width = stage.shape
    early = early_parts(levels)
    shape = (count, width)
    lane = lane_index(shape)
    segment, in_segment, packed_lane = segments(shape)
    from_west_lane = in_segment < EDGE
    at_edge = (lane < EDGE) | (lane >= width - EDGE)
    last_face = {
        shift: q == EDGE - 1
        for shift, q in moved_places(jnp.where(packed_lane, in_segment, -2 * SEG)).items()
    }
    base = levels * count

    def unfolded(x):
        return jnp.concatenate([x, lanes(x, -MET_SEG * levels)])

    met_east = unfolded(east[base:, :])
    met_west = unfolded(west[base:, :])

    def copy(l, half):
        place = pl.ds(half * PACK, PACK)
        return pltpu.make_async_copy(stage.at[place, l], out.at[place, l], sems.at[l, half])

    def level(l, sums, outer_c, edge_c, thickness):
        level_rows = pl.ds(pl.multiple_of(l * count, count), count)
        met_lane = jnp.where(packed_lane, in_segment + MET_SEG * l, 0)
        met = jnp.where(lane - MET_SEG * l < EDGE, met_west, met_east)
        beyond = east_taps(
            pick(met_east, jnp.full(shape, SEG, jnp.int32) + MET_SEG * l),
            pick(met_east, jnp.full(shape, SEG + 1, jnp.int32) + MET_SEG * l),
        )
        mass_flux = pick(met_east, jnp.full(shape, SEG + 2, jnp.int32) + MET_SEG * l)
        inverse = 2.0 / (thickness[l] - jnp.where(lane == width - 1, mass_flux, 0.0))
        face = {
            m: jnp.where(last_face[east_group(m)], -beyond[m - 1], 0.0)
            for m in range(1 - EDGE, EDGE + 1)
        }
        outer = {m: outer_c[m + EDGE, l] for m in range(-EDGE, EDGE + 1) if m != 0}
        for m in range(1, EDGE + 1):
            outer[m] = outer[m] + face[m]
        inside = {m: face[m] for m in range(1 - EDGE, 1)}
        edge_taps = [edge_c[m, l] for m in range(7)]
        packed_taps = north_coefficients(pick(met, met_lane))
        for half in range(2):
            first_lane = EDGE * (segment + PACK * half) + in_segment
            west_index = jnp.where(packed_lane & from_west_lane, first_lane, 0)
            east_index = jnp.where(packed_lane & ~from_west_lane, first_lane - EDGE, 0)
            own_cells = pick(own[level_rows, :], west_index)
            cells = jnp.where(
                from_west_lane,
                pick(west[level_rows, :], west_index),
                pick(east[level_rows, :], east_index),
            )
            inner = cells
            own_inner = own_cells
            for m in range(-3, 4):
                inner = inner + packed_taps[m + 3] * rows(cells, -m)
                own_inner = own_inner + edge_taps[m + 3] * rows(own_cells, -m)
            first = moved_sum(
                east_parts(inside, near_cells(own_cells), east_parts(outer, near_cells(cells)))
            )
            total = moved_sum(
                east_parts(inside, near_cells(own_inner), east_parts(outer, near_cells(inner)))
            )
            for m in range(-3, 4):
                total = total + edge_taps[m + 3] * rows(first, -m)
            for k in range(PACK):
                t = half * PACK + k
                moved = jnp.where(at_edge, lanes(total, width - EDGE - SEG * k), 0.0)
                stage[t, l] = (sums(t, l, half) + moved) * inverse
            copy(l, half).start()

    def sums_after(t, l, half):
        value = after[0][t, l]
        return value if half else jnp.where(2 * l < early, before[0][t, l], value)

    def either(l, carry):
        @pl.when(2 * l + 1 < early)
        def _():
            level(l, lambda t, l, half: before[0][t, l], *before[1:])

        @pl.when(2 * l + 1 >= early)
        def _():
            level(l, sums_after, *after[1:])

        return carry

    lax.fori_loop(0, levels, either, 0)
    for l in range(levels):
        for half in range(2):
            copy(l, half).wait()


def edge_update(west, east, own, before, after):
    sums = before[0]
    tracers, levels, count, width = sums.shape
    vmem = pl.BlockSpec(memory_space=pltpu.VMEM)
    return pl.pallas_call(
        edge_kernel,
        out_shape=jax.ShapeDtypeStruct(sums.shape, jnp.float32),
        in_specs=[vmem] * 11,
        out_specs=pl.BlockSpec(memory_space=pl.ANY),
        scratch_shapes=[pltpu.VMEM(sums.shape, jnp.float32), pltpu.SemaphoreType.DMA((levels, 2))],
        compiler_params=pltpu.CompilerParams(vmem_limit_bytes=24 * 1024 * 1024),
        name="edges",
    )(west, east, own, *before, *after)


def east_group(m):
    return -STEP if m < -1 else (STEP if m > 2 else 0)


def along(x, pairs):
    return lax.ppermute(x, "space", pairs)


def exchange(x, flip):
    size = lax.axis_size("tracer")
    return lax.ppermute(x, "tracer", [(i, i ^ flip) for i in range(size)])


def turn(x, by):
    size = lax.axis_size("tracer")
    return lax.ppermute(x, "tracer", [(i, i // 8 * 8 + (i + 2 * by) % 8) for i in range(size)])


def shards(mass, thick, fe, fn, ce, cn, ne, owner):
    keep, send = prepare(thick, fe, fn, ce, cn, ne)
    last, first = pack(mass)
    me, chosen = position(), owner[0]
    other_core = exchange(send, 1)
    total = jnp.where(chosen == me, keep, jnp.where(chosen == me ^ 1, other_core, 0.0))
    total = total + (turn(total, 1) + turn(total, -1) + turn(total, 2))
    total, last, first = lax.optimization_barrier((total, last, first))
    total = total + exchange(total, 8)
    padded, shifted = copies(mass)
    main = 2 * mass.shape[1] * mass.shape[2]
    mine = total[:main]
    edges = total[main:]
    size = lax.axis_size("space")
    to_east = jnp.concatenate([last, edges])
    to_west = jnp.concatenate([first, edges])
    west = along(to_east, [(i, (i + 1) % size) for i in range(size)])
    other = exchange(mine, 1)
    before = inner_update(lambda levels: (0, early_parts(levels)), mine, other, padded, shifted)
    to_west, before = lax.optimization_barrier((to_west, before))
    east = along(to_west, [(i, (i - 1) % size) for i in range(size)])
    after = inner_update(lambda levels: (early_parts(levels), 2 * levels), mine, other, padded, shifted)
    return edge_update(west, east, last, before, after)


def solution(mesh):
    spec = P("tracer", None, None, "space")
    return jax.shard_map(
        shards, mesh=mesh, in_specs=(spec,) * 7 + (P("space"),), out_specs=spec, check_vma=False
    )
```

```python
import functools

import jax
import jax.numpy as jnp
from jax import lax
from jax.experimental import pallas as pl
from jax.experimental.pallas import tpu as pltpu
from jax.sharding import PartitionSpec as P

NS = 2
EDGE = NS + 3
SEG = 2 * EDGE
PACK = 9
STEP = 4
GROUP = 3
PAD = 8
BLOCK = 8
NEAR = (-1, 1, 2)
MET_SEG = 16


def lane_index(shape):
    return lax.broadcasted_iota(jnp.int32, shape, len(shape) - 1)


def row_index(shape):
    return lax.broadcasted_iota(jnp.int32, shape, len(shape) - 2)


def lanes(x, shift):
    return pltpu.roll(x, shift % x.shape[-1], x.ndim - 1)


def rows(x, shift):
    return pltpu.roll(x, shift % x.shape[-2], x.ndim - 2)


def face_weights(courant):
    fraction = jnp.abs(courant)
    ramp = 1.5 * fraction * (1.0 - 2.0 / 3.0 * fraction)
    near = 0.5 * courant * (1.0 - 0.5 * fraction - ramp)
    far = 0.5 * courant * (0.5 * fraction - ramp)
    mean = courant * ramp
    far_outer = far * (1.0 / 12.0)
    near_outer = near * (1.0 / 12.0)
    return (
        -near_outer,
        7.0 * near_outer - far_outer,
        7.0 * (near_outer + far_outer) + mean,
        7.0 * far_outer - near_outer,
        -far_outer,
    )


def north_taps(courant):
    down1, up0, up1, up2, up3 = (w for w in face_weights(courant))
    forward = courant >= 0.0
    zero = jnp.zeros_like(courant)
    f = {1: down1, 0: up0, -1: up1, -2: up2, -3: up3}
    b = {-2: down1, -1: up0, 0: up1, 1: up2, 2: up3}
    return {m: jnp.where(forward, f.get(m, zero), b.get(m, zero)) for m in range(-3, 3)}


def east_taps(courant, whole):
    weights = face_weights(courant)
    forward = courant >= 0.0
    zero = jnp.zeros_like(courant)
    one = whole == 1.0
    two = whole == 2.0
    some = whole > 0.5
    taps = {}
    for m in range(-EDGE, EDGE):
        ahead = []
        behind = []
        for n in range(NS + 1):
            place = 1 - n - m
            ahead.append(weights[place] if 0 <= place < 5 else zero)
            place = m + 2 - n
            behind.append(weights[place] if 0 <= place < 5 else zero)
        f = jnp.where(two, ahead[2], jnp.where(one, ahead[1], ahead[0]))
        b = jnp.where(two, behind[2], jnp.where(one, behind[1], behind[0]))
        if m == -1:
            f = f + jnp.where(some, 0.5, 0.0)
        if m == -2:
            f = f + jnp.where(two, 0.5, 0.0)
        if m == 0:
            b = b - jnp.where(some, 0.5, 0.0)
        if m == 1:
            b = b - jnp.where(two, 0.5, 0.0)
        taps[m] = jnp.where(forward, f, b)
    return taps


def difference_taps(here, ahead, reach):
    out = {}
    for m in range(-reach, reach + 1):
        if m in here and m - 1 in ahead:
            out[m] = here[m] - ahead[m - 1]
        elif m in here:
            out[m] = here[m]
        else:
            out[m] = -ahead[m - 1]
    return out


def north_coefficients(courant):
    count = courant.shape[0]
    row = row_index(courant.shape)
    here = north_taps(jnp.where(row == 0, 0.0, courant))
    taps = difference_taps(here, {m: rows(here[m], -1) for m in here}, 3)
    return [
        jnp.where((row + m >= 0) & (row + m < count), taps[m], 0.0) for m in range(-3, 4)
    ]


def pick(x, index):
    return jnp.take_along_axis(x, index, axis=1, mode="promise_in_bounds")


def position():
    return lax.axis_index("tracer")


def tile():
    return lax.axis_index("space")


def early_parts(levels):
    return jnp.clip(levels + 1 - tile(), 0, levels)


def prepare_kernel(*refs):
    sources, (keep, send, *fields, sems) = refs[:6], refs[6:]
    copies = [
        pltpu.make_async_copy(source, place, sems.at[k])
        for k, (source, place) in enumerate(zip(sources, fields))
    ]
    for copy in copies:
        copy.start()
    for copy in copies:
        copy.wait()
    thick, fe, fn, ce, cn, ne = fields
    core = position() % 2
    levels, count, width = thick.shape[1:]
    lane = lane_index((count, width))
    row = row_index((count, width))
    half_lane = lane_index((count // 2, width))
    folded = jnp.zeros((count // 2, width), jnp.float32)
    for l in range(levels):
        east_mass = fe[0, l]
        north_mass = jnp.where(row == 0, 0.0, fn[0, l])
        thickness = (
            thick[0, l]
            + (east_mass - jnp.where(lane == width - 1, 0.0, lanes(east_mass, -1)))
            + (north_mass - rows(north_mass, -1))
        )
        whole = ne[0, l].astype(jnp.float32)
        first = (thickness, ce[0, l])
        second = (cn[0, l], whole)
        for k in range(2):
            start = (k * levels + l) * count
            keep[start : start + count, :] = jnp.where(core == 0, first[k], second[k])
            send[start : start + count, :] = jnp.where(core == 0, second[k], first[k])
        for part, start in enumerate((MET_SEG * l, MET_SEG * (levels + l))):
            here = slice(part * count // 2, (part + 1) * count // 2)
            inside = (half_lane >= start) & (half_lane < start + SEG)
            folded = jnp.where(inside, lanes(cn[0, l, here, :], start + EDGE), folded)
            for k, value in enumerate((ce[0, l, here, :], whole[here], east_mass[here])):
                at = start + SEG + k
                folded = jnp.where(half_lane == at, lanes(value, at), folded)
    base = 2 * levels * count
    keep[base:, :] = folded
    send[base:, :] = folded


def prepare(thick, fe, fn, ce, cn, ne):
    levels, count, width = thick.shape[1:]
    vmem = pl.BlockSpec(memory_space=pltpu.VMEM)
    half = pltpu.VMEM((2 * levels * count + count // 2, width), jnp.float32)
    return pl.pallas_call(
        prepare_kernel,
        out_shape=(half, half),
        in_specs=[pl.BlockSpec(memory_space=pl.ANY)] * 6,
        out_specs=(vmem, vmem),
        scratch_shapes=[pltpu.VMEM(thick.shape, jnp.float32)] * 5
        + [pltpu.VMEM(ne.shape, jnp.int32), pltpu.SemaphoreType.DMA((6,))],
        name="prepare",
    )(thick, fe, fn, ce, cn, ne)


def pack_kernel(mass, last, first):
    tracers, levels, count, width = mass.shape
    lane = lane_index((count, width))

    def level(l, carry):
        a = jnp.zeros((count, width), jnp.float32)
        b = a
        for t in range(tracers):
            inside = (lane >= EDGE * t) & (lane < EDGE * (t + 1))
            a = jnp.where(inside, lanes(mass[t, l], EDGE * (t + 1)), a)
            b = jnp.where(inside, lanes(mass[t, l], EDGE * t), b)
        place = pl.ds(pl.multiple_of(l * count, count), count)
        last[place, :] = a
        first[place, :] = b
        return carry

    lax.fori_loop(0, levels, level, 0)


def copies_kernel(mass, padded, moved):
    tracers, levels, count, width = mass.shape
    zero_rows = jnp.zeros((PAD, width), jnp.float32)

    def level(l, carry):
        for t in range(tracers):
            value = mass[t, l]
            padded[t, l, :PAD, :] = zero_rows
            padded[t, l, PAD : PAD + count, :] = value
            padded[t, l, PAD + count :, :] = zero_rows
            for k, shift in enumerate(NEAR):
                moved[k, t, l] = lanes(value, -shift)
        return carry

    lax.fori_loop(0, levels, level, 0)


def in_vmem(kernel, name, shapes, *operands):
    vmem = pl.BlockSpec(memory_space=pltpu.VMEM)
    return pl.pallas_call(
        kernel,
        out_shape=tuple(pltpu.VMEM(shape, jnp.float32) for shape in shapes),
        in_specs=[vmem] * len(operands),
        out_specs=(vmem,) * len(shapes),
        compiler_params=pltpu.CompilerParams(vmem_limit_bytes=24 * 1024 * 1024),
        cost_estimate=pl.CostEstimate(flops=2000000, bytes_accessed=1000000, transcendentals=0),
        name=name,
    )(*operands)


def pack(mass):
    _, levels, count, width = mass.shape
    return in_vmem(pack_kernel, "pack", ((levels * count, width),) * 2, mass)


def copies(mass):
    tracers, levels, count, width = mass.shape
    padded = (tracers, levels, count + 2 * PAD, width)
    return in_vmem(copies_kernel, "copies", (padded, (len(NEAR),) + mass.shape), mass)


def segments(shape):
    lane = lane_index(shape)
    segment = sum(
        ((lane >= SEG * k).astype(jnp.int32) for k in range(1, PACK)), jnp.zeros(shape, jnp.int32)
    )
    return segment, lane - SEG * segment, lane < SEG * PACK


def moved_places(held):
    return {shift: lanes(held, shift) if shift else held for shift in (-STEP, 0, STEP)}


def east_parts(taps, near, parts=None):
    parts = dict(parts or {})
    for m in taps:
        shift = east_group(m)
        term = taps[m] * near[m - shift]
        parts[shift] = parts[shift] + term if shift in parts else term
    return parts


def moved_sum(parts):
    return parts[0] + (lanes(parts[-STEP], STEP) + lanes(parts[STEP], -STEP))


def near_cells(x):
    return {0: x, **{shift: lanes(x, -shift) for shift in NEAR}}


def inner_kernel(span, mine, other, padded, shifted, *refs):
    low_part, high_part = span(refs[0].shape[1])

    @pl.when(low_part < high_part)
    def _():
        inner_body(low_part, high_part, mine, other, padded, shifted, *refs)


def inner_body(
    low_part, high_part, mine, other, padded, shifted, sums, outer_c, edge_c, thickness,
    east_c, north_c, inners, middle, partial,
):
    tracers, levels, count, width = sums.shape
    shape = (count, width)
    lane = lane_index(shape)
    low = position() % 2 == 0
    _, in_segment, packed_lane = segments(shape)
    zero_rows = jnp.zeros((PAD, width), jnp.float32)
    for slot in range(2):
        for j in range(GROUP):
            middle[slot, j, :PAD, :] = zero_rows
            middle[slot, j, PAD + count :, :] = zero_rows
    edge_index = jnp.where(packed_lane, in_segment + (width - EDGE), 0)
    edge_index = jnp.where(edge_index >= width, edge_index - width, edge_index)
    moved_index = moved_places(edge_index)
    moved_segment = moved_places(jnp.where(packed_lane, in_segment, -2 * SEG))

    def level(l, carry):
        fields = []
        for half in range(2):
            for k in range(2):
                place = pl.ds(pl.multiple_of((k * levels + l) * count, count), count)
                a = mine[place, :]
                b = other[place, :]
                fields.append(jnp.where(low, a, b) if half == 0 else jnp.where(low, b, a))
        thick, east_courant, north_courant, whole = fields
        thickness[l] = thick
        here = east_taps(east_courant, whole)
        ahead = {m: jnp.where(lane == width - 1, 0.0, lanes(here[m], -1)) for m in here}
        taps = difference_taps(here, ahead, EDGE)
        for m in range(-EDGE, EDGE + 1):
            value = taps[m]
            if m != 0:
                q = moved_segment[east_group(m)]
                crosses = ((q < EDGE) != (q + m < EDGE)) & (q >= 0)
                outer_c[m + EDGE, l] = jnp.where(crosses, pick(value, moved_index[east_group(m)]), 0.0)
            if m < 0:
                value = jnp.where(lane >= -m, value, 0.0)
            if m > 0:
                value = jnp.where(lane < width - m, value, 0.0)
            shift = east_group(m)
            east_c[m + EDGE, l] = lanes(value, shift) if shift else value
        for m, value in enumerate(north_coefficients(north_courant)):
            north_c[m, l] = value
        for m, value in enumerate(north_coefficients(pick(north_courant, edge_index))):
            edge_c[m, l] = value
        return carry

    lax.fori_loop(low_part // 2, (high_part + 1) // 2, level, 0)
    groups = tracers // GROUP
    low_step, high_step = low_part * (groups // 2), high_part * (groups // 2)

    def block(b):
        return slice(b * BLOCK, (b + 1) * BLOCK)

    def padded_block(b, m=0):
        return slice(PAD + b * BLOCK + m, PAD + (b + 1) * BLOCK + m)

    def place(step):
        step = jnp.clip(step, 0, levels * groups - 1)
        return step // groups, (step % groups) * GROUP

    def weights(ref, l, b, reach):
        return {m: ref[m + reach, l, block(b), :] for m in range(-reach, reach + 1)}

    def front(step):
        l, t0 = place(step)
        slot = (step + 2) % 2
        for b in range(count // BLOCK):
            taps = weights(east_c, l, b, EDGE)
            north = weights(north_c, l, b, 3)
            taps[0] = 1.0 + taps[0]
            north[0] = 1.0 + north[0]
            for j in range(GROUP):
                x = padded[t0 + j, l, padded_block(b), :]
                inner = north[0] * x
                for m in (-3, -2, -1, 1, 2, 3):
                    inner = inner + north[m] * padded[t0 + j, l, padded_block(b, m), :]
                inners[slot, j, block(b), :] = inner
                near = {0: x}
                for k, shift in enumerate(NEAR):
                    near[shift] = shifted[k, t0 + j, l, block(b), :]
                middle[slot, j, padded_block(b), :] = moved_sum(east_parts(taps, near))

    def back(step):
        l, t0 = place(step)
        slot = (step + 2) % 2
        for b in range(count // BLOCK):
            taps = weights(east_c, l, b, EDGE)
            north = weights(north_c, l, b, 3)
            for j in range(GROUP):
                parts = east_parts(taps, near_cells(inners[slot, j, block(b), :]))
                total = 0.5 * padded[t0 + j, l, padded_block(b), :] + parts[0]
                for m in range(-3, 4):
                    total = total + north[m] * middle[slot, j, padded_block(b, m), :]
                partial[slot, 0, j, block(b), :] = total
                partial[slot, 1, j, block(b), :] = parts[-STEP]
                partial[slot, 2, j, block(b), :] = parts[STEP]

    def finish(step):
        l, t0 = place(step)
        slot = (step + 2) % 2
        for b in range(count // BLOCK):
            for j in range(GROUP):
                sums[t0 + j, l, block(b), :] = partial[slot, 0, j, block(b), :] + (
                    lanes(partial[slot, 1, j, block(b), :], STEP)
                    + lanes(partial[slot, 2, j, block(b), :], -STEP)
                )

    def step_of_three(step, carry):
        finish(step - 1)
        back(step)
        front(step + 1)
        return carry

    front(low_step)
    lax.fori_loop(low_step, high_step, step_of_three, 0)
    finish(high_step - 1)


def inner_update(span, mine, other, padded, shifted):
    tracers, levels, count, width = shifted.shape[1:]
    vmem = pl.BlockSpec(memory_space=pltpu.VMEM)
    level = (levels, count, width)
    return pl.pallas_call(
        functools.partial(inner_kernel, span),
        out_shape=(
            pltpu.VMEM((tracers,) + level, jnp.float32),
            pltpu.VMEM((2 * EDGE + 1,) + level, jnp.float32),
            pltpu.VMEM((7,) + level, jnp.float32),
            pltpu.VMEM(level, jnp.float32),
        ),
        in_specs=[vmem] * 4,
        out_specs=(vmem,) * 4,
        scratch_shapes=[
            pltpu.VMEM((2 * EDGE + 1,) + level, jnp.float32),
            pltpu.VMEM((7,) + level, jnp.float32),
            pltpu.VMEM((2, GROUP, count, width), jnp.float32),
            pltpu.VMEM((2, GROUP, count + 2 * PAD, width), jnp.float32),
            pltpu.VMEM((2, 3, GROUP, count, width), jnp.float32),
        ],
        compiler_params=pltpu.CompilerParams(vmem_limit_bytes=24 * 1024 * 1024),
        cost_estimate=pl.CostEstimate(flops=20000000, bytes_accessed=6000000, transcendentals=0),
        name="inner",
    )(mine, other, padded, shifted)


def edge_kernel(west, east, own, *refs):
    before, after, (out, stage, sems) = refs[:4], refs[4:8], refs[8:]
    tracers, levels, count, width = stage.shape
    early = early_parts(levels)
    shape = (count, width)
    lane = lane_index(shape)
    segment, in_segment, packed_lane = segments(shape)
    from_west_lane = in_segment < EDGE
    at_edge = (lane < EDGE) | (lane >= width - EDGE)
    last_face = {
        shift: q == EDGE - 1
        for shift, q in moved_places(jnp.where(packed_lane, in_segment, -2 * SEG)).items()
    }
    base = levels * count

    def unfolded(x):
        return jnp.concatenate([x, lanes(x, -MET_SEG * levels)])

    met_east = unfolded(east[base:, :])
    met_west = unfolded(west[base:, :])

    def copy(l, half):
        place = pl.ds(half * PACK, PACK)
        return pltpu.make_async_copy(stage.at[place, l], out.at[place, l], sems.at[l, half])

    def level(l, sums, outer_c, edge_c, thickness):
        level_rows = pl.ds(pl.multiple_of(l * count, count), count)
        met_lane = jnp.where(packed_lane, in_segment + MET_SEG * l, 0)
        met = jnp.where(lane - MET_SEG * l < EDGE, met_west, met_east)
        beyond = east_taps(
            pick(met_east, jnp.full(shape, SEG, jnp.int32) + MET_SEG * l),
            pick(met_east, jnp.full(shape, SEG + 1, jnp.int32) + MET_SEG * l),
        )
        mass_flux = pick(met_east, jnp.full(shape, SEG + 2, jnp.int32) + MET_SEG * l)
        inverse = 2.0 / (thickness[l] - jnp.where(lane == width - 1, mass_flux, 0.0))
        face = {
            m: jnp.where(last_face[east_group(m)], -beyond[m - 1], 0.0)
            for m in range(1 - EDGE, EDGE + 1)
        }
        outer = {m: outer_c[m + EDGE, l] for m in range(-EDGE, EDGE + 1) if m != 0}
        for m in range(1, EDGE + 1):
            outer[m] = outer[m] + face[m]
        inside = {m: face[m] for m in range(1 - EDGE, 1)}
        edge_taps = [edge_c[m, l] for m in range(7)]
        packed_taps = north_coefficients(pick(met, met_lane))
        for half in range(2):
            first_lane = EDGE * (segment + PACK * half) + in_segment
            west_index = jnp.where(packed_lane & from_west_lane, first_lane, 0)
            east_index = jnp.where(packed_lane & ~from_west_lane, first_lane - EDGE, 0)
            own_cells = pick(own[level_rows, :], west_index)
            cells = jnp.where(
                from_west_lane,
                pick(west[level_rows, :], west_index),
                pick(east[level_rows, :], east_index),
            )
            inner = cells
            own_inner = own_cells
            for m in range(-3, 4):
                inner = inner + packed_taps[m + 3] * rows(cells, -m)
                own_inner = own_inner + edge_taps[m + 3] * rows(own_cells, -m)
            first = moved_sum(
                east_parts(inside, near_cells(own_cells), east_parts(outer, near_cells(cells)))
            )
            total = moved_sum(
                east_parts(inside, near_cells(own_inner), east_parts(outer, near_cells(inner)))
            )
            for m in range(-3, 4):
                total = total + edge_taps[m + 3] * rows(first, -m)
            for k in range(PACK):
                t = half * PACK + k
                moved = jnp.where(at_edge, lanes(total, width - EDGE - SEG * k), 0.0)
                stage[t, l] = (sums(t, l, half) + moved) * inverse
            copy(l, half).start()

    def sums_after(t, l, half):
        value = after[0][t, l]
        return value if half else jnp.where(2 * l < early, before[0][t, l], value)

    def either(l, carry):
        @pl.when(2 * l + 1 < early)
        def _():
            level(l, lambda t, l, half: before[0][t, l], *before[1:])

        @pl.when(2 * l + 1 >= early)
        def _():
            level(l, sums_after, *after[1:])

        return carry

    lax.fori_loop(0, levels, either, 0)
    for l in range(levels):
        for half in range(2):
            copy(l, half).wait()


def edge_update(west, east, own, before, after):
    sums = before[0]
    tracers, levels, count, width = sums.shape
    vmem = pl.BlockSpec(memory_space=pltpu.VMEM)
    return pl.pallas_call(
        edge_kernel,
        out_shape=jax.ShapeDtypeStruct(sums.shape, jnp.float32),
        in_specs=[vmem] * 11,
        out_specs=pl.BlockSpec(memory_space=pl.ANY),
        scratch_shapes=[pltpu.VMEM(sums.shape, jnp.float32), pltpu.SemaphoreType.DMA((levels, 2))],
        compiler_params=pltpu.CompilerParams(vmem_limit_bytes=24 * 1024 * 1024),
        name="edges",
    )(west, east, own, *before, *after)


def east_group(m):
    return -STEP if m < -1 else (STEP if m > 2 else 0)


def along(x, pairs):
    return lax.ppermute(x, "space", pairs)


def exchange(x, flip):
    size = lax.axis_size("tracer")
    return lax.ppermute(x, "tracer", [(i, i ^ flip) for i in range(size)])


def turn(x, by):
    size = lax.axis_size("tracer")
    return lax.ppermute(x, "tracer", [(i, i // 8 * 8 + (i + 2 * by) % 8) for i in range(size)])


def shards(mass, thick, fe, fn, ce, cn, ne, owner):
    keep, send = prepare(thick, fe, fn, ce, cn, ne)
    last, first = pack(mass)
    me, chosen = position(), owner[0]
    other_core = exchange(send, 1)
    total = jnp.where(chosen == me, keep, jnp.where(chosen == me ^ 1, other_core, 0.0))
    total = total + turn(total, 1) + turn(total, -1) + turn(total, 2)
    total, last, first = lax.optimization_barrier((total, last, first))
    total = total + exchange(total, 8)
    padded, shifted = copies(mass)
    main = 2 * mass.shape[1] * mass.shape[2]
    mine = total[:main]
    edges = total[main:]
    size = lax.axis_size("space")
    to_east = jnp.concatenate([last, edges])
    to_west = jnp.concatenate([first, edges])
    west = along(to_east, [(i, (i + 1) % size) for i in range(size)])
    other = exchange(mine, 1)
    before = inner_update(lambda levels: (0, early_parts(levels)), mine, other, padded, shifted)
    to_west, before = lax.optimization_barrier((to_west, before))
    east = along(to_west, [(i, (i - 1) % size) for i in range(size)])
    after = inner_update(lambda levels: (early_parts(levels), 2 * levels), mine, other, padded, shifted)
    return edge_update(west, east, last, before, after)


def solution(mesh):
    spec = P("tracer", None, None, "space")
    return jax.shard_map(
        shards, mesh=mesh, in_specs=(spec,) * 7 + (P("space"),), out_specs=spec, check_vma=False
    )
```

```python
import functools

import jax
import jax.numpy as jnp
from jax import lax
from jax.experimental import pallas as pl
from jax.experimental.pallas import tpu as pltpu
from jax.sharding import PartitionSpec as P

NS = 2
EDGE = NS + 3
SEG = 2 * EDGE
PACK = 9
STEP = 4
GROUP = 3
PAD = 8
BLOCK = 8
NEAR = (-1, 1, 2)
MET_SEG = 16


def lane_index(shape):
    return lax.broadcasted_iota(jnp.int32, shape, len(shape) - 1)


def row_index(shape):
    return lax.broadcasted_iota(jnp.int32, shape, len(shape) - 2)


def lanes(x, shift):
    return pltpu.roll(x, shift % x.shape[-1], x.ndim - 1)


def rows(x, shift):
    return pltpu.roll(x, shift % x.shape[-2], x.ndim - 2)


def face_weights(courant):
    fraction = jnp.abs(courant)
    ramp = 1.5 * fraction * (1.0 - 2.0 / 3.0 * fraction)
    near = 0.5 * courant * (1.0 - 0.5 * fraction - ramp)
    far = 0.5 * courant * (0.5 * fraction - ramp)
    mean = courant * ramp
    far_outer = far * (1.0 / 12.0)
    near_outer = near * (1.0 / 12.0)
    return (
        -near_outer,
        7.0 * near_outer - far_outer,
        7.0 * (near_outer + far_outer) + mean,
        7.0 * far_outer - near_outer,
        -far_outer,
    )


def north_taps(courant):
    down1, up0, up1, up2, up3 = (w for w in face_weights(courant))
    forward = courant >= 0.0
    zero = jnp.zeros_like(courant)
    f = {1: down1, 0: up0, -1: up1, -2: up2, -3: up3}
    b = {-2: down1, -1: up0, 0: up1, 1: up2, 2: up3}
    return {m: jnp.where(forward, f.get(m, zero), b.get(m, zero)) for m in range(-3, 3)}


def east_taps(courant, whole):
    weights = face_weights(courant)
    forward = courant >= 0.0
    zero = jnp.zeros_like(courant)
    one = whole == 1.0
    two = whole == 2.0
    some = whole > 0.5
    taps = {}
    for m in range(-EDGE, EDGE):
        ahead = []
        behind = []
        for n in range(NS + 1):
            place = 1 - n - m
            ahead.append(weights[place] if 0 <= place < 5 else zero)
            place = m + 2 - n
            behind.append(weights[place] if 0 <= place < 5 else zero)
        f = jnp.where(two, ahead[2], jnp.where(one, ahead[1], ahead[0]))
        b = jnp.where(two, behind[2], jnp.where(one, behind[1], behind[0]))
        if m == -1:
            f = f + jnp.where(some, 0.5, 0.0)
        if m == -2:
            f = f + jnp.where(two, 0.5, 0.0)
        if m == 0:
            b = b - jnp.where(some, 0.5, 0.0)
        if m == 1:
            b = b - jnp.where(two, 0.5, 0.0)
        taps[m] = jnp.where(forward, f, b)
    return taps


def difference_taps(here, ahead, reach):
    out = {}
    for m in range(-reach, reach + 1):
        if m in here and m - 1 in ahead:
            out[m] = here[m] - ahead[m - 1]
        elif m in here:
            out[m] = here[m]
        else:
            out[m] = -ahead[m - 1]
    return out


def north_coefficients(courant):
    count = courant.shape[0]
    row = row_index(courant.shape)
    here = north_taps(jnp.where(row == 0, 0.0, courant))
    taps = difference_taps(here, {m: rows(here[m], -1) for m in here}, 3)
    return [
        jnp.where((row + m >= 0) & (row + m < count), taps[m], 0.0) for m in range(-3, 4)
    ]


def pick(x, index):
    return jnp.take_along_axis(x, index, axis=1, mode="promise_in_bounds")


def position():
    return lax.axis_index("tracer")


def tile():
    return lax.axis_index("space")


def early_parts(levels):
    return jnp.clip(levels + 1 - tile(), 0, levels)


def prepare_kernel(*refs):
    sources, (keep, send, *fields, sems) = refs[:6], refs[6:]
    copies = [
        pltpu.make_async_copy(source, place, sems.at[k])
        for k, (source, place) in enumerate(zip(sources, fields))
    ]
    for copy in copies:
        copy.start()
    for copy in copies:
        copy.wait()
    thick, fe, fn, ce, cn, ne = fields
    core = position() % 2
    levels, count, width = thick.shape[1:]
    lane = lane_index((count, width))
    row = row_index((count, width))
    half_lane = lane_index((count // 2, width))
    folded = jnp.zeros((count // 2, width), jnp.float32)
    for l in range(levels):
        east_mass = fe[0, l]
        north_mass = jnp.where(row == 0, 0.0, fn[0, l])
        thickness = (
            thick[0, l]
            + (east_mass - jnp.where(lane == width - 1, 0.0, lanes(east_mass, -1)))
            + (north_mass - rows(north_mass, -1))
        )
        whole = ne[0, l].astype(jnp.float32)
        first = (thickness, ce[0, l])
        second = (cn[0, l], whole)
        for k in range(2):
            start = (k * levels + l) * count
            keep[start : start + count, :] = jnp.where(core == 0, first[k], second[k])
            send[start : start + count, :] = jnp.where(core == 0, second[k], first[k])
        for part, start in enumerate((MET_SEG * l, MET_SEG * (levels + l))):
            here = slice(part * count // 2, (part + 1) * count // 2)
            inside = (half_lane >= start) & (half_lane < start + SEG)
            folded = jnp.where(inside, lanes(cn[0, l, here, :], start + EDGE), folded)
            for k, value in enumerate((ce[0, l, here, :], whole[here], east_mass[here])):
                at = start + SEG + k
                folded = jnp.where(half_lane == at, lanes(value, at), folded)
    base = 2 * levels * count
    keep[base:, :] = folded
    send[base:, :] = folded


def prepare(thick, fe, fn, ce, cn, ne):
    levels, count, width = thick.shape[1:]
    vmem = pl.BlockSpec(memory_space=pltpu.VMEM)
    half = pltpu.VMEM((2 * levels * count + count // 2, width), jnp.float32)
    return pl.pallas_call(
        prepare_kernel,
        out_shape=(half, half),
        in_specs=[pl.BlockSpec(memory_space=pl.ANY)] * 6,
        out_specs=(vmem, vmem),
        scratch_shapes=[pltpu.VMEM(thick.shape, jnp.float32)] * 5
        + [pltpu.VMEM(ne.shape, jnp.int32), pltpu.SemaphoreType.DMA((6,))],
        name="prepare",
    )(thick, fe, fn, ce, cn, ne)


def pack_kernel(mass, last, first):
    tracers, levels, count, width = mass.shape
    lane = lane_index((count, width))

    def level(l, carry):
        a = jnp.zeros((count, width), jnp.float32)
        b = a
        for t in range(tracers):
            inside = (lane >= EDGE * t) & (lane < EDGE * (t + 1))
            a = jnp.where(inside, lanes(mass[t, l], EDGE * (t + 1)), a)
            b = jnp.where(inside, lanes(mass[t, l], EDGE * t), b)
        place = pl.ds(pl.multiple_of(l * count, count), count)
        last[place, :] = a
        first[place, :] = b
        return carry

    lax.fori_loop(0, levels, level, 0)


def copies_kernel(mass, padded, moved):
    tracers, levels, count, width = mass.shape
    zero_rows = jnp.zeros((PAD, width), jnp.float32)

    def level(l, carry):
        for t in range(tracers):
            value = mass[t, l]
            padded[t, l, :PAD, :] = zero_rows
            padded[t, l, PAD : PAD + count, :] = value
            padded[t, l, PAD + count :, :] = zero_rows
            for k, shift in enumerate(NEAR):
                moved[k, t, l] = lanes(value, -shift)
        return carry

    lax.fori_loop(0, levels, level, 0)


def in_vmem(kernel, name, shapes, *operands):
    vmem = pl.BlockSpec(memory_space=pltpu.VMEM)
    return pl.pallas_call(
        kernel,
        out_shape=tuple(pltpu.VMEM(shape, jnp.float32) for shape in shapes),
        in_specs=[vmem] * len(operands),
        out_specs=(vmem,) * len(shapes),
        compiler_params=pltpu.CompilerParams(vmem_limit_bytes=24 * 1024 * 1024),
        cost_estimate=pl.CostEstimate(flops=2000000, bytes_accessed=1000000, transcendentals=0),
        name=name,
    )(*operands)


def pack(mass):
    _, levels, count, width = mass.shape
    return in_vmem(pack_kernel, "pack", ((levels * count, width),) * 2, mass)


def copies(mass):
    tracers, levels, count, width = mass.shape
    padded = (tracers, levels, count + 2 * PAD, width)
    return in_vmem(copies_kernel, "copies", (padded, (len(NEAR),) + mass.shape), mass)


def segments(shape):
    lane = lane_index(shape)
    segment = sum(
        ((lane >= SEG * k).astype(jnp.int32) for k in range(1, PACK)), jnp.zeros(shape, jnp.int32)
    )
    return segment, lane - SEG * segment, lane < SEG * PACK


def moved_places(held):
    return {shift: lanes(held, shift) if shift else held for shift in (-STEP, 0, STEP)}


def east_parts(taps, near, parts=None):
    parts = dict(parts or {})
    for m in taps:
        shift = east_group(m)
        term = taps[m] * near[m - shift]
        parts[shift] = parts[shift] + term if shift in parts else term
    return parts


def moved_sum(parts):
    return parts[0] + (lanes(parts[-STEP], STEP) + lanes(parts[STEP], -STEP))


def near_cells(x):
    return {0: x, **{shift: lanes(x, -shift) for shift in NEAR}}


def inner_kernel(span, mine, other, padded, shifted, *refs):
    low_part, high_part = span(refs[0].shape[1])

    @pl.when(low_part < high_part)
    def _():
        inner_body(low_part, high_part, mine, other, padded, shifted, *refs)


def inner_body(
    low_part, high_part, mine, other, padded, shifted, sums, outer_c, edge_c, thickness,
    east_c, north_c, inners, middle, partial,
):
    tracers, levels, count, width = sums.shape
    shape = (count, width)
    lane = lane_index(shape)
    low = position() % 2 == 0
    _, in_segment, packed_lane = segments(shape)
    zero_rows = jnp.zeros((PAD, width), jnp.float32)
    for slot in range(2):
        for j in range(GROUP):
            middle[slot, j, :PAD, :] = zero_rows
            middle[slot, j, PAD + count :, :] = zero_rows
    edge_index = jnp.where(packed_lane, in_segment + (width - EDGE), 0)
    edge_index = jnp.where(edge_index >= width, edge_index - width, edge_index)
    moved_index = moved_places(edge_index)
    moved_segment = moved_places(jnp.where(packed_lane, in_segment, -2 * SEG))

    def level(l, carry):
        fields = []
        for half in range(2):
            for k in range(2):
                place = pl.ds(pl.multiple_of((k * levels + l) * count, count), count)
                a = mine[place, :]
                b = other[place, :]
                fields.append(jnp.where(low, a, b) if half == 0 else jnp.where(low, b, a))
        thick, east_courant, north_courant, whole = fields
        thickness[l] = thick
        here = east_taps(east_courant, whole)
        ahead = {m: jnp.where(lane == width - 1, 0.0, lanes(here[m], -1)) for m in here}
        taps = difference_taps(here, ahead, EDGE)
        for m in range(-EDGE, EDGE + 1):
            value = taps[m]
            if m != 0:
                q = moved_segment[east_group(m)]
                crosses = ((q < EDGE) != (q + m < EDGE)) & (q >= 0)
                outer_c[m + EDGE, l] = jnp.where(crosses, pick(value, moved_index[east_group(m)]), 0.0)
            if m < 0:
                value = jnp.where(lane >= -m, value, 0.0)
            if m > 0:
                value = jnp.where(lane < width - m, value, 0.0)
            shift = east_group(m)
            east_c[m + EDGE, l] = lanes(value, shift) if shift else value
        for m, value in enumerate(north_coefficients(north_courant)):
            north_c[m, l] = value
        for m, value in enumerate(north_coefficients(pick(north_courant, edge_index))):
            edge_c[m, l] = value
        return carry

    lax.fori_loop(low_part // 2, (high_part + 1) // 2, level, 0)
    groups = tracers // GROUP
    low_step, high_step = low_part * (groups // 2), high_part * (groups // 2)

    def block(b):
        return slice(b * BLOCK, (b + 1) * BLOCK)

    def padded_block(b, m=0):
        return slice(PAD + b * BLOCK + m, PAD + (b + 1) * BLOCK + m)

    def place(step):
        step = jnp.clip(step, 0, levels * groups - 1)
        return step // groups, (step % groups) * GROUP

    def weights(ref, l, b, reach):
        return {m: ref[m + reach, l, block(b), :] for m in range(-reach, reach + 1)}

    def front(step):
        l, t0 = place(step)
        slot = (step + 2) % 2
        for b in range(count // BLOCK):
            taps = weights(east_c, l, b, EDGE)
            north = weights(north_c, l, b, 3)
            taps[0] = 1.0 + taps[0]
            north[0] = 1.0 + north[0]
            for j in range(GROUP):
                x = padded[t0 + j, l, padded_block(b), :]
                inner = north[0] * x
                for m in (-3, -2, -1, 1, 2, 3):
                    inner = inner + north[m] * padded[t0 + j, l, padded_block(b, m), :]
                inners[slot, j, block(b), :] = inner
                near = {0: x}
                for k, shift in enumerate(NEAR):
                    near[shift] = shifted[k, t0 + j, l, block(b), :]
                middle[slot, j, padded_block(b), :] = moved_sum(east_parts(taps, near))

    def back(step):
        l, t0 = place(step)
        slot = (step + 2) % 2
        for b in range(count // BLOCK):
            taps = weights(east_c, l, b, EDGE)
            north = weights(north_c, l, b, 3)
            for j in range(GROUP):
                parts = east_parts(taps, near_cells(inners[slot, j, block(b), :]))
                total = 0.5 * padded[t0 + j, l, padded_block(b), :] + parts[0]
                for m in range(-3, 4):
                    total = total + north[m] * middle[slot, j, padded_block(b, m), :]
                partial[slot, 0, j, block(b), :] = total
                partial[slot, 1, j, block(b), :] = parts[-STEP]
                partial[slot, 2, j, block(b), :] = parts[STEP]

    def finish(step):
        l, t0 = place(step)
        slot = (step + 2) % 2
        for b in range(count // BLOCK):
            for j in range(GROUP):
                sums[t0 + j, l, block(b), :] = partial[slot, 0, j, block(b), :] + (
                    lanes(partial[slot, 1, j, block(b), :], STEP)
                    + lanes(partial[slot, 2, j, block(b), :], -STEP)
                )

    def step_of_three(step, carry):
        finish(step - 1)
        back(step)
        front(step + 1)
        return carry

    front(low_step)
    lax.fori_loop(low_step, high_step, step_of_three, 0)
    finish(high_step - 1)


def inner_update(span, mine, other, padded, shifted):
    tracers, levels, count, width = shifted.shape[1:]
    vmem = pl.BlockSpec(memory_space=pltpu.VMEM)
    level = (levels, count, width)
    return pl.pallas_call(
        functools.partial(inner_kernel, span),
        out_shape=(
            pltpu.VMEM((tracers,) + level, jnp.float32),
            pltpu.VMEM((2 * EDGE + 1,) + level, jnp.float32),
            pltpu.VMEM((7,) + level, jnp.float32),
            pltpu.VMEM(level, jnp.float32),
        ),
        in_specs=[vmem] * 4,
        out_specs=(vmem,) * 4,
        scratch_shapes=[
            pltpu.VMEM((2 * EDGE + 1,) + level, jnp.float32),
            pltpu.VMEM((7,) + level, jnp.float32),
            pltpu.VMEM((2, GROUP, count, width), jnp.float32),
            pltpu.VMEM((2, GROUP, count + 2 * PAD, width), jnp.float32),
            pltpu.VMEM((2, 3, GROUP, count, width), jnp.float32),
        ],
        compiler_params=pltpu.CompilerParams(vmem_limit_bytes=24 * 1024 * 1024),
        cost_estimate=pl.CostEstimate(flops=20000000, bytes_accessed=6000000, transcendentals=0),
        name="inner",
    )(mine, other, padded, shifted)


def edge_kernel(west, east, own, *refs):
    before, after, (out, stage, sems) = refs[:4], refs[4:8], refs[8:]
    tracers, levels, count, width = stage.shape
    early = early_parts(levels)
    shape = (count, width)
    lane = lane_index(shape)
    segment, in_segment, packed_lane = segments(shape)
    from_west_lane = in_segment < EDGE
    at_edge = (lane < EDGE) | (lane >= width - EDGE)
    last_face = {
        shift: q == EDGE - 1
        for shift, q in moved_places(jnp.where(packed_lane, in_segment, -2 * SEG)).items()
    }
    base = levels * count

    def unfolded(x):
        return jnp.concatenate([x, lanes(x, -MET_SEG * levels)])

    met_east = unfolded(east[base:, :])
    met_west = unfolded(west[base:, :])

    def copy(l, half):
        place = pl.ds(half * PACK, PACK)
        return pltpu.make_async_copy(stage.at[place, l], out.at[place, l], sems.at[l, half])

    def level(l, sums, outer_c, edge_c, thickness):
        level_rows = pl.ds(pl.multiple_of(l * count, count), count)
        met_lane = jnp.where(packed_lane, in_segment + MET_SEG * l, 0)
        met = jnp.where(lane - MET_SEG * l < EDGE, met_west, met_east)
        beyond = east_taps(
            pick(met_east, jnp.full(shape, SEG, jnp.int32) + MET_SEG * l),
            pick(met_east, jnp.full(shape, SEG + 1, jnp.int32) + MET_SEG * l),
        )
        mass_flux = pick(met_east, jnp.full(shape, SEG + 2, jnp.int32) + MET_SEG * l)
        inverse = 2.0 / (thickness[l] - jnp.where(lane == width - 1, mass_flux, 0.0))
        face = {
            m: jnp.where(last_face[east_group(m)], -beyond[m - 1], 0.0)
            for m in range(1 - EDGE, EDGE + 1)
        }
        outer = {m: outer_c[m + EDGE, l] for m in range(-EDGE, EDGE + 1) if m != 0}
        for m in range(1, EDGE + 1):
            outer[m] = outer[m] + face[m]
        inside = {m: face[m] for m in range(1 - EDGE, 1)}
        edge_taps = [edge_c[m, l] for m in range(7)]
        packed_taps = north_coefficients(pick(met, met_lane))
        for half in range(2):
            first_lane = EDGE * (segment + PACK * half) + in_segment
            west_index = jnp.where(packed_lane & from_west_lane, first_lane, 0)
            east_index = jnp.where(packed_lane & ~from_west_lane, first_lane - EDGE, 0)
            own_cells = pick(own[level_rows, :], west_index)
            cells = jnp.where(
                from_west_lane,
                pick(west[level_rows, :], west_index),
                pick(east[level_rows, :], east_index),
            )
            inner = cells
            own_inner = own_cells
            for m in range(-3, 4):
                inner = inner + packed_taps[m + 3] * rows(cells, -m)
                own_inner = own_inner + edge_taps[m + 3] * rows(own_cells, -m)
            first = moved_sum(
                east_parts(inside, near_cells(own_cells), east_parts(outer, near_cells(cells)))
            )
            total = moved_sum(
                east_parts(inside, near_cells(own_inner), east_parts(outer, near_cells(inner)))
            )
            for m in range(-3, 4):
                total = total + edge_taps[m + 3] * rows(first, -m)
            for k in range(PACK):
                t = half * PACK + k
                moved = jnp.where(at_edge, lanes(total, width - EDGE - SEG * k), 0.0)
                stage[t, l] = (sums(t, l, half) + moved) * inverse
            copy(l, half).start()

    def sums_after(t, l, half):
        value = after[0][t, l]
        return value if half else jnp.where(2 * l < early, before[0][t, l], value)

    def either(l, carry):
        @pl.when(2 * l + 1 < early)
        def _():
            level(l, lambda t, l, half: before[0][t, l], *before[1:])

        @pl.when(2 * l + 1 >= early)
        def _():
            level(l, sums_after, *after[1:])

        return carry

    lax.fori_loop(0, levels, either, 0)
    for l in range(levels):
        for half in range(2):
            copy(l, half).wait()


def edge_update(west, east, own, before, after):
    sums = before[0]
    tracers, levels, count, width = sums.shape
    vmem = pl.BlockSpec(memory_space=pltpu.VMEM)
    return pl.pallas_call(
        edge_kernel,
        out_shape=jax.ShapeDtypeStruct(sums.shape, jnp.float32),
        in_specs=[vmem] * 11,
        out_specs=pl.BlockSpec(memory_space=pl.ANY),
        scratch_shapes=[pltpu.VMEM(sums.shape, jnp.float32), pltpu.SemaphoreType.DMA((levels, 2))],
        compiler_params=pltpu.CompilerParams(vmem_limit_bytes=24 * 1024 * 1024),
        name="edges",
    )(west, east, own, *before, *after)


def east_group(m):
    return -STEP if m < -1 else (STEP if m > 2 else 0)


def along(x, pairs):
    return lax.ppermute(x, "space", pairs)


def exchange(x, flip):
    size = lax.axis_size("tracer")
    return lax.ppermute(x, "tracer", [(i, i ^ flip) for i in range(size)])


def turn(x, by):
    size = lax.axis_size("tracer")
    return lax.ppermute(x, "tracer", [(i, i // 8 * 8 + (i + 2 * by) % 8) for i in range(size)])


def shards(mass, thick, fe, fn, ce, cn, ne, owner):
    keep, send = prepare(thick, fe, fn, ce, cn, ne)
    last, first = pack(mass)
    me, chosen = position(), owner[0]
    other_core = exchange(send, 1)
    total = jnp.where(chosen == me, keep, jnp.where(chosen == me ^ 1, other_core, 0.0))
    total = total + exchange(total, 8)
    total, last, first = lax.optimization_barrier((total, last, first))
    total = total + (turn(total, 1) + turn(total, -1) + turn(total, 2))
    padded, shifted = copies(mass)
    main = 2 * mass.shape[1] * mass.shape[2]
    mine = total[:main]
    edges = total[main:]
    size = lax.axis_size("space")
    to_east = jnp.concatenate([last, edges])
    to_west = jnp.concatenate([first, edges])
    west = along(to_east, [(i, (i + 1) % size) for i in range(size)])
    other = exchange(mine, 1)
    before = inner_update(lambda levels: (0, early_parts(levels)), mine, other, padded, shifted)
    to_west, before = lax.optimization_barrier((to_west, before))
    east = along(to_west, [(i, (i - 1) % size) for i in range(size)])
    after = inner_update(lambda levels: (early_parts(levels), 2 * levels), mine, other, padded, shifted)
    return edge_update(west, east, last, before, after)


def solution(mesh):
    spec = P("tracer", None, None, "space")
    return jax.shard_map(
        shards, mesh=mesh, in_specs=(spec,) * 7 + (P("space"),), out_specs=spec, check_vma=False
    )
```

```python
import functools

import jax
import jax.numpy as jnp
from jax import lax
from jax.experimental import pallas as pl
from jax.experimental.pallas import tpu as pltpu
from jax.sharding import PartitionSpec as P

NS = 2
EDGE = NS + 3
SEG = 2 * EDGE
PACK = 9
STEP = 4
GROUP = 3
PAD = 8
BLOCK = 8
NEAR = (-1, 1, 2)
MET_SEG = 16


def lane_index(shape):
    return lax.broadcasted_iota(jnp.int32, shape, len(shape) - 1)


def row_index(shape):
    return lax.broadcasted_iota(jnp.int32, shape, len(shape) - 2)


def lanes(x, shift):
    return pltpu.roll(x, shift % x.shape[-1], x.ndim - 1)


def rows(x, shift):
    return pltpu.roll(x, shift % x.shape[-2], x.ndim - 2)


def face_weights(courant):
    fraction = jnp.abs(courant)
    ramp = 1.5 * fraction * (1.0 - 2.0 / 3.0 * fraction)
    near = 0.5 * courant * (1.0 - 0.5 * fraction - ramp)
    far = 0.5 * courant * (0.5 * fraction - ramp)
    mean = courant * ramp
    far_outer = far * (1.0 / 12.0)
    near_outer = near * (1.0 / 12.0)
    return (
        -near_outer,
        7.0 * near_outer - far_outer,
        7.0 * (near_outer + far_outer) + mean,
        7.0 * far_outer - near_outer,
        -far_outer,
    )


def north_taps(courant):
    down1, up0, up1, up2, up3 = (w for w in face_weights(courant))
    forward = courant >= 0.0
    zero = jnp.zeros_like(courant)
    f = {1: down1, 0: up0, -1: up1, -2: up2, -3: up3}
    b = {-2: down1, -1: up0, 0: up1, 1: up2, 2: up3}
    return {m: jnp.where(forward, f.get(m, zero), b.get(m, zero)) for m in range(-3, 3)}


def east_taps(courant, whole):
    weights = face_weights(courant)
    forward = courant >= 0.0
    zero = jnp.zeros_like(courant)
    one = whole == 1.0
    two = whole == 2.0
    some = whole > 0.5
    taps = {}
    for m in range(-EDGE, EDGE):
        ahead = []
        behind = []
        for n in range(NS + 1):
            place = 1 - n - m
            ahead.append(weights[place] if 0 <= place < 5 else zero)
            place = m + 2 - n
            behind.append(weights[place] if 0 <= place < 5 else zero)
        f = jnp.where(two, ahead[2], jnp.where(one, ahead[1], ahead[0]))
        b = jnp.where(two, behind[2], jnp.where(one, behind[1], behind[0]))
        if m == -1:
            f = f + jnp.where(some, 0.5, 0.0)
        if m == -2:
            f = f + jnp.where(two, 0.5, 0.0)
        if m == 0:
            b = b - jnp.where(some, 0.5, 0.0)
        if m == 1:
            b = b - jnp.where(two, 0.5, 0.0)
        taps[m] = jnp.where(forward, f, b)
    return taps


def difference_taps(here, ahead, reach):
    out = {}
    for m in range(-reach, reach + 1):
        if m in here and m - 1 in ahead:
            out[m] = here[m] - ahead[m - 1]
        elif m in here:
            out[m] = here[m]
        else:
            out[m] = -ahead[m - 1]
    return out


def north_coefficients(courant):
    count = courant.shape[0]
    row = row_index(courant.shape)
    here = north_taps(jnp.where(row == 0, 0.0, courant))
    taps = difference_taps(here, {m: rows(here[m], -1) for m in here}, 3)
    return [
        jnp.where((row + m >= 0) & (row + m < count), taps[m], 0.0) for m in range(-3, 4)
    ]


def pick(x, index):
    return jnp.take_along_axis(x, index, axis=1, mode="promise_in_bounds")


def position():
    return lax.axis_index("tracer")


def tile():
    return lax.axis_index("space")


def early_parts(levels):
    return jnp.clip(levels + 1 - tile(), 0, levels)


def prepare_kernel(*refs):
    sources, (keep, send, *fields, sems) = refs[:6], refs[6:]
    copies = [
        pltpu.make_async_copy(source, place, sems.at[k])
        for k, (source, place) in enumerate(zip(sources, fields))
    ]
    for copy in copies:
        copy.start()
    for copy in copies:
        copy.wait()
    thick, fe, fn, ce, cn, ne = fields
    core = position() % 2
    levels, count, width = thick.shape[1:]
    lane = lane_index((count, width))
    row = row_index((count, width))
    half_lane = lane_index((count // 2, width))
    folded = jnp.zeros((count // 2, width), jnp.float32)
    for l in range(levels):
        east_mass = fe[0, l]
        north_mass = jnp.where(row == 0, 0.0, fn[0, l])
        thickness = (
            thick[0, l]
            + (east_mass - jnp.where(lane == width - 1, 0.0, lanes(east_mass, -1)))
            + (north_mass - rows(north_mass, -1))
        )
        whole = ne[0, l].astype(jnp.float32)
        first = (thickness, ce[0, l])
        second = (cn[0, l], whole)
        for k in range(2):
            start = (k * levels + l) * count
            keep[start : start + count, :] = jnp.where(core == 0, first[k], second[k])
            send[start : start + count, :] = jnp.where(core == 0, second[k], first[k])
        for part, start in enumerate((MET_SEG * l, MET_SEG * (levels + l))):
            here = slice(part * count // 2, (part + 1) * count // 2)
            inside = (half_lane >= start) & (half_lane < start + SEG)
            folded = jnp.where(inside, lanes(cn[0, l, here, :], start + EDGE), folded)
            for k, value in enumerate((ce[0, l, here, :], whole[here], east_mass[here])):
                at = start + SEG + k
                folded = jnp.where(half_lane == at, lanes(value, at), folded)
    base = 2 * levels * count
    keep[base:, :] = folded
    send[base:, :] = folded


def prepare(thick, fe, fn, ce, cn, ne):
    levels, count, width = thick.shape[1:]
    vmem = pl.BlockSpec(memory_space=pltpu.VMEM)
    half = pltpu.VMEM((2 * levels * count + count // 2, width), jnp.float32)
    return pl.pallas_call(
        prepare_kernel,
        out_shape=(half, half),
        in_specs=[pl.BlockSpec(memory_space=pl.ANY)] * 6,
        out_specs=(vmem, vmem),
        scratch_shapes=[pltpu.VMEM(thick.shape, jnp.float32)] * 5
        + [pltpu.VMEM(ne.shape, jnp.int32), pltpu.SemaphoreType.DMA((6,))],
        name="prepare",
    )(thick, fe, fn, ce, cn, ne)


def pack_kernel(mass, last, first, own):
    tracers, levels, count, width = mass.shape
    lane = lane_index((count, width))
    segment, in_segment, packed_lane = segments((count, width))

    def level(l, carry):
        a = jnp.zeros((count, width), jnp.float32)
        b = a
        for t in range(tracers):
            inside = (lane >= EDGE * t) & (lane < EDGE * (t + 1))
            a = jnp.where(inside, lanes(mass[t, l], EDGE * (t + 1)), a)
            b = jnp.where(inside, lanes(mass[t, l], EDGE * t), b)
        place = pl.ds(pl.multiple_of(l * count, count), count)
        last[place, :] = a
        first[place, :] = b
        for half in range(tracers // PACK):
            index = EDGE * (segment + PACK * half) + in_segment
            cells = pick(a, jnp.where(packed_lane & (in_segment < EDGE), index, 0))
            own[half, 0, l] = cells
            for k, shift in enumerate(NEAR):
                own[half, k + 1, l] = lanes(cells, -shift)
        return carry

    lax.fori_loop(0, levels, level, 0)


def copies_kernel(mass, padded, moved):
    tracers, levels, count, width = mass.shape
    zero_rows = jnp.zeros((PAD, width), jnp.float32)

    def level(l, carry):
        for t in range(tracers):
            value = mass[t, l]
            padded[t, l, :PAD, :] = zero_rows
            padded[t, l, PAD : PAD + count, :] = value
            padded[t, l, PAD + count :, :] = zero_rows
            for k, shift in enumerate(NEAR):
                moved[k, t, l] = lanes(value, -shift)
        return carry

    lax.fori_loop(0, levels, level, 0)


def in_vmem(kernel, name, shapes, *operands):
    vmem = pl.BlockSpec(memory_space=pltpu.VMEM)
    return pl.pallas_call(
        kernel,
        out_shape=tuple(pltpu.VMEM(shape, jnp.float32) for shape in shapes),
        in_specs=[vmem] * len(operands),
        out_specs=(vmem,) * len(shapes),
        compiler_params=pltpu.CompilerParams(vmem_limit_bytes=24 * 1024 * 1024),
        cost_estimate=pl.CostEstimate(flops=2000000, bytes_accessed=1000000, transcendentals=0),
        name=name,
    )(*operands)


def pack(mass):
    tracers, levels, count, width = mass.shape
    own = (tracers // PACK, 1 + len(NEAR), levels, count, width)
    return in_vmem(pack_kernel, "pack", ((levels * count, width),) * 2 + (own,), mass)


def copies(mass):
    tracers, levels, count, width = mass.shape
    padded = (tracers, levels, count + 2 * PAD, width)
    return in_vmem(copies_kernel, "copies", (padded, (len(NEAR),) + mass.shape), mass)


def segments(shape):
    lane = lane_index(shape)
    segment = sum(
        ((lane >= SEG * k).astype(jnp.int32) for k in range(1, PACK)), jnp.zeros(shape, jnp.int32)
    )
    return segment, lane - SEG * segment, lane < SEG * PACK


def moved_places(held):
    return {shift: lanes(held, shift) if shift else held for shift in (-STEP, 0, STEP)}


def east_parts(taps, near, parts=None):
    parts = dict(parts or {})
    for m in taps:
        shift = east_group(m)
        term = taps[m] * near[m - shift]
        parts[shift] = parts[shift] + term if shift in parts else term
    return parts


def moved_sum(parts):
    return parts[0] + (lanes(parts[-STEP], STEP) + lanes(parts[STEP], -STEP))


def near_cells(x):
    return {0: x, **{shift: lanes(x, -shift) for shift in NEAR}}


def inner_kernel(span, mine, other, padded, shifted, *refs):
    low_part, high_part = span(refs[0].shape[1])

    @pl.when(low_part < high_part)
    def _():
        inner_body(low_part, high_part, mine, other, padded, shifted, *refs)


def inner_body(
    low_part, high_part, mine, other, padded, shifted, sums, outer_c, edge_c, thickness,
    east_c, north_c, inners, middle, partial,
):
    tracers, levels, count, width = sums.shape
    shape = (count, width)
    lane = lane_index(shape)
    low = position() % 2 == 0
    _, in_segment, packed_lane = segments(shape)
    zero_rows = jnp.zeros((PAD, width), jnp.float32)
    for slot in range(2):
        for j in range(GROUP):
            middle[slot, j, :PAD, :] = zero_rows
            middle[slot, j, PAD + count :, :] = zero_rows
    edge_index = jnp.where(packed_lane, in_segment + (width - EDGE), 0)
    edge_index = jnp.where(edge_index >= width, edge_index - width, edge_index)
    moved_index = moved_places(edge_index)
    moved_segment = moved_places(jnp.where(packed_lane, in_segment, -2 * SEG))

    def level(l, carry):
        fields = []
        for half in range(2):
            for k in range(2):
                place = pl.ds(pl.multiple_of((k * levels + l) * count, count), count)
                a = mine[place, :]
                b = other[place, :]
                fields.append(jnp.where(low, a, b) if half == 0 else jnp.where(low, b, a))
        thick, east_courant, north_courant, whole = fields
        thickness[l] = thick
        here = east_taps(east_courant, whole)
        ahead = {m: jnp.where(lane == width - 1, 0.0, lanes(here[m], -1)) for m in here}
        taps = difference_taps(here, ahead, EDGE)
        for m in range(-EDGE, EDGE + 1):
            value = taps[m]
            if m != 0:
                q = moved_segment[east_group(m)]
                crosses = ((q < EDGE) != (q + m < EDGE)) & (q >= 0)
                outer_c[m + EDGE, l] = jnp.where(crosses, pick(value, moved_index[east_group(m)]), 0.0)
            if m < 0:
                value = jnp.where(lane >= -m, value, 0.0)
            if m > 0:
                value = jnp.where(lane < width - m, value, 0.0)
            shift = east_group(m)
            east_c[m + EDGE, l] = lanes(value, shift) if shift else value
        for m, value in enumerate(north_coefficients(north_courant)):
            north_c[m, l] = value
        for m, value in enumerate(north_coefficients(pick(north_courant, edge_index))):
            edge_c[m, l] = value
        return carry

    lax.fori_loop(low_part // 2, (high_part + 1) // 2, level, 0)
    groups = tracers // GROUP
    low_step, high_step = low_part * (groups // 2), high_part * (groups // 2)

    def block(b):
        return slice(b * BLOCK, (b + 1) * BLOCK)

    def padded_block(b, m=0):
        return slice(PAD + b * BLOCK + m, PAD + (b + 1) * BLOCK + m)

    def place(step):
        step = jnp.clip(step, 0, levels * groups - 1)
        return step // groups, (step % groups) * GROUP

    def weights(ref, l, b, reach):
        return {m: ref[m + reach, l, block(b), :] for m in range(-reach, reach + 1)}

    def front(step):
        l, t0 = place(step)
        slot = (step + 2) % 2
        for b in range(count // BLOCK):
            taps = weights(east_c, l, b, EDGE)
            north = weights(north_c, l, b, 3)
            taps[0] = 1.0 + taps[0]
            north[0] = 1.0 + north[0]
            for j in range(GROUP):
                x = padded[t0 + j, l, padded_block(b), :]
                inner = north[0] * x
                for m in (-3, -2, -1, 1, 2, 3):
                    inner = inner + north[m] * padded[t0 + j, l, padded_block(b, m), :]
                inners[slot, j, block(b), :] = inner
                near = {0: x}
                for k, shift in enumerate(NEAR):
                    near[shift] = shifted[k, t0 + j, l, block(b), :]
                middle[slot, j, padded_block(b), :] = moved_sum(east_parts(taps, near))

    def back(step):
        l, t0 = place(step)
        slot = (step + 2) % 2
        for b in range(count // BLOCK):
            taps = weights(east_c, l, b, EDGE)
            north = weights(north_c, l, b, 3)
            for j in range(GROUP):
                parts = east_parts(taps, near_cells(inners[slot, j, block(b), :]))
                total = 0.5 * padded[t0 + j, l, padded_block(b), :] + parts[0]
                for m in range(-3, 4):
                    total = total + north[m] * middle[slot, j, padded_block(b, m), :]
                partial[slot, 0, j, block(b), :] = total
                partial[slot, 1, j, block(b), :] = parts[-STEP]
                partial[slot, 2, j, block(b), :] = parts[STEP]

    def finish(step):
        l, t0 = place(step)
        slot = (step + 2) % 2
        for b in range(count // BLOCK):
            for j in range(GROUP):
                sums[t0 + j, l, block(b), :] = partial[slot, 0, j, block(b), :] + (
                    lanes(partial[slot, 1, j, block(b), :], STEP)
                    + lanes(partial[slot, 2, j, block(b), :], -STEP)
                )

    def step_of_three(step, carry):
        finish(step - 1)
        back(step)
        front(step + 1)
        return carry

    front(low_step)
    lax.fori_loop(low_step, high_step, step_of_three, 0)
    finish(high_step - 1)


def inner_update(span, mine, other, padded, shifted):
    tracers, levels, count, width = shifted.shape[1:]
    vmem = pl.BlockSpec(memory_space=pltpu.VMEM)
    level = (levels, count, width)
    return pl.pallas_call(
        functools.partial(inner_kernel, span),
        out_shape=(
            pltpu.VMEM((tracers,) + level, jnp.float32),
            pltpu.VMEM((2 * EDGE + 1,) + level, jnp.float32),
            pltpu.VMEM((7,) + level, jnp.float32),
            pltpu.VMEM(level, jnp.float32),
        ),
        in_specs=[vmem] * 4,
        out_specs=(vmem,) * 4,
        scratch_shapes=[
            pltpu.VMEM((2 * EDGE + 1,) + level, jnp.float32),
            pltpu.VMEM((7,) + level, jnp.float32),
            pltpu.VMEM((2, GROUP, count, width), jnp.float32),
            pltpu.VMEM((2, GROUP, count + 2 * PAD, width), jnp.float32),
            pltpu.VMEM((2, 3, GROUP, count, width), jnp.float32),
        ],
        compiler_params=pltpu.CompilerParams(vmem_limit_bytes=24 * 1024 * 1024),
        cost_estimate=pl.CostEstimate(flops=20000000, bytes_accessed=6000000, transcendentals=0),
        name="inner",
    )(mine, other, padded, shifted)


def edge_kernel(west, east, own, *refs):
    before, after, (out, stage, sems) = refs[:4], refs[4:8], refs[8:]
    tracers, levels, count, width = stage.shape
    early = early_parts(levels)
    shape = (count, width)
    lane = lane_index(shape)
    segment, in_segment, packed_lane = segments(shape)
    from_west_lane = in_segment < EDGE
    at_edge = (lane < EDGE) | (lane >= width - EDGE)
    last_face = {
        shift: q == EDGE - 1
        for shift, q in moved_places(jnp.where(packed_lane, in_segment, -2 * SEG)).items()
    }
    base = levels * count

    def unfolded(x):
        return jnp.concatenate([x, lanes(x, -MET_SEG * levels)])

    met_east = unfolded(east[base:, :])
    met_west = unfolded(west[base:, :])

    def copy(l, half):
        place = pl.ds(half * PACK, PACK)
        return pltpu.make_async_copy(stage.at[place, l], out.at[place, l], sems.at[l, half])

    def level(l, sums, outer_c, edge_c, thickness):
        level_rows = pl.ds(pl.multiple_of(l * count, count), count)
        met_lane = jnp.where(packed_lane, in_segment + MET_SEG * l, 0)
        met = jnp.where(lane - MET_SEG * l < EDGE, met_west, met_east)
        beyond = east_taps(
            pick(met_east, jnp.full(shape, SEG, jnp.int32) + MET_SEG * l),
            pick(met_east, jnp.full(shape, SEG + 1, jnp.int32) + MET_SEG * l),
        )
        mass_flux = pick(met_east, jnp.full(shape, SEG + 2, jnp.int32) + MET_SEG * l)
        inverse = 2.0 / (thickness[l] - jnp.where(lane == width - 1, mass_flux, 0.0))
        face = {
            m: jnp.where(last_face[east_group(m)], -beyond[m - 1], 0.0)
            for m in range(1 - EDGE, EDGE + 1)
        }
        outer = {m: outer_c[m + EDGE, l] for m in range(-EDGE, EDGE + 1) if m != 0}
        for m in range(1, EDGE + 1):
            outer[m] = outer[m] + face[m]
        inside = {m: face[m] for m in range(1 - EDGE, 1)}
        edge_taps = [edge_c[m, l] for m in range(7)]
        packed_taps = north_coefficients(pick(met, met_lane))
        for half in range(2):
            first_lane = EDGE * (segment + PACK * half) + in_segment
            west_index = jnp.where(packed_lane & from_west_lane, first_lane, 0)
            east_index = jnp.where(packed_lane & ~from_west_lane, first_lane - EDGE, 0)
            own_cells = own[half, 0, l]
            own_near = {0: own_cells, **{shift: own[half, k + 1, l] for k, shift in enumerate(NEAR)}}
            cells = jnp.where(
                from_west_lane,
                pick(west[level_rows, :], west_index),
                pick(east[level_rows, :], east_index),
            )
            inner = cells
            own_inner = own_cells
            for m in range(-3, 4):
                inner = inner + packed_taps[m + 3] * rows(cells, -m)
                own_inner = own_inner + edge_taps[m + 3] * rows(own_cells, -m)
            first = moved_sum(
                east_parts(inside, own_near, east_parts(outer, near_cells(cells)))
            )
            total = moved_sum(
                east_parts(inside, near_cells(own_inner), east_parts(outer, near_cells(inner)))
            )
            for m in range(-3, 4):
                total = total + edge_taps[m + 3] * rows(first, -m)
            for k in range(PACK):
                t = half * PACK + k
                moved = jnp.where(at_edge, lanes(total, width - EDGE - SEG * k), 0.0)
                stage[t, l] = (sums(t, l, half) + moved) * inverse
            copy(l, half).start()

    def sums_after(t, l, half):
        value = after[0][t, l]
        return value if half else jnp.where(2 * l < early, before[0][t, l], value)

    def either(l, carry):
        @pl.when(2 * l + 1 < early)
        def _():
            level(l, lambda t, l, half: before[0][t, l], *before[1:])

        @pl.when(2 * l + 1 >= early)
        def _():
            level(l, sums_after, *after[1:])

        return carry

    lax.fori_loop(0, levels, either, 0)
    for l in range(levels):
        for half in range(2):
            copy(l, half).wait()


def edge_update(west, east, own, before, after):
    sums = before[0]
    tracers, levels, count, width = sums.shape
    vmem = pl.BlockSpec(memory_space=pltpu.VMEM)
    return pl.pallas_call(
        edge_kernel,
        out_shape=jax.ShapeDtypeStruct(sums.shape, jnp.float32),
        in_specs=[vmem] * 11,
        out_specs=pl.BlockSpec(memory_space=pl.ANY),
        scratch_shapes=[pltpu.VMEM(sums.shape, jnp.float32), pltpu.SemaphoreType.DMA((levels, 2))],
        compiler_params=pltpu.CompilerParams(vmem_limit_bytes=24 * 1024 * 1024),
        name="edges",
    )(west, east, own, *before, *after)


def east_group(m):
    return -STEP if m < -1 else (STEP if m > 2 else 0)


def along(x, pairs):
    return lax.ppermute(x, "space", pairs)


def exchange(x, flip):
    size = lax.axis_size("tracer")
    return lax.ppermute(x, "tracer", [(i, i ^ flip) for i in range(size)])


def turn(x, by):
    size = lax.axis_size("tracer")
    return lax.ppermute(x, "tracer", [(i, i // 8 * 8 + (i + 2 * by) % 8) for i in range(size)])


def shards(mass, thick, fe, fn, ce, cn, ne, owner):
    keep, send = prepare(thick, fe, fn, ce, cn, ne)
    last, first, own = pack(mass)
    me, chosen = position(), owner[0]
    other_core = exchange(send, 1)
    total = jnp.where(chosen == me, keep, jnp.where(chosen == me ^ 1, other_core, 0.0))
    total = total + (turn(total, 1) + turn(total, -1) + turn(total, 2))
    total, last, first, own = lax.optimization_barrier((total, last, first, own))
    total = total + exchange(total, 8)
    padded, shifted = copies(mass)
    main = 2 * mass.shape[1] * mass.shape[2]
    mine = total[:main]
    edges = total[main:]
    size = lax.axis_size("space")
    to_east = jnp.concatenate([last, edges])
    to_west = jnp.concatenate([first, edges])
    west = along(to_east, [(i, (i + 1) % size) for i in range(size)])
    other = exchange(mine, 1)
    before = inner_update(lambda levels: (0, early_parts(levels)), mine, other, padded, shifted)
    to_west, before = lax.optimization_barrier((to_west, before))
    east = along(to_west, [(i, (i - 1) % size) for i in range(size)])
    after = inner_update(lambda levels: (early_parts(levels), 2 * levels), mine, other, padded, shifted)
    return edge_update(west, east, own, before, after)


def solution(mesh):
    spec = P("tracer", None, None, "space")
    return jax.shard_map(
        shards, mesh=mesh, in_specs=(spec,) * 7 + (P("space"),), out_specs=spec, check_vma=False
    )
```

```python
import functools

import jax
import jax.numpy as jnp
from jax import lax
from jax.experimental import pallas as pl
from jax.experimental.pallas import tpu as pltpu
from jax.sharding import PartitionSpec as P

NS = 2
EDGE = NS + 3
SEG = 2 * EDGE
PACK = 9
STEP = 4
GROUP = 3
PAD = 8
BLOCK = 8
NEAR = (-1, 1, 2)
MET_SEG = 16


def lane_index(shape):
    return lax.broadcasted_iota(jnp.int32, shape, len(shape) - 1)


def row_index(shape):
    return lax.broadcasted_iota(jnp.int32, shape, len(shape) - 2)


def lanes(x, shift):
    return pltpu.roll(x, shift % x.shape[-1], x.ndim - 1)


def rows(x, shift):
    return pltpu.roll(x, shift % x.shape[-2], x.ndim - 2)


def face_weights(courant):
    fraction = jnp.abs(courant)
    ramp = 1.5 * fraction * (1.0 - 2.0 / 3.0 * fraction)
    near = 0.5 * courant * (1.0 - 0.5 * fraction - ramp)
    far = 0.5 * courant * (0.5 * fraction - ramp)
    mean = courant * ramp
    far_outer = far * (1.0 / 12.0)
    near_outer = near * (1.0 / 12.0)
    return (
        -near_outer,
        7.0 * near_outer - far_outer,
        7.0 * (near_outer + far_outer) + mean,
        7.0 * far_outer - near_outer,
        -far_outer,
    )


def north_taps(courant):
    down1, up0, up1, up2, up3 = (w for w in face_weights(courant))
    forward = courant >= 0.0
    zero = jnp.zeros_like(courant)
    f = {1: down1, 0: up0, -1: up1, -2: up2, -3: up3}
    b = {-2: down1, -1: up0, 0: up1, 1: up2, 2: up3}
    return {m: jnp.where(forward, f.get(m, zero), b.get(m, zero)) for m in range(-3, 3)}


def east_taps(courant, whole):
    weights = face_weights(courant)
    forward = courant >= 0.0
    zero = jnp.zeros_like(courant)
    one = whole == 1.0
    two = whole == 2.0
    some = whole > 0.5
    taps = {}
    for m in range(-EDGE, EDGE):
        ahead = []
        behind = []
        for n in range(NS + 1):
            place = 1 - n - m
            ahead.append(weights[place] if 0 <= place < 5 else zero)
            place = m + 2 - n
            behind.append(weights[place] if 0 <= place < 5 else zero)
        f = jnp.where(two, ahead[2], jnp.where(one, ahead[1], ahead[0]))
        b = jnp.where(two, behind[2], jnp.where(one, behind[1], behind[0]))
        if m == -1:
            f = f + jnp.where(some, 0.5, 0.0)
        if m == -2:
            f = f + jnp.where(two, 0.5, 0.0)
        if m == 0:
            b = b - jnp.where(some, 0.5, 0.0)
        if m == 1:
            b = b - jnp.where(two, 0.5, 0.0)
        taps[m] = jnp.where(forward, f, b)
    return taps


def difference_taps(here, ahead, reach):
    out = {}
    for m in range(-reach, reach + 1):
        if m in here and m - 1 in ahead:
            out[m] = here[m] - ahead[m - 1]
        elif m in here:
            out[m] = here[m]
        else:
            out[m] = -ahead[m - 1]
    return out


def north_coefficients(courant):
    count = courant.shape[0]
    row = row_index(courant.shape)
    here = north_taps(jnp.where(row == 0, 0.0, courant))
    taps = difference_taps(here, {m: rows(here[m], -1) for m in here}, 3)
    return [
        jnp.where((row + m >= 0) & (row + m < count), taps[m], 0.0) for m in range(-3, 4)
    ]


def pick(x, index):
    return jnp.take_along_axis(x, index, axis=1, mode="promise_in_bounds")


def position():
    return lax.axis_index("tracer")


def tile():
    return lax.axis_index("space")


def early_parts(levels):
    return jnp.clip(levels + 1 - tile(), 0, levels)


def prepare_kernel(*refs):
    sources, (keep, send, *fields, sems) = refs[:6], refs[6:]
    copies = [
        pltpu.make_async_copy(source, place, sems.at[k])
        for k, (source, place) in enumerate(zip(sources, fields))
    ]
    for copy in copies:
        copy.start()
    for copy in copies:
        copy.wait()
    thick, fe, fn, ce, cn, ne = fields
    core = position() % 2
    levels, count, width = thick.shape[1:]
    lane = lane_index((count, width))
    row = row_index((count, width))
    half_lane = lane_index((count // 2, width))
    folded = jnp.zeros((count // 2, width), jnp.float32)
    for l in range(levels):
        east_mass = fe[0, l]
        north_mass = jnp.where(row == 0, 0.0, fn[0, l])
        thickness = (
            thick[0, l]
            + (east_mass - jnp.where(lane == width - 1, 0.0, lanes(east_mass, -1)))
            + (north_mass - rows(north_mass, -1))
        )
        whole = ne[0, l].astype(jnp.float32)
        first = (thickness, ce[0, l])
        second = (cn[0, l], whole)
        for k in range(2):
            start = (k * levels + l) * count
            keep[start : start + count, :] = jnp.where(core == 0, first[k], second[k])
            send[start : start + count, :] = jnp.where(core == 0, second[k], first[k])
        for part, start in enumerate((MET_SEG * l, MET_SEG * (levels + l))):
            here = slice(part * count // 2, (part + 1) * count // 2)
            inside = (half_lane >= start) & (half_lane < start + SEG)
            folded = jnp.where(inside, lanes(cn[0, l, here, :], start + EDGE), folded)
            for k, value in enumerate((ce[0, l, here, :], whole[here], east_mass[here])):
                at = start + SEG + k
                folded = jnp.where(half_lane == at, lanes(value, at), folded)
    base = 2 * levels * count
    keep[base:, :] = folded
    send[base:, :] = folded


def prepare(thick, fe, fn, ce, cn, ne):
    levels, count, width = thick.shape[1:]
    vmem = pl.BlockSpec(memory_space=pltpu.VMEM)
    half = pltpu.VMEM((2 * levels * count + count // 2, width), jnp.float32)
    return pl.pallas_call(
        prepare_kernel,
        out_shape=(half, half),
        in_specs=[pl.BlockSpec(memory_space=pl.ANY)] * 6,
        out_specs=(vmem, vmem),
        scratch_shapes=[pltpu.VMEM(thick.shape, jnp.float32)] * 5
        + [pltpu.VMEM(ne.shape, jnp.int32), pltpu.SemaphoreType.DMA((6,))],
        name="prepare",
    )(thick, fe, fn, ce, cn, ne)


def pack_kernel(mass, last, first, own):
    tracers, levels, count, width = mass.shape
    lane = lane_index((count, width))
    segment, in_segment, packed_lane = segments((count, width))

    def level(l, carry):
        a = jnp.zeros((count, width), jnp.float32)
        b = a
        for t in range(tracers):
            inside = (lane >= EDGE * t) & (lane < EDGE * (t + 1))
            a = jnp.where(inside, lanes(mass[t, l], EDGE * (t + 1)), a)
            b = jnp.where(inside, lanes(mass[t, l], EDGE * t), b)
        place = pl.ds(pl.multiple_of(l * count, count), count)
        last[place, :] = a
        first[place, :] = b
        for half in range(tracers // PACK):
            index = EDGE * (segment + PACK * half) + in_segment
            cells = pick(a, jnp.where(packed_lane & (in_segment < EDGE), index, 0))
            own[half, 0, l] = cells
            for k, shift in enumerate(NEAR):
                own[half, k + 1, l] = lanes(cells, -shift)
        return carry

    lax.fori_loop(0, levels, level, 0)


def copies_kernel(mass, padded, moved):
    tracers, levels, count, width = mass.shape
    zero_rows = jnp.zeros((PAD, width), jnp.float32)

    def level(l, carry):
        for t in range(tracers):
            value = mass[t, l]
            padded[t, l, :PAD, :] = zero_rows
            padded[t, l, PAD : PAD + count, :] = value
            padded[t, l, PAD + count :, :] = zero_rows
            for k, shift in enumerate(NEAR):
                moved[k, t, l] = lanes(value, -shift)
        return carry

    lax.fori_loop(0, levels, level, 0)


def in_vmem(kernel, name, shapes, *operands):
    vmem = pl.BlockSpec(memory_space=pltpu.VMEM)
    return pl.pallas_call(
        kernel,
        out_shape=tuple(pltpu.VMEM(shape, jnp.float32) for shape in shapes),
        in_specs=[vmem] * len(operands),
        out_specs=(vmem,) * len(shapes),
        compiler_params=pltpu.CompilerParams(vmem_limit_bytes=24 * 1024 * 1024),
        cost_estimate=pl.CostEstimate(flops=2000000, bytes_accessed=1000000, transcendentals=0),
        name=name,
    )(*operands)


def pack(mass):
    tracers, levels, count, width = mass.shape
    own = (tracers // PACK, 1 + len(NEAR), levels, count, width)
    return in_vmem(pack_kernel, "pack", ((levels * count, width),) * 2 + (own,), mass)


def copies(mass):
    tracers, levels, count, width = mass.shape
    padded = (tracers, levels, count + 2 * PAD, width)
    return in_vmem(copies_kernel, "copies", (padded, (len(NEAR),) + mass.shape), mass)


def segments(shape):
    lane = lane_index(shape)
    segment = sum(
        ((lane >= SEG * k).astype(jnp.int32) for k in range(1, PACK)), jnp.zeros(shape, jnp.int32)
    )
    return segment, lane - SEG * segment, lane < SEG * PACK


def moved_places(held):
    return {shift: lanes(held, shift) if shift else held for shift in (-STEP, 0, STEP)}


def east_parts(taps, near, parts=None):
    parts = dict(parts or {})
    for m in taps:
        shift = east_group(m)
        term = taps[m] * near[m - shift]
        parts[shift] = parts[shift] + term if shift in parts else term
    return parts


def moved_sum(parts):
    return parts[0] + (lanes(parts[-STEP], STEP) + lanes(parts[STEP], -STEP))


def near_cells(x):
    return {0: x, **{shift: lanes(x, -shift) for shift in NEAR}}


def inner_kernel(span, mine, other, padded, shifted, *refs):
    low_part, high_part = span(refs[0].shape[1])

    @pl.when(low_part < high_part)
    def _():
        inner_body(low_part, high_part, mine, other, padded, shifted, *refs)


def inner_body(
    low_part, high_part, mine, other, padded, shifted, sums, outer_c, edge_c, thickness,
    east_c, north_c, inners, middle, partial,
):
    tracers, levels, count, width = sums.shape
    shape = (count, width)
    lane = lane_index(shape)
    low = position() % 2 == 0
    _, in_segment, packed_lane = segments(shape)
    zero_rows = jnp.zeros((PAD, width), jnp.float32)
    for slot in range(2):
        for j in range(GROUP):
            middle[slot, j, :PAD, :] = zero_rows
            middle[slot, j, PAD + count :, :] = zero_rows
    edge_index = jnp.where(packed_lane, in_segment + (width - EDGE), 0)
    edge_index = jnp.where(edge_index >= width, edge_index - width, edge_index)
    moved_index = moved_places(edge_index)
    moved_segment = moved_places(jnp.where(packed_lane, in_segment, -2 * SEG))

    def level(l, carry):
        fields = []
        for half in range(2):
            for k in range(2):
                place = pl.ds(pl.multiple_of((k * levels + l) * count, count), count)
                a = mine[place, :]
                b = other[place, :]
                fields.append(jnp.where(low, a, b) if half == 0 else jnp.where(low, b, a))
        thick, east_courant, north_courant, whole = fields
        thickness[l] = thick
        here = east_taps(east_courant, whole)
        ahead = {m: jnp.where(lane == width - 1, 0.0, lanes(here[m], -1)) for m in here}
        taps = difference_taps(here, ahead, EDGE)
        for m in range(-EDGE, EDGE + 1):
            value = taps[m]
            if m != 0:
                q = moved_segment[east_group(m)]
                crosses = ((q < EDGE) != (q + m < EDGE)) & (q >= 0)
                outer_c[m + EDGE, l] = jnp.where(crosses, pick(value, moved_index[east_group(m)]), 0.0)
            if m < 0:
                value = jnp.where(lane >= -m, value, 0.0)
            if m > 0:
                value = jnp.where(lane < width - m, value, 0.0)
            shift = east_group(m)
            east_c[m + EDGE, l] = lanes(value, shift) if shift else value
        for m, value in enumerate(north_coefficients(north_courant)):
            north_c[m, l] = value
        for m, value in enumerate(north_coefficients(pick(north_courant, edge_index))):
            edge_c[m, l] = value
        return carry

    lax.fori_loop(low_part // 2, (high_part + 1) // 2, level, 0)
    groups = tracers // GROUP
    low_step, high_step = low_part * (groups // 2), high_part * (groups // 2)

    def block(b):
        return slice(b * BLOCK, (b + 1) * BLOCK)

    def padded_block(b, m=0):
        return slice(PAD + b * BLOCK + m, PAD + (b + 1) * BLOCK + m)

    def place(step):
        step = jnp.clip(step, 0, levels * groups - 1)
        return step // groups, (step % groups) * GROUP

    def weights(ref, l, b, reach):
        return {m: ref[m + reach, l, block(b), :] for m in range(-reach, reach + 1)}

    def front(step):
        l, t0 = place(step)
        slot = (step + 2) % 2
        for b in range(count // BLOCK):
            taps = weights(east_c, l, b, EDGE)
            north = weights(north_c, l, b, 3)
            taps[0] = 1.0 + taps[0]
            north[0] = 1.0 + north[0]
            for j in range(GROUP):
                x = padded[t0 + j, l, padded_block(b), :]
                inner = north[0] * x
                for m in (-3, -2, -1, 1, 2, 3):
                    inner = inner + north[m] * padded[t0 + j, l, padded_block(b, m), :]
                inners[slot, j, block(b), :] = inner
                near = {0: x}
                for k, shift in enumerate(NEAR):
                    near[shift] = shifted[k, t0 + j, l, block(b), :]
                middle[slot, j, padded_block(b), :] = moved_sum(east_parts(taps, near))

    def back(step):
        l, t0 = place(step)
        slot = (step + 2) % 2
        for b in range(count // BLOCK):
            taps = weights(east_c, l, b, EDGE)
            north = weights(north_c, l, b, 3)
            for j in range(GROUP):
                parts = east_parts(taps, near_cells(inners[slot, j, block(b), :]))
                total = 0.5 * padded[t0 + j, l, padded_block(b), :] + parts[0]
                for m in range(-3, 4):
                    total = total + north[m] * middle[slot, j, padded_block(b, m), :]
                partial[slot, 0, j, block(b), :] = total
                partial[slot, 1, j, block(b), :] = parts[-STEP]
                partial[slot, 2, j, block(b), :] = parts[STEP]

    def finish(step):
        l, t0 = place(step)
        slot = (step + 2) % 2
        for b in range(count // BLOCK):
            for j in range(GROUP):
                sums[t0 + j, l, block(b), :] = partial[slot, 0, j, block(b), :] + (
                    lanes(partial[slot, 1, j, block(b), :], STEP)
                    + lanes(partial[slot, 2, j, block(b), :], -STEP)
                )

    def step_of_three(step, carry):
        finish(step - 1)
        back(step)
        front(step + 1)
        return carry

    front(low_step)
    lax.fori_loop(low_step, high_step, step_of_three, 0)
    finish(high_step - 1)


def inner_update(span, mine, other, padded, shifted):
    tracers, levels, count, width = shifted.shape[1:]
    vmem = pl.BlockSpec(memory_space=pltpu.VMEM)
    level = (levels, count, width)
    return pl.pallas_call(
        functools.partial(inner_kernel, span),
        out_shape=(
            pltpu.VMEM((tracers,) + level, jnp.float32),
            pltpu.VMEM((2 * EDGE + 1,) + level, jnp.float32),
            pltpu.VMEM((7,) + level, jnp.float32),
            pltpu.VMEM(level, jnp.float32),
        ),
        in_specs=[vmem] * 4,
        out_specs=(vmem,) * 4,
        scratch_shapes=[
            pltpu.VMEM((2 * EDGE + 1,) + level, jnp.float32),
            pltpu.VMEM((7,) + level, jnp.float32),
            pltpu.VMEM((2, GROUP, count, width), jnp.float32),
            pltpu.VMEM((2, GROUP, count + 2 * PAD, width), jnp.float32),
            pltpu.VMEM((2, 3, GROUP, count, width), jnp.float32),
        ],
        compiler_params=pltpu.CompilerParams(vmem_limit_bytes=24 * 1024 * 1024),
        cost_estimate=pl.CostEstimate(flops=20000000, bytes_accessed=6000000, transcendentals=0),
        name="inner",
    )(mine, other, padded, shifted)


def edge_kernel(west, east, own, *refs):
    before, after, (out, stage, sems) = refs[:4], refs[4:8], refs[8:]
    tracers, levels, count, width = stage.shape
    early = early_parts(levels)
    shape = (count, width)
    lane = lane_index(shape)
    segment, in_segment, packed_lane = segments(shape)
    from_west_lane = in_segment < EDGE
    at_edge = (lane < EDGE) | (lane >= width - EDGE)
    last_face = {
        shift: q == EDGE - 1
        for shift, q in moved_places(jnp.where(packed_lane, in_segment, -2 * SEG)).items()
    }
    base = levels * count

    def unfolded(x):
        return jnp.concatenate([x, lanes(x, -MET_SEG * levels)])

    met_east = unfolded(east[base:, :])
    met_west = unfolded(west[base:, :])

    def copy(l, half):
        place = pl.ds(half * PACK, PACK)
        return pltpu.make_async_copy(stage.at[place, l], out.at[place, l], sems.at[l, half])

    def level(l, sums, outer_c, edge_c, thickness):
        level_rows = pl.ds(pl.multiple_of(l * count, count), count)
        met_lane = jnp.where(packed_lane, in_segment + MET_SEG * l, 0)
        met = jnp.where(lane - MET_SEG * l < EDGE, met_west, met_east)
        beyond = east_taps(
            pick(met_east, jnp.full(shape, SEG, jnp.int32) + MET_SEG * l),
            pick(met_east, jnp.full(shape, SEG + 1, jnp.int32) + MET_SEG * l),
        )
        mass_flux = pick(met_east, jnp.full(shape, SEG + 2, jnp.int32) + MET_SEG * l)
        inverse = 2.0 / (thickness[l] - jnp.where(lane == width - 1, mass_flux, 0.0))
        face = {
            m: jnp.where(last_face[east_group(m)], -beyond[m - 1], 0.0)
            for m in range(1 - EDGE, EDGE + 1)
        }
        outer = {m: outer_c[m + EDGE, l] for m in range(-EDGE, EDGE + 1) if m != 0}
        for m in range(1, EDGE + 1):
            outer[m] = outer[m] + face[m]
        inside = {m: face[m] for m in range(1 - EDGE, 1)}
        edge_taps = [edge_c[m, l] for m in range(7)]
        packed_taps = north_coefficients(pick(met, met_lane))
        for half in range(2):
            first_lane = EDGE * (segment + PACK * half) + in_segment
            west_index = jnp.where(packed_lane & from_west_lane, first_lane, 0)
            east_index = jnp.where(packed_lane & ~from_west_lane, first_lane - EDGE, 0)
            own_cells = own[half, 0, l]
            own_near = {0: own_cells, **{shift: own[half, k + 1, l] for k, shift in enumerate(NEAR)}}
            cells = jnp.where(
                from_west_lane,
                pick(west[level_rows, :], west_index),
                pick(east[level_rows, :], east_index),
            )
            inner = cells
            own_inner = own_cells
            for m in range(-3, 4):
                inner = inner + packed_taps[m + 3] * rows(cells, -m)
                own_inner = own_inner + edge_taps[m + 3] * rows(own_cells, -m)
            first = moved_sum(
                east_parts(inside, own_near, east_parts(outer, near_cells(cells)))
            )
            total = moved_sum(
                east_parts(inside, near_cells(own_inner), east_parts(outer, near_cells(inner)))
            )
            for m in range(-3, 4):
                total = total + edge_taps[m + 3] * rows(first, -m)
            for k in range(PACK):
                t = half * PACK + k
                moved = jnp.where(at_edge, lanes(total, width - EDGE - SEG * k), 0.0)
                stage[t, l] = (sums(t, l, half) + moved) * inverse
            copy(l, half).start()

    def sums_after(t, l, half):
        value = after[0][t, l]
        return value if half else jnp.where(2 * l < early, before[0][t, l], value)

    def either(l, carry):
        @pl.when(2 * l + 1 < early)
        def _():
            level(l, lambda t, l, half: before[0][t, l], *before[1:])

        @pl.when(2 * l + 1 >= early)
        def _():
            level(l, sums_after, *after[1:])

        return carry

    lax.fori_loop(0, levels, either, 0)
    for l in range(levels):
        for half in range(2):
            copy(l, half).wait()


def edge_update(west, east, own, before, after):
    sums = before[0]
    tracers, levels, count, width = sums.shape
    vmem = pl.BlockSpec(memory_space=pltpu.VMEM)
    return pl.pallas_call(
        edge_kernel,
        out_shape=jax.ShapeDtypeStruct(sums.shape, jnp.float32),
        in_specs=[vmem] * 11,
        out_specs=pl.BlockSpec(memory_space=pl.ANY),
        scratch_shapes=[pltpu.VMEM(sums.shape, jnp.float32), pltpu.SemaphoreType.DMA((levels, 2))],
        compiler_params=pltpu.CompilerParams(vmem_limit_bytes=24 * 1024 * 1024),
        name="edges",
    )(west, east, own, *before, *after)


def east_group(m):
    return -STEP if m < -1 else (STEP if m > 2 else 0)


def along(x, pairs):
    return lax.ppermute(x, "space", pairs)


def exchange(x, flip):
    size = lax.axis_size("tracer")
    return lax.ppermute(x, "tracer", [(i, i ^ flip) for i in range(size)])


def turn(x, by):
    size = lax.axis_size("tracer")
    return lax.ppermute(x, "tracer", [(i, i // 8 * 8 + (i + 2 * by) % 8) for i in range(size)])


def shards(mass, thick, fe, fn, ce, cn, ne, owner):
    keep, send = prepare(thick, fe, fn, ce, cn, ne)
    last, first, own = pack(mass)
    me, chosen = position(), owner[0]
    other_core = exchange(send, 1)
    total = jnp.where(chosen == me, keep, jnp.where(chosen == me ^ 1, other_core, 0.0))
    far = turn(total, 2)
    total = (total + turn(total, 1)) + (turn(total, -1) + far)
    total, last, first, own = lax.optimization_barrier((total, last, first, own))
    total = total + exchange(total, 8)
    padded, shifted = copies(mass)
    main = 2 * mass.shape[1] * mass.shape[2]
    mine = total[:main]
    edges = total[main:]
    size = lax.axis_size("space")
    to_east = jnp.concatenate([last, edges])
    to_west = jnp.concatenate([first, edges])
    west = along(to_east, [(i, (i + 1) % size) for i in range(size)])
    other = exchange(mine, 1)
    before = inner_update(lambda levels: (0, early_parts(levels)), mine, other, padded, shifted)
    to_west, before = lax.optimization_barrier((to_west, before))
    east = along(to_west, [(i, (i - 1) % size) for i in range(size)])
    after = inner_update(lambda levels: (early_parts(levels), 2 * levels), mine, other, padded, shifted)
    return edge_update(west, east, own, before, after)


def solution(mesh):
    spec = P("tracer", None, None, "space")
    return jax.shard_map(
        shards, mesh=mesh, in_specs=(spec,) * 7 + (P("space"),), out_specs=spec, check_vma=False
    )
```
